32 devices in a mesh: gx: 4 (over y, x), gy: 8 (over z, core).
Axes of the slice: x: 2, y: 2, z: 4, core: 2. Of those that a mesh axis runs over, the one named last changes fastest.
Arguments:
- basis: float32 [32, 64, 64, 128], P(None, 'gx', 'gy'), may hold values from -21 to 21
- classes: int32 [64, 64, 128], P('gx', 'gy'), may hold values from 0 to 7
- ports: int32 [64, 64, 128], P('gx', 'gy'), may hold values from 0 to 8, as said below
- taps: float32 [8, 42], replicated, may hold values from 0.05 to 0.5
- port_gain: float32 [8], replicated, may hold values from 0.5 to 4
Outputs:
- next_block: float32 [8, 64, 64, 128], P(None, 'gx', 'gy')
- projection: float32 [32, 8], replicated
- triangle: float32 [8, 8], replicated
The draws below stay inside these ranges and needn't reach their ends.
Inputs may be any that keep to these rules, and one draw needn't show every extreme that they name: `ports`: 0 means the cell belongs to no port; p in 1..8 names port p.
All inputs are finite; a program needn't handle non-finite values.
Results may differ from the reference program's by a relative error of at most 0.00029.
Values sent between devices are 32-bit elements; how exact they have to be, the bound alone decides.
A program may use at most 64 MiB of HBM per device.

```python
import math
import jax
import jax.numpy as jnp
from jax import lax

COLS = 8
BLOCKS = 4
REACH = 7
MAT = 8
PORTS = 8
NX = 64
NY = 64
NZ = 128


def draw_basis(key, part):
    first, second = jax.random.split(key)
    shape = (BLOCKS * COLS, NX, NY, NZ)
    values = jnp.clip(jax.random.normal(first, shape, jnp.float32), -6.0, 6.0)
    spread = jax.random.uniform(second, (1, NX, NY, NZ), jnp.float32)
    cell_scale = jnp.power(10.0, spread) / 4.6365
    position = jnp.arange(NX, dtype=jnp.float32) / NX
    ramp = jnp.power(3.0, position) / 1.9082
    return values * cell_scale * ramp[None, :, None, None]


def draw_ports(key, part):
    first, second = jax.random.split(jax.random.fold_in(key, 17))
    chosen = jax.random.randint(first, (NX, NY, NZ), 0, 4)
    which = jax.random.randint(second, (NX, NY, NZ), 1, PORTS + 1)
    return jnp.where(chosen == 0, which, 0).astype(jnp.int32)


def place_ends(array, own_key, smallest, top_value):
    spot = [jax.random.randint(jax.random.fold_in(own_key, axis), (), 0, length) for axis, length in enumerate(array.shape)]
    widest = array.shape.index(max(array.shape))
    beside = spot[:widest] + [(spot[widest] + 1) % array.shape[widest]] + spot[widest + 1:]
    return array.at[tuple(spot)].set(smallest).at[tuple(beside)].set(top_value)


def setup_inputs(seed: int = 0) -> dict:
    splits = jax.random.split(jax.random.key(seed), 6)
    basis = draw_basis(jax.random.fold_in(splits[5], 71), 0)
    classes = place_ends(jax.random.randint(splits[1], (NX, NY, NZ), 0, MAT), jax.random.fold_in(splits[1], 1), 0, MAT - 1).astype(jnp.int32)
    ports = draw_ports(jax.random.fold_in(splits[5], 71), 0)
    taps = jnp.clip(jnp.exp(jax.random.uniform(splits[3], (MAT, 6 * REACH), jnp.float32, math.log(0.05), math.log(0.5))), 0.05, 0.5)
    port_gain = jnp.clip(jnp.exp(jax.random.uniform(splits[4], (PORTS,), jnp.float32, math.log(0.5), math.log(4.0))), 0.5, 4.0)
    return dict(basis=basis, classes=classes, ports=ports, taps=taps, port_gain=port_gain)


def reference(basis, classes, ports, taps, port_gain):
    highest = lax.Precision.HIGHEST
    gains_full = jnp.concatenate([jnp.zeros((1,), jnp.float32), port_gain])
    diag = 1.0 + jnp.sum(taps, axis=1)[classes] + gains_full[ports]
    block = basis[(BLOCKS - 1) * COLS:]
    sizes_all = (NX, NY, NZ)

    def apply_column(column):
        result = diag * column
        for dim in range(3):
            widths = [(0, 0), (0, 0), (0, 0)]
            widths[dim] = (REACH, REACH)
            padded = jnp.pad(column, widths)
            for j in range(2 * REACH):
                offset = j - REACH if j < REACH else j - REACH + 1
                shifted = lax.slice_in_dim(padded, REACH + offset, REACH + offset + sizes_all[dim], axis=dim)
                result = result - taps[:, 2 * REACH * dim + j][classes] * shifted
        return result
    image = lax.map(apply_column, block)
    cells = NX * NY * NZ
    basis_flat = basis.reshape(BLOCKS * COLS, cells)
    image_flat = image.reshape(COLS, cells)
    projection = jnp.dot(basis_flat, image_flat.T, precision=highest) / cells
    remainder = image_flat - jnp.dot(projection.T, basis_flat, precision=highest)
    gram = jnp.dot(remainder, remainder.T, precision=highest) / cells
    lower = jnp.linalg.cholesky(gram)
    solved = lax.linalg.triangular_solve(lower, remainder, left_side=True, lower=True)
    return (solved.reshape(COLS, NX, NY, NZ), projection, lower.T)
```

```python
import functools

import jax
import jax.numpy as jnp
from jax import lax
from jax.experimental import pallas as pl
from jax.experimental.pallas import tpu as pltpu
from jax.sharding import PartitionSpec as P

COLS = 8
BLOCKS = 4
REACH = 7
MAT = 8
PORTS = 8
GROUP = 4
MESH = pl.DeviceIdType.MESH
NT = (((1,), (1,)), ((), ()))
HIGHEST = lax.Precision.HIGHEST


def offset_of(j):
    return j - REACH if j < REACH else j - REACH + 1


def halves(value):
    high = value.astype(jnp.bfloat16).astype(jnp.float32)
    return jnp.concatenate([high, value - high], axis=0).astype(jnp.bfloat16)


class Exchange:
    def __init__(self, axis, buf, send, recv):
        self.axis, self.buf, self.send, self.recv = axis, buf, send, recv
        self.me, self.count = lax.axis_index(axis), lax.axis_size(axis)

    def copy(self, step, slot, peer):
        return pltpu.make_async_remote_copy(
            src_ref=self.buf.at[slot],
            dst_ref=self.buf.at[slot],
            send_sem=self.send.at[step],
            recv_sem=self.recv.at[slot],
            device_id={self.axis: peer},
            device_id_type=MESH,
        )

    def start(self, value):
        self.buf[self.me] = value

        def body(step, carry):
            self.copy(step, self.me, lax.rem(self.me + step, self.count)).start()
            return carry

        lax.fori_loop(1, self.count, body, 0)

    def finish(self):
        def body(step, carry):
            peer = lax.rem(self.me + step, self.count)
            self.copy(step, peer, peer).wait_recv()
            self.copy(step, self.me, peer).wait_send()
            return carry

        lax.fori_loop(1, self.count, body, 0)
        total = self.buf[0]
        for slot in range(1, self.count):
            total = total + self.buf[slot]
        return total


def kernel(
    total_cells,
    taps_ref,
    gain_ref,
    basis4,
    basis2,
    classes_hbm,
    ports_hbm,
    out2,
    proj_ref,
    tri_ref,
    pad,
    q2,
    qs,
    w2,
    ws,
    coefs,
    diag,
    classes,
    ports,
    qq_y,
    qq_x,
    g_y,
    g_x,
    local_sem,
    block_sem,
    halo_send,
    halo_recv,
    qq_y_send,
    qq_y_recv,
    qq_x_send,
    qq_x_recv,
    g_y_send,
    g_y_recv,
    g_x_send,
    g_x_recv,
):
    size_x, size_y, size_z = classes.shape
    rows = size_x * size_y
    first = (BLOCKS - 1) * COLS
    gx, gy = lax.axis_index("gx"), lax.axis_index("gy")
    nx, ny = lax.axis_size("gx"), lax.axis_size("gy")
    chunks, _, span = qs.shape
    per_chunk = span // size_z

    barrier = pltpu.get_barrier_semaphore()
    for axis, me, count in (("gx", gx, nx), ("gy", gy, ny)):

        def greet(step, carry, axis=axis, me=me, count=count):
            pl.semaphore_signal(
                barrier, inc=1, device_id={axis: lax.rem(me + step, count)}, device_id_type=MESH
            )
            return carry

        lax.fori_loop(1, count, greet, 0)

    load_classes = pltpu.make_async_copy(classes_hbm, classes, local_sem.at[0])
    load_ports = pltpu.make_async_copy(ports_hbm, ports, local_sem.at[1])
    load_basis = pltpu.make_async_copy(basis2, q2, local_sem.at[2])
    load_block = pltpu.make_async_copy(
        basis4.at[pl.ds(first, COLS)],
        pad.at[:, pl.ds(REACH, size_x), pl.ds(size_y, size_y), :],
        block_sem,
    )
    load_classes.start()
    load_ports.start()
    load_block.start()
    load_basis.start()
    pl.semaphore_wait(barrier, nx + ny - 2)

    inner_x, inner_y = pl.ds(REACH, size_x), pl.ds(size_y, size_y)
    ways = (
        ("gy", 1, gy < ny - 1, gy > 0,
         (slice(None), pl.ds(size_y - REACH, REACH)), (inner_x, pl.ds(size_y - REACH, REACH))),
        ("gy", -1, gy > 0, gy < ny - 1,
         (slice(None), pl.ds(0, REACH)), (inner_x, pl.ds(2 * size_y, REACH))),
        ("gx", 1, gx < nx - 1, gx > 0,
         (pl.ds(size_x - REACH, REACH), slice(None)), (pl.ds(0, REACH), inner_y)),
        ("gx", -1, gx > 0, gx < nx - 1,
         (pl.ds(0, REACH), slice(None)), (pl.ds(REACH + size_x, REACH), inner_y)),
    )

    def halo(way, group):
        axis, step, _, _, (from_x, from_y), (to_x, to_y) = ways[way]
        return pltpu.make_async_remote_copy(
            src_ref=basis4.at[pl.ds(first + group * GROUP, GROUP), from_x, from_y, :],
            dst_ref=pad.at[pl.ds(group * GROUP, GROUP), to_x, to_y, :],
            send_sem=halo_send.at[way, group],
            recv_sem=halo_recv.at[way, group],
            device_id={axis: lax.axis_index(axis) + step},
            device_id_type=MESH,
        )

    for group in range(COLS // GROUP):
        for way in range(4):

            @pl.when(ways[way][2])
            def _(way=way, group=group):
                halo(way, group).start()

    for way in range(4):

        @pl.when(jnp.logical_not(ways[way][3]))
        def _(way=way):
            to_x, to_y = ways[way][5]
            pad[:, to_x, to_y, :] = jnp.zeros((COLS, to_x.size, to_y.size, size_z), jnp.float32)

    load_classes.wait()
    load_ports.wait()
    lane = lax.broadcasted_iota(jnp.int32, (size_y, size_z), 1)

    def make_coefs(x, carry):
        kind, port = classes[x], ports[x]
        bits = [(kind & (1 << b)) != 0 for b in range(3)]
        gain = jnp.zeros((size_y, size_z), jnp.float32)
        for p in range(PORTS):
            gain = jnp.where(port == p + 1, gain_ref[p], gain)
        total = 1.0 + gain
        for t in range(6 * REACH):
            level = [taps_ref[m, t] for m in range(MAT)]
            for bit in bits:
                level = [
                    jnp.where(bit, level[2 * i + 1], level[2 * i]) for i in range(len(level) // 2)
                ]
            total = total + level[0]
            value = level[0]
            if t >= 4 * REACH:
                k = offset_of(t - 4 * REACH)
                value = jnp.where((lane + k >= 0) & (lane + k < size_z), value, 0.0)
            coefs[t, x] = value
        diag[x] = total
        return carry

    lax.fori_loop(0, size_x, make_coefs, 0)
    load_block.wait()

    def along_z(x, carry):
        for c in range(COLS):
            own = pad[c, x + REACH, pl.ds(size_y, size_y), :]
            image = diag[x] * own
            for j in range(2 * REACH):
                shifted = pltpu.roll(own, (-offset_of(j)) % size_z, 1)
                image = image - coefs[4 * REACH + j, x] * shifted
            w2[pl.ds(pl.multiple_of(c * rows + x * size_y, size_y), size_y), :] = image
        return carry

    lax.fori_loop(0, size_x, along_z, 0)
    load_basis.wait()

    def gather(ref, count, chunk):
        return jnp.concatenate(
            [
                ref[pl.ds(chunk * per_chunk + i, count, stride=rows), :]
                for i in range(per_chunk)
            ],
            axis=1,
        )

    def own_products(chunk, acc):
        both = halves(gather(q2, BLOCKS * COLS, chunk))
        qs[chunk] = both
        return acc + lax.dot_general(both, both, NT, preferred_element_type=jnp.float32)

    wide = BLOCKS * COLS
    acc = lax.fori_loop(0, chunks, own_products, jnp.zeros((2 * wide, 2 * wide), jnp.float32))
    acc = acc[:wide] + acc[wide:]
    local_qq = acc[:, :wide] + acc[:, wide:]
    fill = jnp.zeros((wide, 128 - wide), jnp.float32)
    exchange = Exchange("gy", qq_y, qq_y_send, qq_y_recv)
    exchange.start(jnp.concatenate([local_qq, fill], axis=1))

    for group in range(COLS // GROUP):
        for way in range(4):

            @pl.when(ways[way][3])
            def _(way=way, group=group):
                halo(way, group).wait_recv()

        def along_xy(x, carry, group=group):
            columns = range(group * GROUP, (group + 1) * GROUP)
            places = [
                pl.ds(pl.multiple_of(c * rows + x * size_y, size_y), size_y) for c in columns
            ]
            images = [w2[place, :] for place in places]
            for j in range(2 * REACH):
                k = offset_of(j)
                coef_x, coef_y = coefs[j, x], coefs[2 * REACH + j, x]
                for i, c in enumerate(columns):
                    images[i] = images[i] - coef_x * pad[c, x + REACH + k, inner_y, :]
                    images[i] = images[i] - coef_y * pad[c, x + REACH, pl.ds(size_y + k, size_y), :]
            for place, image in zip(places, images):
                w2[place, :] = image
            return carry

        lax.fori_loop(0, size_x, along_xy, 0)

    exchange_x = Exchange("gx", qq_x, qq_x_send, qq_x_recv)
    exchange_x.start(exchange.finish())

    def image_products(chunk, acc):
        both = halves(gather(w2, COLS, chunk))
        ws[chunk] = both
        acc_q, acc_w = acc
        acc_q = acc_q + lax.dot_general(both, qs[chunk], NT, preferred_element_type=jnp.float32)
        acc_w = acc_w + lax.dot_general(both, both, NT, preferred_element_type=jnp.float32)
        return acc_q, acc_w

    acc_q, acc_w = lax.fori_loop(
        0,
        chunks,
        image_products,
        (
            jnp.zeros((2 * COLS, 2 * wide), jnp.float32),
            jnp.zeros((2 * COLS, 2 * COLS), jnp.float32),
        ),
    )
    acc_q, acc_w = acc_q[:COLS] + acc_q[COLS:], acc_w[:COLS] + acc_w[COLS:]
    local_g = jnp.concatenate(
        [
            acc_q[:, :wide] + acc_q[:, wide:],
            acc_w[:, :COLS] + acc_w[:, COLS:],
            jnp.zeros((COLS, 128 - wide - COLS), jnp.float32),
        ],
        axis=1,
    )
    g_exchange = Exchange("gy", g_y, g_y_send, g_y_recv)
    g_exchange.start(local_g)
    sum_qq = exchange_x.finish()
    g_exchange_x = Exchange("gx", g_x, g_x_send, g_x_recv)
    g_exchange_x.start(g_exchange.finish())
    sums = g_exchange_x.finish() / total_cells

    proj_t = sums[:, :wide]
    proj_ref[...] = proj_t.T
    row = lax.broadcasted_iota(jnp.int32, (wide, wide), 0)
    column = lax.broadcasted_iota(jnp.int32, (wide, wide), 1)
    middle = jnp.where(row == column, 2.0, 0.0) - sum_qq[:, :wide] / total_cells
    left = jnp.dot(proj_t, middle, precision=HIGHEST, preferred_element_type=jnp.float32)
    gram = sums[:, wide : wide + COLS] - lax.dot_general(
        left, proj_t, NT, precision=HIGHEST, preferred_element_type=jnp.float32
    )
    row = lax.broadcasted_iota(jnp.int32, (COLS, COLS), 0)
    column = lax.broadcasted_iota(jnp.int32, (COLS, COLS), 1)
    eye = jnp.where(row == column, 1.0, 0.0)
    table = jnp.concatenate([-proj_t, eye, gram], axis=1)
    base = wide + COLS
    index = lax.broadcasted_iota(jnp.int32, table.shape, 0)
    for j in range(COLS):
        pivot = table[j : j + 1, :]
        scale = lax.rsqrt(pivot[:, base + j : base + j + 1])
        pivot = pivot * scale
        factor = table[:, base + j : base + j + 1] * scale
        table = jnp.where(index == j, pivot, jnp.where(index > j, table - factor * pivot, table))
    tri_ref[...] = jnp.where(row <= column, table[:, base:], 0.0)

    mix = table[:, :base]
    high = mix.astype(jnp.bfloat16).astype(jnp.float32)
    mix = jnp.concatenate([high, mix - high], axis=0)
    mix = jnp.concatenate([mix[:, :wide], mix[:, :wide]], axis=1), jnp.concatenate(
        [mix[:, wide:], mix[:, wide:]], axis=1
    )
    mix_q, mix_w = mix[0].astype(jnp.bfloat16), mix[1].astype(jnp.bfloat16)

    def combine(chunk, carry):
        result = jnp.dot(mix_q, qs[chunk], preferred_element_type=jnp.float32)
        result = result + jnp.dot(mix_w, ws[chunk], preferred_element_type=jnp.float32)
        result = result[:COLS] + result[COLS:]
        for i in range(per_chunk):
            out2[pl.ds(chunk * per_chunk + i, COLS, stride=rows), :] = result[
                :, i * size_z : (i + 1) * size_z
            ]
        return carry

    lax.fori_loop(0, chunks, combine, 0)
    for group in range(COLS // GROUP):
        for way in range(4):

            @pl.when(ways[way][2])
            def _(way=way, group=group):
                halo(way, group).wait_send()


def per_device(basis, classes, ports, taps, port_gain):
    size_x, size_y, size_z = classes.shape
    rows = size_x * size_y
    wide = BLOCKS * COLS
    nx, ny = lax.axis_size("gx"), lax.axis_size("gy")
    per_chunk = 16 if rows % 16 == 0 else 1
    chunks, span = rows // per_chunk, per_chunk * size_z
    vmem = functools.partial(pltpu.VMEM, dtype=jnp.float32)
    dma = pltpu.SemaphoreType.DMA
    any_space = pl.BlockSpec(memory_space=pl.ANY)
    smem = pl.BlockSpec(memory_space=pltpu.SMEM)
    vmem_spec = pl.BlockSpec(memory_space=pltpu.VMEM)
    groups = COLS // GROUP
    out, projection, triangle = pl.pallas_call(
        functools.partial(kernel, float(rows * size_z * nx * ny)),
        out_shape=(
            jax.ShapeDtypeStruct((COLS * rows, size_z), jnp.float32),
            jax.ShapeDtypeStruct((wide, COLS), jnp.float32),
            jax.ShapeDtypeStruct((COLS, COLS), jnp.float32),
        ),
        in_specs=[smem, smem, any_space, any_space, any_space, any_space],
        out_specs=(vmem_spec, vmem_spec, vmem_spec),
        scratch_shapes=[
            vmem((COLS, size_x + 2 * REACH, 3 * size_y, size_z)),
            vmem((wide * rows, size_z)),
            pltpu.VMEM((chunks, 2 * wide, span), jnp.bfloat16),
            vmem((COLS * rows, size_z)),
            pltpu.VMEM((chunks, 2 * COLS, span), jnp.bfloat16),
            vmem((6 * REACH, size_x, size_y, size_z)),
            vmem((size_x, size_y, size_z)),
            pltpu.VMEM((size_x, size_y, size_z), jnp.int32),
            pltpu.VMEM((size_x, size_y, size_z), jnp.int32),
            vmem((ny, wide, 128)),
            vmem((nx, wide, 128)),
            vmem((ny, COLS, 128)),
            vmem((nx, COLS, 128)),
            dma((3,)),
            dma,
            dma((4, groups)),
            dma((4, groups)),
            dma((ny,)),
            dma((ny,)),
            dma((nx,)),
            dma((nx,)),
            dma((ny,)),
            dma((ny,)),
            dma((nx,)),
            dma((nx,)),
        ],
        compiler_params=pltpu.CompilerParams(
            collective_id=0, has_side_effects=True, vmem_limit_bytes=40 * 1024 * 1024
        ),
    )(taps, port_gain, basis, basis.reshape(wide * rows, size_z), classes, ports)
    return out.reshape(COLS, size_x, size_y, size_z), projection, triangle


def solution(mesh):
    in_specs = (P(None, "gx", "gy", None), P("gx", "gy", None), P("gx", "gy", None), P(), P())
    out_specs = (P(None, "gx", "gy", None), P(), P())
    return jax.shard_map(
        per_device, mesh=mesh, in_specs=in_specs, out_specs=out_specs, check_vma=False
    )
```

```python
import functools

import jax
import jax.numpy as jnp
from jax import lax
from jax.experimental import pallas as pl
from jax.experimental.pallas import tpu as pltpu
from jax.sharding import PartitionSpec as P

COLS = 8
BLOCKS = 4
REACH = 7
MAT = 8
PORTS = 8
GROUP = 4
MESH = pl.DeviceIdType.MESH
NT = (((1,), (1,)), ((), ()))
HIGHEST = lax.Precision.HIGHEST


def offset_of(j):
    return j - REACH if j < REACH else j - REACH + 1


def halves(value):
    high = value.astype(jnp.bfloat16).astype(jnp.float32)
    return jnp.concatenate([high, value - high], axis=0).astype(jnp.bfloat16)


class Exchange:
    def __init__(self, axis, buf, send, recv):
        self.axis, self.buf, self.send, self.recv = axis, buf, send, recv
        self.me, self.count = lax.axis_index(axis), lax.axis_size(axis)

    def copy(self, step, slot, peer):
        return pltpu.make_async_remote_copy(
            src_ref=self.buf.at[slot],
            dst_ref=self.buf.at[slot],
            send_sem=self.send.at[step],
            recv_sem=self.recv.at[slot],
            device_id={self.axis: peer},
            device_id_type=MESH,
        )

    def start(self, value):
        self.buf[self.me] = value

        def body(step, carry):
            self.copy(step, self.me, lax.rem(self.me + step, self.count)).start()
            return carry

        lax.fori_loop(1, self.count, body, 0)

    def finish(self):
        def body(step, carry):
            peer = lax.rem(self.me + step, self.count)
            self.copy(step, peer, peer).wait_recv()
            self.copy(step, self.me, peer).wait_send()
            return carry

        lax.fori_loop(1, self.count, body, 0)
        total = self.buf[0]
        for slot in range(1, self.count):
            total = total + self.buf[slot]
        return total


def gather_kernel(
    taps_hbm,
    gain_hbm,
    basis4,
    basis2,
    classes_hbm,
    ports_hbm,
    qs_out,
    ws_out,
    sums_out,
    taps_ref,
    gain_ref,
    pad,
    q2,
    qs,
    w2,
    ws,
    coefs,
    diag,
    classes,
    ports,
    sums,
    qq_y,
    qq_x,
    g_y,
    g_x,
    local_sem,
    block_sem,
    halo_send,
    halo_recv,
    qq_y_send,
    qq_y_recv,
    qq_x_send,
    qq_x_recv,
    g_y_send,
    g_y_recv,
    g_x_send,
    g_x_recv,
):
    size_x, size_y, size_z = classes.shape
    rows = size_x * size_y
    first = (BLOCKS - 1) * COLS
    gx, gy = lax.axis_index("gx"), lax.axis_index("gy")
    nx, ny = lax.axis_size("gx"), lax.axis_size("gy")
    chunks, _, span = qs.shape
    per_chunk = span // size_z

    barrier = pltpu.get_barrier_semaphore()
    for axis, me, count in (("gx", gx, nx), ("gy", gy, ny)):

        def greet(step, carry, axis=axis, me=me, count=count):
            pl.semaphore_signal(
                barrier, inc=1, device_id={axis: lax.rem(me + step, count)}, device_id_type=MESH
            )
            return carry

        lax.fori_loop(1, count, greet, 0)

    load_classes = pltpu.make_async_copy(classes_hbm, classes, local_sem.at[0])
    load_ports = pltpu.make_async_copy(ports_hbm, ports, local_sem.at[1])
    load_basis = pltpu.make_async_copy(basis2, q2, local_sem.at[2])
    load_block = pltpu.make_async_copy(
        basis4.at[pl.ds(first, COLS)],
        pad.at[:, pl.ds(REACH, size_x), pl.ds(size_y, size_y), :],
        block_sem,
    )
    load_taps = pltpu.make_async_copy(taps_hbm, taps_ref, local_sem.at[3])
    load_gain = pltpu.make_async_copy(gain_hbm, gain_ref, local_sem.at[4])
    load_taps.start()
    load_gain.start()
    load_classes.start()
    load_ports.start()
    load_block.start()
    load_basis.start()
    pl.semaphore_wait(barrier, nx + ny - 2)

    inner_x, inner_y = pl.ds(REACH, size_x), pl.ds(size_y, size_y)
    ways = (
        ("gy", 1, gy < ny - 1, gy > 0,
         (slice(None), pl.ds(size_y - REACH, REACH)), (inner_x, pl.ds(size_y - REACH, REACH))),
        ("gy", -1, gy > 0, gy < ny - 1,
         (slice(None), pl.ds(0, REACH)), (inner_x, pl.ds(2 * size_y, REACH))),
        ("gx", 1, gx < nx - 1, gx > 0,
         (pl.ds(size_x - REACH, REACH), slice(None)), (pl.ds(0, REACH), inner_y)),
        ("gx", -1, gx > 0, gx < nx - 1,
         (pl.ds(0, REACH), slice(None)), (pl.ds(REACH + size_x, REACH), inner_y)),
    )

    def halo(way, group):
        axis, step, _, _, (from_x, from_y), (to_x, to_y) = ways[way]
        return pltpu.make_async_remote_copy(
            src_ref=basis4.at[pl.ds(first + group * GROUP, GROUP), from_x, from_y, :],
            dst_ref=pad.at[pl.ds(group * GROUP, GROUP), to_x, to_y, :],
            send_sem=halo_send.at[way, group],
            recv_sem=halo_recv.at[way, group],
            device_id={axis: lax.axis_index(axis) + step},
            device_id_type=MESH,
        )

    for group in range(COLS // GROUP):
        for way in range(4):

            @pl.when(ways[way][2])
            def _(way=way, group=group):
                halo(way, group).start()

    for way in range(4):

        @pl.when(jnp.logical_not(ways[way][3]))
        def _(way=way):
            to_x, to_y = ways[way][5]
            pad[:, to_x, to_y, :] = jnp.zeros((COLS, to_x.size, to_y.size, size_z), jnp.float32)

    load_taps.wait()
    load_gain.wait()
    load_classes.wait()
    load_ports.wait()
    lane = lax.broadcasted_iota(jnp.int32, (size_y, size_z), 1)

    def make_coefs(x, carry):
        kind, port = classes[x], ports[x]
        bits = [(kind & (1 << b)) != 0 for b in range(3)]
        gain = jnp.zeros((size_y, size_z), jnp.float32)
        for p in range(PORTS):
            gain = jnp.where(port == p + 1, gain_ref[p], gain)
        total = 1.0 + gain
        for t in range(6 * REACH):
            level = [taps_ref[m, t] for m in range(MAT)]
            for bit in bits:
                level = [
                    jnp.where(bit, level[2 * i + 1], level[2 * i]) for i in range(len(level) // 2)
                ]
            total = total + level[0]
            value = level[0]
            if t >= 4 * REACH:
                k = offset_of(t - 4 * REACH)
                value = jnp.where((lane + k >= 0) & (lane + k < size_z), value, 0.0)
            coefs[t, x] = value
        diag[x] = total
        return carry

    lax.fori_loop(0, size_x, make_coefs, 0)
    load_block.wait()

    def along_z(x, carry):
        for c in range(COLS):
            own = pad[c, x + REACH, pl.ds(size_y, size_y), :]
            image = diag[x] * own
            for j in range(2 * REACH):
                shifted = pltpu.roll(own, (-offset_of(j)) % size_z, 1)
                image = image - coefs[4 * REACH + j, x] * shifted
            w2[pl.ds(pl.multiple_of(c * rows + x * size_y, size_y), size_y), :] = image
        return carry

    lax.fori_loop(0, size_x, along_z, 0)
    load_basis.wait()

    def gather(ref, count, chunk):
        return jnp.concatenate(
            [
                ref[pl.ds(chunk * per_chunk + i, count, stride=rows), :]
                for i in range(per_chunk)
            ],
            axis=1,
        )

    def own_products(chunk, acc):
        both = halves(gather(q2, BLOCKS * COLS, chunk))
        qs[chunk] = both
        return acc + lax.dot_general(both, both, NT, preferred_element_type=jnp.float32)

    wide = BLOCKS * COLS
    acc = lax.fori_loop(0, chunks, own_products, jnp.zeros((2 * wide, 2 * wide), jnp.float32))
    store_qs = pltpu.make_async_copy(qs, qs_out, local_sem.at[5])
    store_qs.start()
    acc = acc[:wide] + acc[wide:]
    local_qq = acc[:, :wide] + acc[:, wide:]
    fill = jnp.zeros((wide, 128 - wide), jnp.float32)
    exchange = Exchange("gy", qq_y, qq_y_send, qq_y_recv)
    exchange.start(jnp.concatenate([local_qq, fill], axis=1))

    for axis, first_way in (("gy", 0), ("gx", 2)):
        for group in range(COLS // GROUP):
            for way in (first_way, first_way + 1):

                @pl.when(ways[way][3])
                def _(way=way, group=group):
                    halo(way, group).wait_recv()

            def along(x, carry, axis=axis, group=group):
                columns = range(group * GROUP, (group + 1) * GROUP)
                places = [
                    pl.ds(pl.multiple_of(c * rows + x * size_y, size_y), size_y) for c in columns
                ]
                images = [w2[place, :] for place in places]
                for j in range(2 * REACH):
                    k = offset_of(j)
                    if axis == "gx":
                        coef, at_x, at_y = coefs[j, x], x + REACH + k, inner_y
                    else:
                        coef, at_x = coefs[2 * REACH + j, x], x + REACH
                        at_y = pl.ds(size_y + k, size_y)
                    for i, c in enumerate(columns):
                        images[i] = images[i] - coef * pad[c, at_x, at_y, :]
                for place, image in zip(places, images):
                    w2[place, :] = image
                return carry

            lax.fori_loop(0, size_x, along, 0)

    exchange_x = Exchange("gx", qq_x, qq_x_send, qq_x_recv)
    exchange_x.start(exchange.finish())

    def image_products(chunk, acc):
        both = halves(gather(w2, COLS, chunk))
        ws[chunk] = both
        acc_q, acc_w = acc
        acc_q = acc_q + lax.dot_general(both, qs[chunk], NT, preferred_element_type=jnp.float32)
        acc_w = acc_w + lax.dot_general(both, both, NT, preferred_element_type=jnp.float32)
        return acc_q, acc_w

    acc_q, acc_w = lax.fori_loop(
        0,
        chunks,
        image_products,
        (
            jnp.zeros((2 * COLS, 2 * wide), jnp.float32),
            jnp.zeros((2 * COLS, 2 * COLS), jnp.float32),
        ),
    )
    acc_q, acc_w = acc_q[:COLS] + acc_q[COLS:], acc_w[:COLS] + acc_w[COLS:]
    local_g = jnp.concatenate(
        [
            acc_q[:, :wide] + acc_q[:, wide:],
            acc_w[:, :COLS] + acc_w[:, COLS:],
            jnp.zeros((COLS, 128 - wide - COLS), jnp.float32),
        ],
        axis=1,
    )
    g_exchange = Exchange("gy", g_y, g_y_send, g_y_recv)
    g_exchange.start(local_g)
    store_ws = pltpu.make_async_copy(ws, ws_out, local_sem.at[6])
    store_ws.start()
    sums[COLS:, :] = exchange_x.finish()
    g_exchange_x = Exchange("gx", g_x, g_x_send, g_x_recv)
    g_exchange_x.start(g_exchange.finish())
    sums[:COLS, :] = g_exchange_x.finish()
    store_sums = pltpu.make_async_copy(sums, sums_out, local_sem.at[7])
    store_sums.start()
    for group in range(COLS // GROUP):
        for way in range(4):

            @pl.when(ways[way][2])
            def _(way=way, group=group):
                halo(way, group).wait_send()

    store_qs.wait()
    store_ws.wait()
    store_sums.wait()


def combine_kernel(
    total_cells,
    qs_hbm,
    ws_hbm,
    sums_hbm,
    out_hbm,
    proj_hbm,
    tri_hbm,
    qs,
    ws,
    both_sums,
    out2,
    proj_ref,
    tri_ref,
    qs_sem,
    ws_sem,
    small_sem,
    out_sem,
):
    chunks, _, span = qs.shape
    rows, size_z = out2.shape[0] // COLS, out2.shape[1]
    per_chunk = span // size_z
    wide = BLOCKS * COLS
    load_sums = pltpu.make_async_copy(sums_hbm, both_sums, small_sem.at[0])
    load_sums.start()
    load_ws = pltpu.make_async_copy(ws_hbm, ws, ws_sem)
    load_qs = pltpu.make_async_copy(qs_hbm, qs, qs_sem)
    load_ws.start()
    load_qs.start()
    load_sums.wait()
    sums = both_sums[:COLS, :] / total_cells
    sum_qq = both_sums[COLS:, :]
    proj_t = sums[:, :wide]
    proj_ref[...] = proj_t
    row = lax.broadcasted_iota(jnp.int32, (wide, wide), 0)
    column = lax.broadcasted_iota(jnp.int32, (wide, wide), 1)
    middle = jnp.where(row == column, 2.0, 0.0) - sum_qq[:, :wide] / total_cells
    left = jnp.dot(proj_t, middle, precision=HIGHEST, preferred_element_type=jnp.float32)
    gram = sums[:, wide : wide + COLS] - lax.dot_general(
        left, proj_t, NT, precision=HIGHEST, preferred_element_type=jnp.float32
    )
    row = lax.broadcasted_iota(jnp.int32, (COLS, COLS), 0)
    column = lax.broadcasted_iota(jnp.int32, (COLS, COLS), 1)
    eye = jnp.where(row == column, 1.0, 0.0)
    table = jnp.concatenate([-proj_t, eye, gram], axis=1)
    base = wide + COLS
    index = lax.broadcasted_iota(jnp.int32, table.shape, 0)
    for j in range(COLS):
        pivot = table[j : j + 1, :]
        scale = lax.rsqrt(pivot[:, base + j : base + j + 1])
        pivot = pivot * scale
        factor = table[:, base + j : base + j + 1] * scale
        table = jnp.where(index == j, pivot, jnp.where(index > j, table - factor * pivot, table))
    tri_ref[...] = jnp.where(row <= column, table[:, base:], 0.0)
    store_proj = pltpu.make_async_copy(proj_ref, proj_hbm, small_sem.at[1])
    store_tri = pltpu.make_async_copy(tri_ref, tri_hbm, small_sem.at[2])
    store_proj.start()
    store_tri.start()

    mix = table[:, :base]
    high = mix.astype(jnp.bfloat16).astype(jnp.float32)
    mix = jnp.concatenate([high, mix - high], axis=0)
    mix = jnp.concatenate([mix[:, :wide], mix[:, :wide]], axis=1), jnp.concatenate(
        [mix[:, wide:], mix[:, wide:]], axis=1
    )
    mix_q, mix_w = mix[0].astype(jnp.bfloat16), mix[1].astype(jnp.bfloat16)

    load_ws.wait()
    load_qs.wait()

    def store(chunk):
        part = pl.ds(pl.multiple_of(chunk * per_chunk, per_chunk), per_chunk)
        return pltpu.make_async_copy(
            out2.reshape(COLS, rows, size_z).at[:, part, :], out_hbm.at[:, part, :], out_sem.at[chunk]
        )

    def combine(chunk, carry):
        result = jnp.dot(mix_q, qs[chunk], preferred_element_type=jnp.float32)
        result = result + jnp.dot(mix_w, ws[chunk], preferred_element_type=jnp.float32)
        result = result[:COLS] + result[COLS:]
        for i in range(per_chunk):
            out2[pl.ds(chunk * per_chunk + i, COLS, stride=rows), :] = result[
                :, i * size_z : (i + 1) * size_z
            ]
        store(chunk).start()
        return carry

    lax.fori_loop(0, chunks, combine, 0)

    def drain(chunk, carry):
        store(chunk).wait()
        return carry

    lax.fori_loop(0, chunks, drain, 0)
    store_proj.wait()
    store_tri.wait()


def per_device(basis, classes, ports, taps, port_gain):
    size_x, size_y, size_z = classes.shape
    rows = size_x * size_y
    wide = BLOCKS * COLS
    nx, ny = lax.axis_size("gx"), lax.axis_size("gy")
    per_chunk = 16 if rows % 16 == 0 else 1
    chunks, span = rows // per_chunk, per_chunk * size_z
    vmem = functools.partial(pltpu.VMEM, dtype=jnp.float32)
    dma = pltpu.SemaphoreType.DMA
    hbm = pl.BlockSpec(memory_space=pltpu.HBM)
    any_space = pl.BlockSpec(memory_space=pl.ANY)
    groups = COLS // GROUP
    qs_shape, ws_shape = (chunks, 2 * wide, span), (chunks, 2 * COLS, span)
    sums_shape = (COLS + wide, 128)
    qs, ws, sums = pl.pallas_call(
        gather_kernel,
        out_shape=(
            jax.ShapeDtypeStruct(qs_shape, jnp.bfloat16),
            jax.ShapeDtypeStruct(ws_shape, jnp.bfloat16),
            jax.ShapeDtypeStruct(sums_shape, jnp.float32),
        ),
        in_specs=[hbm] * 6,
        out_specs=(any_space,) * 3,
        scratch_shapes=[
            pltpu.SMEM(taps.shape, jnp.float32),
            pltpu.SMEM(port_gain.shape, jnp.float32),
            vmem((COLS, size_x + 2 * REACH, 3 * size_y, size_z)),
            vmem((wide * rows, size_z)),
            pltpu.VMEM(qs_shape, jnp.bfloat16),
            vmem((COLS * rows, size_z)),
            pltpu.VMEM(ws_shape, jnp.bfloat16),
            vmem((6 * REACH, size_x, size_y, size_z)),
            vmem((size_x, size_y, size_z)),
            pltpu.VMEM((size_x, size_y, size_z), jnp.int32),
            pltpu.VMEM((size_x, size_y, size_z), jnp.int32),
            vmem(sums_shape),
            vmem((ny, wide, 128)),
            vmem((nx, wide, 128)),
            vmem((ny, COLS, 128)),
            vmem((nx, COLS, 128)),
            dma((8,)),
            dma,
            dma((4, groups)),
            dma((4, groups)),
            dma((ny,)),
            dma((ny,)),
            dma((nx,)),
            dma((nx,)),
            dma((ny,)),
            dma((ny,)),
            dma((nx,)),
            dma((nx,)),
        ],
        compiler_params=pltpu.CompilerParams(
            collective_id=0, has_side_effects=True, vmem_limit_bytes=40 * 1024 * 1024
        ),
    )(
        *(
            pltpu.with_memory_space_constraint(operand, pltpu.HBM)
            for operand in (
                taps, port_gain, basis, basis.reshape(wide * rows, size_z), classes, ports
            )
        )
    )
    out, projection, triangle = pl.pallas_call(
        functools.partial(combine_kernel, float(rows * size_z * nx * ny)),
        out_shape=(
            jax.ShapeDtypeStruct((COLS, rows, size_z), jnp.float32),
            jax.ShapeDtypeStruct((COLS, wide), jnp.float32),
            jax.ShapeDtypeStruct((COLS, COLS), jnp.float32),
        ),
        in_specs=[any_space] * 3,
        out_specs=(hbm,) * 3,
        scratch_shapes=[
            pltpu.VMEM(qs_shape, jnp.bfloat16),
            pltpu.VMEM(ws_shape, jnp.bfloat16),
            vmem(sums_shape),
            vmem((COLS * rows, size_z)),
            vmem((COLS, wide)),
            vmem((COLS, COLS)),
            dma,
            dma,
            dma((3,)),
            dma((chunks,)),
        ],
        compiler_params=pltpu.CompilerParams(vmem_limit_bytes=24 * 1024 * 1024),
    )(qs, ws, sums)
    return out.reshape(COLS, size_x, size_y, size_z), projection.T, triangle


def solution(mesh):
    in_specs = (P(None, "gx", "gy", None), P("gx", "gy", None), P("gx", "gy", None), P(), P())
    out_specs = (P(None, "gx", "gy", None), P(), P())
    return jax.shard_map(
        per_device, mesh=mesh, in_specs=in_specs, out_specs=out_specs, check_vma=False
    )
```

```python
import functools

import jax
import jax.numpy as jnp
from jax import lax
from jax.experimental import pallas as pl
from jax.experimental.pallas import tpu as pltpu
from jax.sharding import PartitionSpec as P

COLS = 8
BLOCKS = 4
REACH = 7
MAT = 8
PORTS = 8
GROUP = 4
LAYERS = 4
UNROLL = 4
MESH = pl.DeviceIdType.MESH
NT = (((1,), (1,)), ((), ()))
HIGHEST = lax.Precision.HIGHEST


def offset_of(j):
    return j - REACH if j < REACH else j - REACH + 1


def halves(value):
    high = value.astype(jnp.bfloat16).astype(jnp.float32)
    return jnp.concatenate([high, value - high], axis=0).astype(jnp.bfloat16)


class Exchange:
    def __init__(self, axis, buf, send, recv):
        self.axis, self.buf, self.send, self.recv = axis, buf, send, recv
        self.me, self.count = lax.axis_index(axis), lax.axis_size(axis)

    def copy(self, step, slot, peer):
        return pltpu.make_async_remote_copy(
            src_ref=self.buf.at[slot],
            dst_ref=self.buf.at[slot],
            send_sem=self.send.at[step],
            recv_sem=self.recv.at[slot],
            device_id={self.axis: peer},
            device_id_type=MESH,
        )

    def start(self, value):
        self.buf[self.me] = value

        def body(step, carry):
            self.copy(step, self.me, lax.rem(self.me + step, self.count)).start()
            return carry

        lax.fori_loop(1, self.count, body, 0)

    def finish(self):
        def body(step, carry):
            peer = lax.rem(self.me + step, self.count)
            self.copy(step, peer, peer).wait_recv()
            self.copy(step, self.me, peer).wait_send()
            return carry

        lax.fori_loop(1, self.count, body, 0)
        total = self.buf[0]
        for slot in range(1, self.count):
            total = total + self.buf[slot]
        return total


def gather_kernel(
    taps_hbm,
    gain_hbm,
    basis4,
    basis2,
    classes_hbm,
    ports_hbm,
    qs,
    ws,
    sums,
    taps_ref,
    gain_ref,
    pad,
    q2,
    w2,
    coefs,
    diag,
    classes,
    ports,
    qq_y,
    qq_x,
    g_y,
    g_x,
    local_sem,
    block_sem,
    halo_send,
    halo_recv,
    qq_y_send,
    qq_y_recv,
    qq_x_send,
    qq_x_recv,
    g_y_send,
    g_y_recv,
    g_x_send,
    g_x_recv,
):
    size_x, size_y, size_z = classes.shape
    rows = size_x * size_y
    first = (BLOCKS - 1) * COLS
    gx, gy = lax.axis_index("gx"), lax.axis_index("gy")
    nx, ny = lax.axis_size("gx"), lax.axis_size("gy")
    chunks, _, span = qs.shape
    per_chunk = span // size_z

    barrier = pltpu.get_barrier_semaphore()
    for axis, me, count in (("gx", gx, nx), ("gy", gy, ny)):

        def greet(step, carry, axis=axis, me=me, count=count):
            pl.semaphore_signal(
                barrier, inc=1, device_id={axis: lax.rem(me + step, count)}, device_id_type=MESH
            )
            return carry

        lax.fori_loop(1, count, greet, 0)

    load_classes = pltpu.make_async_copy(classes_hbm, classes, local_sem.at[0])
    load_ports = pltpu.make_async_copy(ports_hbm, ports, local_sem.at[1])
    load_basis = pltpu.make_async_copy(basis2, q2, local_sem.at[2])
    load_block = pltpu.make_async_copy(
        basis4.at[pl.ds(first, COLS)],
        pad.at[:, pl.ds(REACH, size_x), pl.ds(size_y, size_y), :],
        block_sem,
    )
    load_taps = pltpu.make_async_copy(taps_hbm, taps_ref, local_sem.at[3])
    load_gain = pltpu.make_async_copy(gain_hbm, gain_ref, local_sem.at[4])
    load_taps.start()
    load_gain.start()
    load_classes.start()
    load_ports.start()
    load_block.start()
    load_basis.start()
    pl.semaphore_wait(barrier, nx + ny - 2)

    inner_x, inner_y = pl.ds(REACH, size_x), pl.ds(size_y, size_y)
    ways = (
        ("gy", 1, gy < ny - 1, gy > 0,
         (slice(None), pl.ds(size_y - REACH, REACH)), (inner_x, pl.ds(size_y - REACH, REACH))),
        ("gy", -1, gy > 0, gy < ny - 1,
         (slice(None), pl.ds(0, REACH)), (inner_x, pl.ds(2 * size_y, REACH))),
        ("gx", 1, gx < nx - 1, gx > 0,
         (pl.ds(size_x - REACH, REACH), slice(None)), (pl.ds(0, REACH), inner_y)),
        ("gx", -1, gx > 0, gx < nx - 1,
         (pl.ds(0, REACH), slice(None)), (pl.ds(REACH + size_x, REACH), inner_y)),
    )

    def halo(way, group):
        axis, step, _, _, (from_x, from_y), (to_x, to_y) = ways[way]
        return pltpu.make_async_remote_copy(
            src_ref=basis4.at[pl.ds(first + group * GROUP, GROUP), from_x, from_y, :],
            dst_ref=pad.at[pl.ds(group * GROUP, GROUP), to_x, to_y, :],
            send_sem=halo_send.at[way, group],
            recv_sem=halo_recv.at[way, group],
            device_id={axis: lax.axis_index(axis) + step},
            device_id_type=MESH,
        )

    for group in range(COLS // GROUP):
        for way in (2, 3, 0, 1):

            @pl.when(ways[way][2])
            def _(way=way, group=group):
                halo(way, group).start()

    for way in range(4):

        @pl.when(jnp.logical_not(ways[way][3]))
        def _(way=way):
            to_x, to_y = ways[way][5]
            pad[:, to_x, to_y, :] = jnp.zeros((COLS, to_x.size, to_y.size, size_z), jnp.float32)

    load_taps.wait()
    load_gain.wait()
    load_classes.wait()
    load_ports.wait()
    layers = LAYERS if size_x % LAYERS == 0 else 1
    lane = lax.broadcasted_iota(jnp.int32, (layers, size_y, size_z), 2)

    def make_coefs(step, carry):
        place = pl.ds(step * layers, layers)
        kind, port = classes[place], ports[place]
        bits = [(kind & (1 << b)) != 0 for b in range(3)]
        total = jnp.ones(kind.shape, jnp.float32)
        for p in range(PORTS):
            total = jnp.where(port == p + 1, 1.0 + gain_ref[p], total)
        for t in range(6 * REACH):
            level = [taps_ref[m, t] for m in range(MAT)]
            for bit in bits:
                level = [
                    jnp.where(bit, level[2 * i + 1], level[2 * i]) for i in range(len(level) // 2)
                ]
            value = level[0]
            total = total + value
            if t >= 4 * REACH:
                k = offset_of(t - 4 * REACH)
                value = jnp.where(lane < -k if k < 0 else lane >= size_z - k, 0.0, value)
            coefs[t, place] = value
        diag[place] = total
        return carry

    lax.fori_loop(0, size_x // layers, make_coefs, 0)
    load_block.wait()

    def along_z(x, carry):
        for c in range(COLS):
            own = pad[c, x + REACH, pl.ds(size_y, size_y), :]
            image = diag[x] * own
            for j in range(2 * REACH):
                shifted = pltpu.roll(own, (-offset_of(j)) % size_z, 1)
                image = image - coefs[4 * REACH + j, x] * shifted
            w2[pl.ds(pl.multiple_of(c * rows + x * size_y, size_y), size_y), :] = image
        return carry

    lax.fori_loop(0, size_x, along_z, 0)
    load_basis.wait()

    def gather(ref, count, chunk):
        return jnp.concatenate(
            [
                ref[pl.ds(chunk * per_chunk + i, count, stride=rows), :]
                for i in range(per_chunk)
            ],
            axis=1,
        )

    def own_products(chunk, acc):
        both = halves(gather(q2, BLOCKS * COLS, chunk))
        qs[chunk] = both
        return acc + lax.dot_general(both, both, NT, preferred_element_type=jnp.float32)

    wide = BLOCKS * COLS
    acc = lax.fori_loop(
        0, chunks, own_products, jnp.zeros((2 * wide, 2 * wide), jnp.float32), unroll=UNROLL
    )
    acc = acc[:wide] + acc[wide:]
    local_qq = acc[:, :wide] + acc[:, wide:]
    fill = jnp.zeros((wide, 128 - wide), jnp.float32)
    exchange = Exchange("gy", qq_y, qq_y_send, qq_y_recv)
    exchange.start(jnp.concatenate([local_qq, fill], axis=1))

    for axis, first_way in (("gy", 0), ("gx", 2)):
        for group in range(COLS // GROUP):
            for way in (first_way, first_way + 1):

                @pl.when(ways[way][3])
                def _(way=way, group=group):
                    halo(way, group).wait_recv()

            def along(x, carry, axis=axis, group=group):
                columns = range(group * GROUP, (group + 1) * GROUP)
                places = [
                    pl.ds(pl.multiple_of(c * rows + x * size_y, size_y), size_y) for c in columns
                ]
                images = [w2[place, :] for place in places]
                for j in range(2 * REACH):
                    k = offset_of(j)
                    if axis == "gx":
                        coef, at_x, at_y = coefs[j, x], x + REACH + k, inner_y
                    else:
                        coef, at_x = coefs[2 * REACH + j, x], x + REACH
                        at_y = pl.ds(size_y + k, size_y)
                    for i, c in enumerate(columns):
                        images[i] = images[i] - coef * pad[c, at_x, at_y, :]
                for place, image in zip(places, images):
                    w2[place, :] = image
                return carry

            lax.fori_loop(0, size_x, along, 0)

    exchange_x = Exchange("gx", qq_x, qq_x_send, qq_x_recv)
    exchange_x.start(exchange.finish())

    def image_products(chunk, acc):
        both = halves(gather(w2, COLS, chunk))
        ws[chunk] = both
        acc_q, acc_w = acc
        acc_q = acc_q + lax.dot_general(both, qs[chunk], NT, preferred_element_type=jnp.float32)
        acc_w = acc_w + lax.dot_general(both, both, NT, preferred_element_type=jnp.float32)
        return acc_q, acc_w

    acc_q, acc_w = lax.fori_loop(
        0,
        chunks,
        image_products,
        (
            jnp.zeros((2 * COLS, 2 * wide), jnp.float32),
            jnp.zeros((2 * COLS, 2 * COLS), jnp.float32),
        ),
        unroll=UNROLL,
    )
    acc_q, acc_w = acc_q[:COLS] + acc_q[COLS:], acc_w[:COLS] + acc_w[COLS:]
    local_g = jnp.concatenate(
        [
            acc_q[:, :wide] + acc_q[:, wide:],
            acc_w[:, :COLS] + acc_w[:, COLS:],
            jnp.zeros((COLS, 128 - wide - COLS), jnp.float32),
        ],
        axis=1,
    )
    g_exchange = Exchange("gy", g_y, g_y_send, g_y_recv)
    g_exchange.start(local_g)
    sums[COLS:, :] = exchange_x.finish()
    g_exchange_x = Exchange("gx", g_x, g_x_send, g_x_recv)
    g_exchange_x.start(g_exchange.finish())
    sums[:COLS, :] = g_exchange_x.finish()
    for group in range(COLS // GROUP):
        for way in range(4):

            @pl.when(ways[way][2])
            def _(way=way, group=group):
                halo(way, group).wait_send()


def combine_kernel(
    total_cells,
    qs,
    ws,
    both_sums,
    out_hbm,
    proj_hbm,
    tri_hbm,
    out2,
    proj_ref,
    tri_ref,
    small_sem,
    out_sem,
):
    chunks, _, span = qs.shape
    rows, size_z = out2.shape[0] // COLS, out2.shape[1]
    per_chunk = span // size_z
    wide = BLOCKS * COLS
    sums = both_sums[:COLS, :] / total_cells
    sum_qq = both_sums[COLS:, :]
    proj_t = sums[:, :wide]
    proj_ref[...] = proj_t
    row = lax.broadcasted_iota(jnp.int32, (wide, wide), 0)
    column = lax.broadcasted_iota(jnp.int32, (wide, wide), 1)
    middle = jnp.where(row == column, 2.0, 0.0) - sum_qq[:, :wide] / total_cells
    left = jnp.dot(proj_t, middle, precision=HIGHEST, preferred_element_type=jnp.float32)
    gram = sums[:, wide : wide + COLS] - lax.dot_general(
        left, proj_t, NT, precision=HIGHEST, preferred_element_type=jnp.float32
    )
    row = lax.broadcasted_iota(jnp.int32, (COLS, COLS), 0)
    column = lax.broadcasted_iota(jnp.int32, (COLS, COLS), 1)
    eye = jnp.where(row == column, 1.0, 0.0)
    table = jnp.concatenate([-proj_t, eye, gram], axis=1)
    base = wide + COLS
    index = lax.broadcasted_iota(jnp.int32, table.shape, 0)
    for j in range(COLS - 1):
        factor = jnp.broadcast_to(table[:, base + j : base + j + 1], table.shape)
        factor = jnp.where(index > j, factor / factor[j : j + 1, :], 0.0)
        table = table - factor * table[j : j + 1, :]
    pivots = jnp.sum(jnp.where(row == column, table[:, base:], 0.0), axis=1, keepdims=True)
    table = table * lax.rsqrt(pivots)
    tri_ref[...] = jnp.where(row <= column, table[:, base:], 0.0)
    store_proj = pltpu.make_async_copy(proj_ref, proj_hbm, small_sem.at[0])
    store_tri = pltpu.make_async_copy(tri_ref, tri_hbm, small_sem.at[1])
    store_proj.start()
    store_tri.start()

    mix = table[:, :base]
    high = mix.astype(jnp.bfloat16).astype(jnp.float32)
    mix = jnp.concatenate([high, mix - high], axis=0)
    mix = jnp.concatenate([mix[:, :wide], mix[:, :wide]], axis=1), jnp.concatenate(
        [mix[:, wide:], mix[:, wide:]], axis=1
    )
    mix_q, mix_w = mix[0].astype(jnp.bfloat16), mix[1].astype(jnp.bfloat16)

    def store(chunk):
        part = pl.ds(pl.multiple_of(chunk * per_chunk, per_chunk), per_chunk)
        return pltpu.make_async_copy(
            out2.reshape(COLS, rows, size_z).at[:, part, :], out_hbm.at[:, part, :], out_sem.at[chunk]
        )

    def combine(chunk, carry):
        result = jnp.dot(mix_q, qs[chunk], preferred_element_type=jnp.float32)
        result = result + jnp.dot(mix_w, ws[chunk], preferred_element_type=jnp.float32)
        result = result[:COLS] + result[COLS:]
        for i in range(per_chunk):
            out2[pl.ds(chunk * per_chunk + i, COLS, stride=rows), :] = result[
                :, i * size_z : (i + 1) * size_z
            ]
        store(chunk).start()
        return carry

    lax.fori_loop(0, chunks, combine, 0, unroll=UNROLL)

    def drain(chunk, carry):
        store(chunk).wait()
        return carry

    lax.fori_loop(0, chunks, drain, 0)
    store_proj.wait()
    store_tri.wait()


def per_device(basis, classes, ports, taps, port_gain):
    size_x, size_y, size_z = classes.shape
    rows = size_x * size_y
    wide = BLOCKS * COLS
    nx, ny = lax.axis_size("gx"), lax.axis_size("gy")
    per_chunk = 16 if rows % 16 == 0 else 1
    chunks, span = rows // per_chunk, per_chunk * size_z
    vmem = functools.partial(pltpu.VMEM, dtype=jnp.float32)
    dma = pltpu.SemaphoreType.DMA
    hbm = pl.BlockSpec(memory_space=pltpu.HBM)
    vmem_spec = pl.BlockSpec(memory_space=pltpu.VMEM)
    groups = COLS // GROUP
    qs_shape, ws_shape = (chunks, 2 * wide, span), (chunks, 2 * COLS, span)
    sums_shape = (COLS + wide, 128)
    qs, ws, sums = pl.pallas_call(
        gather_kernel,
        out_shape=(
            jax.ShapeDtypeStruct(qs_shape, jnp.bfloat16),
            jax.ShapeDtypeStruct(ws_shape, jnp.bfloat16),
            jax.ShapeDtypeStruct(sums_shape, jnp.float32),
        ),
        in_specs=[hbm] * 6,
        out_specs=(vmem_spec,) * 3,
        scratch_shapes=[
            pltpu.SMEM(taps.shape, jnp.float32),
            pltpu.SMEM(port_gain.shape, jnp.float32),
            vmem((COLS, size_x + 2 * REACH, 3 * size_y, size_z)),
            vmem((wide * rows, size_z)),
            vmem((COLS * rows, size_z)),
            vmem((6 * REACH, size_x, size_y, size_z)),
            vmem((size_x, size_y, size_z)),
            pltpu.VMEM((size_x, size_y, size_z), jnp.int32),
            pltpu.VMEM((size_x, size_y, size_z), jnp.int32),
            vmem((ny, wide, 128)),
            vmem((nx, wide, 128)),
            vmem((ny, COLS, 128)),
            vmem((nx, COLS, 128)),
            dma((5,)),
            dma,
            dma((4, groups)),
            dma((4, groups)),
            dma((ny,)),
            dma((ny,)),
            dma((nx,)),
            dma((nx,)),
            dma((ny,)),
            dma((ny,)),
            dma((nx,)),
            dma((nx,)),
        ],
        compiler_params=pltpu.CompilerParams(
            collective_id=0, has_side_effects=True, vmem_limit_bytes=40 * 1024 * 1024
        ),
    )(
        *(
            pltpu.with_memory_space_constraint(operand, pltpu.HBM)
            for operand in (
                taps, port_gain, basis, basis.reshape(wide * rows, size_z), classes, ports
            )
        )
    )
    out, projection, triangle = pl.pallas_call(
        functools.partial(combine_kernel, float(rows * size_z * nx * ny)),
        out_shape=(
            jax.ShapeDtypeStruct((COLS, rows, size_z), jnp.float32),
            jax.ShapeDtypeStruct((COLS, wide), jnp.float32),
            jax.ShapeDtypeStruct((COLS, COLS), jnp.float32),
        ),
        in_specs=[vmem_spec] * 3,
        out_specs=(hbm,) * 3,
        scratch_shapes=[
            vmem((COLS * rows, size_z)),
            vmem((COLS, wide)),
            vmem((COLS, COLS)),
            dma((2,)),
            dma((chunks,)),
        ],
        compiler_params=pltpu.CompilerParams(vmem_limit_bytes=24 * 1024 * 1024),
    )(qs, ws, sums)
    return out.reshape(COLS, size_x, size_y, size_z), projection.T, triangle


def solution(mesh):
    in_specs = (P(None, "gx", "gy", None), P("gx", "gy", None), P("gx", "gy", None), P(), P())
    out_specs = (P(None, "gx", "gy", None), P(), P())
    return jax.shard_map(
        per_device, mesh=mesh, in_specs=in_specs, out_specs=out_specs, check_vma=False
    )
```

```python
import functools

import jax
import jax.numpy as jnp
from jax import lax
from jax.experimental import pallas as pl
from jax.experimental.pallas import tpu as pltpu
from jax.sharding import PartitionSpec as P

COLS = 8
BLOCKS = 4
REACH = 7
MAT = 8
PORTS = 8
GROUP = 4
LAYERS = 4
UNROLL = 4
MESH = pl.DeviceIdType.MESH
NT = (((1,), (1,)), ((), ()))
HIGHEST = lax.Precision.HIGHEST


def offset_of(j):
    return j - REACH if j < REACH else j - REACH + 1


def halves(value):
    high = value.astype(jnp.bfloat16).astype(jnp.float32)
    return jnp.concatenate([high, value - high], axis=0).astype(jnp.bfloat16)


class Exchange:
    def __init__(self, axis, buf, send, recv):
        self.axis, self.buf, self.send, self.recv = axis, buf, send, recv
        self.me, self.count = lax.axis_index(axis), lax.axis_size(axis)

    def copy(self, step, slot, peer):
        return pltpu.make_async_remote_copy(
            src_ref=self.buf.at[slot],
            dst_ref=self.buf.at[slot],
            send_sem=self.send.at[step],
            recv_sem=self.recv.at[slot],
            device_id={self.axis: peer},
            device_id_type=MESH,
        )

    def start(self, value):
        self.buf[self.me] = value

        def body(step, carry):
            self.copy(step, self.me, lax.rem(self.me + step, self.count)).start()
            return carry

        lax.fori_loop(1, self.count, body, 0)

    def finish(self):
        def body(step, carry):
            peer = lax.rem(self.me + step, self.count)
            self.copy(step, peer, peer).wait_recv()
            return carry

        lax.fori_loop(1, self.count, body, 0)
        total = self.buf[0]
        for slot in range(1, self.count):
            total = total + self.buf[slot]
        return total

    def drain(self):
        def body(step, carry):
            self.copy(step, self.me, lax.rem(self.me + step, self.count)).wait_send()
            return carry

        lax.fori_loop(1, self.count, body, 0)


def gather_kernel(
    row_length,
    taps_hbm,
    gain_hbm,
    basis4,
    basis2,
    classes_hbm,
    ports_hbm,
    qs,
    ws,
    sums,
    taps_ref,
    gain_ref,
    pad,
    q2,
    w2,
    coefs,
    diag,
    classes,
    ports,
    relay,
    qq_y,
    qq_x,
    g_y,
    g_x,
    local_sem,
    block_sem,
    halo_send,
    halo_recv,
    relay_send,
    relay_recv,
    forward_send,
    qq_y_send,
    qq_y_recv,
    qq_x_send,
    qq_x_recv,
    g_y_send,
    g_y_recv,
    g_x_send,
    g_x_recv,
):
    size_x, size_y, size_z = classes.shape
    rows = size_x * size_y
    first = (BLOCKS - 1) * COLS
    gx, gy = lax.axis_index("gx"), lax.axis_index("gy")
    nx, ny = lax.axis_size("gx"), lax.axis_size("gy")
    chunks, _, span = qs.shape
    per_chunk = span // size_z

    barrier = pltpu.get_barrier_semaphore()
    for axis, me, count in (("gx", gx, nx), ("gy", gy, ny)):

        def greet(step, carry, axis=axis, me=me, count=count):
            pl.semaphore_signal(
                barrier, inc=1, device_id={axis: lax.rem(me + step, count)}, device_id_type=MESH
            )
            return carry

        lax.fori_loop(1, count, greet, 0)

    load_classes = pltpu.make_async_copy(classes_hbm, classes, local_sem.at[0])
    load_ports = pltpu.make_async_copy(ports_hbm, ports, local_sem.at[1])
    load_basis = pltpu.make_async_copy(basis2, q2, local_sem.at[2])
    load_block = pltpu.make_async_copy(
        basis4.at[pl.ds(first, COLS)],
        pad.at[:, pl.ds(REACH, size_x), pl.ds(size_y, size_y), :],
        block_sem,
    )
    load_taps = pltpu.make_async_copy(taps_hbm, taps_ref, local_sem.at[3])
    load_gain = pltpu.make_async_copy(gain_hbm, gain_ref, local_sem.at[4])
    load_taps.start()
    load_gain.start()
    load_classes.start()
    load_ports.start()
    load_block.start()
    load_basis.start()
    pl.semaphore_wait(barrier, nx + ny - 2)

    inner_x, inner_y = pl.ds(REACH, size_x), pl.ds(size_y, size_y)
    ways = (
        ("gy", 1, gy < ny - 1, gy > 0,
         (slice(None), pl.ds(size_y - REACH, REACH)), (inner_x, pl.ds(size_y - REACH, REACH))),
        ("gy", -1, gy > 0, gy < ny - 1,
         (slice(None), pl.ds(0, REACH)), (inner_x, pl.ds(2 * size_y, REACH))),
        ("gx", 1, gx < nx - 1, gx > 0,
         (pl.ds(size_x - REACH, REACH), slice(None)), (pl.ds(0, REACH), inner_y)),
        ("gx", -1, gx > 0, gx < nx - 1,
         (pl.ds(0, REACH), slice(None)), (pl.ds(REACH + size_x, REACH), inner_y)),
    )

    def halo(way, group):
        axis, step, _, _, (from_x, from_y), (to_x, to_y) = ways[way]
        return pltpu.make_async_remote_copy(
            src_ref=basis4.at[pl.ds(first + group * GROUP, GROUP), from_x, from_y, :],
            dst_ref=pad.at[pl.ds(group * GROUP, GROUP), to_x, to_y, :],
            send_sem=halo_send.at[way, group],
            recv_sem=halo_recv.at[way, group],
            device_id={axis: lax.axis_index(axis) + step},
            device_id_type=MESH,
        )

    turns = []
    if row_length:
        for last in range(row_length - 1, nx - 1, row_length):
            corners = (last + 1 - row_length, last + row_length)
            turns += [(0, last, last + 1, corners), (1, last + 1, last, corners)]
    turning = [jnp.bool_(False), jnp.bool_(False)]
    for direction, source, _, _ in turns:
        turning[direction] = jnp.logical_or(turning[direction], gx == source)

    def to_corner(direction, group, corner):
        from_x, from_y = ways[2 + direction][4]
        return pltpu.make_async_remote_copy(
            src_ref=basis4.at[pl.ds(first + group * GROUP, GROUP), from_x, from_y, :],
            dst_ref=relay.at[direction],
            send_sem=relay_send.at[direction, group],
            recv_sem=relay_recv.at[direction],
            device_id={"gx": corner},
            device_id_type=MESH,
        )

    def from_corner(direction, group, target):
        to_x, to_y = ways[2 + direction][5]
        return pltpu.make_async_remote_copy(
            src_ref=relay.at[direction],
            dst_ref=pad.at[pl.ds(group * GROUP, GROUP), to_x, to_y, :],
            send_sem=forward_send.at[direction],
            recv_sem=halo_recv.at[2 + direction, group],
            device_id={"gx": target},
            device_id_type=MESH,
        )

    def pass_on(early):
        for direction, _, target, corners in turns:
            group = direction if not early else 1 - direction

            @pl.when(gx == corners[group])
            def _(direction=direction, target=target, group=group):
                to_corner(direction, group, target).wait_recv()
                from_corner(direction, group, target).start()

    for direction, source, _, corners in turns:

        @pl.when(gx == source)
        def _(direction=direction, corners=corners):
            for group in range(2):
                to_corner(direction, group, corners[group]).start()

    sends = [ways[way][2] for way in range(4)]
    for direction in range(2):
        sends[2 + direction] = jnp.logical_and(
            sends[2 + direction], jnp.logical_not(turning[direction])
        )
    for group in range(COLS // GROUP):
        for way in (2, 3, 0, 1):

            @pl.when(sends[way])
            def _(way=way, group=group):
                halo(way, group).start()

    for way in range(4):

        @pl.when(jnp.logical_not(ways[way][3]))
        def _(way=way):
            to_x, to_y = ways[way][5]
            pad[:, to_x, to_y, :] = jnp.zeros((COLS, to_x.size, to_y.size, size_z), jnp.float32)

    load_taps.wait()
    load_gain.wait()
    load_classes.wait()
    load_ports.wait()
    layers = LAYERS if size_x % LAYERS == 0 else 1
    lane = lax.broadcasted_iota(jnp.int32, (layers, size_y, size_z), 2)

    def make_coefs(step, carry):
        place = pl.ds(step * layers, layers)
        kind, port = classes[place], ports[place]
        bits = [(kind & (1 << b)) != 0 for b in range(3)]
        total = jnp.ones(kind.shape, jnp.float32)
        for p in range(PORTS):
            total = jnp.where(port == p + 1, 1.0 + gain_ref[p], total)
        for t in range(6 * REACH):
            level = [taps_ref[m, t] for m in range(MAT)]
            for bit in bits:
                level = [
                    jnp.where(bit, level[2 * i + 1], level[2 * i]) for i in range(len(level) // 2)
                ]
            value = level[0]
            total = total + value
            if t >= 4 * REACH:
                k = offset_of(t - 4 * REACH)
                value = jnp.where(lane < -k if k < 0 else lane >= size_z - k, 0.0, value)
            coefs[t, place] = value
        diag[place] = total
        return carry

    lax.fori_loop(0, size_x // layers, make_coefs, 0)
    load_block.wait()

    def along_z(x, carry):
        for c in range(COLS):
            own = pad[c, x + REACH, pl.ds(size_y, size_y), :]
            image = diag[x] * own
            for j in range(2 * REACH):
                shifted = pltpu.roll(own, (-offset_of(j)) % size_z, 1)
                image = image - coefs[4 * REACH + j, x] * shifted
            w2[pl.ds(pl.multiple_of(c * rows + x * size_y, size_y), size_y), :] = image
        return carry

    lax.fori_loop(0, size_x, along_z, 0)
    pass_on(True)
    load_basis.wait()

    def gather(ref, count, chunk):
        return jnp.concatenate(
            [
                ref[pl.ds(chunk * per_chunk + i, count, stride=rows), :]
                for i in range(per_chunk)
            ],
            axis=1,
        )

    def own_products(chunk, acc):
        both = halves(gather(q2, BLOCKS * COLS, chunk))
        qs[chunk] = both
        return acc + lax.dot_general(both, both, NT, preferred_element_type=jnp.float32)

    wide = BLOCKS * COLS
    acc = lax.fori_loop(
        0, chunks, own_products, jnp.zeros((2 * wide, 2 * wide), jnp.float32), unroll=UNROLL
    )
    pass_on(False)
    acc = acc[:wide] + acc[wide:]
    local_qq = acc[:, :wide] + acc[:, wide:]
    fill = jnp.zeros((wide, 128 - wide), jnp.float32)
    exchange = Exchange("gy", qq_y, qq_y_send, qq_y_recv)
    exchange.start(jnp.concatenate([local_qq, fill], axis=1))

    for axis, first_way in (("gy", 0), ("gx", 2)):
        for group in range(COLS // GROUP):
            for way in (first_way, first_way + 1):

                @pl.when(ways[way][3])
                def _(way=way, group=group):
                    halo(way, group).wait_recv()

            def along(x, carry, axis=axis, group=group):
                columns = range(group * GROUP, (group + 1) * GROUP)
                places = [
                    pl.ds(pl.multiple_of(c * rows + x * size_y, size_y), size_y) for c in columns
                ]
                images = [w2[place, :] for place in places]
                for j in range(2 * REACH):
                    k = offset_of(j)
                    if axis == "gx":
                        coef, at_x, at_y = coefs[j, x], x + REACH + k, inner_y
                    else:
                        coef, at_x = coefs[2 * REACH + j, x], x + REACH
                        at_y = pl.ds(size_y + k, size_y)
                    for i, c in enumerate(columns):
                        images[i] = images[i] - coef * pad[c, at_x, at_y, :]
                for place, image in zip(places, images):
                    w2[place, :] = image
                return carry

            lax.fori_loop(0, size_x, along, 0)

    exchange_x = Exchange("gx", qq_x, qq_x_send, qq_x_recv)
    exchange_x.start(exchange.finish())

    def image_products(chunk, acc):
        both = halves(gather(w2, COLS, chunk))
        ws[chunk] = both
        acc_q, acc_w = acc
        acc_q = acc_q + lax.dot_general(both, qs[chunk], NT, preferred_element_type=jnp.float32)
        acc_w = acc_w + lax.dot_general(both, both, NT, preferred_element_type=jnp.float32)
        return acc_q, acc_w

    acc_q, acc_w = lax.fori_loop(
        0,
        chunks,
        image_products,
        (
            jnp.zeros((2 * COLS, 2 * wide), jnp.float32),
            jnp.zeros((2 * COLS, 2 * COLS), jnp.float32),
        ),
        unroll=UNROLL,
    )
    acc_q, acc_w = acc_q[:COLS] + acc_q[COLS:], acc_w[:COLS] + acc_w[COLS:]
    local_g = jnp.concatenate(
        [
            acc_q[:, :wide] + acc_q[:, wide:],
            acc_w[:, :COLS] + acc_w[:, COLS:],
            jnp.zeros((COLS, 128 - wide - COLS), jnp.float32),
        ],
        axis=1,
    )
    g_exchange = Exchange("gy", g_y, g_y_send, g_y_recv)
    g_exchange.start(local_g)
    sums[COLS:, :] = exchange_x.finish()
    g_exchange_x = Exchange("gx", g_x, g_x_send, g_x_recv)
    g_exchange_x.start(g_exchange.finish())
    sums[:COLS, :] = g_exchange_x.finish()
    for group in range(COLS // GROUP):
        for way in range(4):

            @pl.when(sends[way])
            def _(way=way, group=group):
                halo(way, group).wait_send()

    for direction, source, target, corners in turns:
        for group in range(2):

            @pl.when(gx == source)
            def _(direction=direction, group=group, corner=corners[group]):
                to_corner(direction, group, corner).wait_send()

            @pl.when(gx == corners[group])
            def _(direction=direction, group=group, target=target):
                from_corner(direction, group, target).wait_send()

    for each in (exchange, exchange_x, g_exchange, g_exchange_x):
        each.drain()


def combine_kernel(
    total_cells,
    qs,
    ws,
    both_sums,
    out_hbm,
    proj_hbm,
    tri_hbm,
    out2,
    proj_ref,
    tri_ref,
    small_sem,
    out_sem,
):
    chunks, _, span = qs.shape
    rows, size_z = out2.shape[0] // COLS, out2.shape[1]
    per_chunk = span // size_z
    wide = BLOCKS * COLS
    sums = both_sums[:COLS, :] / total_cells
    sum_qq = both_sums[COLS:, :]
    proj_t = sums[:, :wide]
    proj_ref[...] = proj_t
    row = lax.broadcasted_iota(jnp.int32, (wide, wide), 0)
    column = lax.broadcasted_iota(jnp.int32, (wide, wide), 1)
    middle = jnp.where(row == column, 2.0, 0.0) - sum_qq[:, :wide] / total_cells
    left = jnp.dot(proj_t, middle, precision=HIGHEST, preferred_element_type=jnp.float32)
    gram = sums[:, wide : wide + COLS] - lax.dot_general(
        left, proj_t, NT, precision=HIGHEST, preferred_element_type=jnp.float32
    )
    row = lax.broadcasted_iota(jnp.int32, (COLS, COLS), 0)
    column = lax.broadcasted_iota(jnp.int32, (COLS, COLS), 1)
    eye = jnp.where(row == column, 1.0, 0.0)
    table = jnp.concatenate([-proj_t, eye, gram], axis=1)
    base = wide + COLS
    index = lax.broadcasted_iota(jnp.int32, table.shape, 0)
    for j in range(COLS - 1):
        factor = jnp.broadcast_to(table[:, base + j : base + j + 1], table.shape)
        factor = jnp.where(index > j, factor / factor[j : j + 1, :], 0.0)
        table = table - factor * table[j : j + 1, :]
    pivots = jnp.sum(jnp.where(row == column, table[:, base:], 0.0), axis=1, keepdims=True)
    table = table * lax.rsqrt(pivots)
    tri_ref[...] = jnp.where(row <= column, table[:, base:], 0.0)
    store_proj = pltpu.make_async_copy(proj_ref, proj_hbm, small_sem.at[0])
    store_tri = pltpu.make_async_copy(tri_ref, tri_hbm, small_sem.at[1])
    store_proj.start()
    store_tri.start()

    mix = table[:, :base]
    high = mix.astype(jnp.bfloat16).astype(jnp.float32)
    mix = jnp.concatenate([high, mix - high], axis=0)
    mix = jnp.concatenate([mix[:, :wide], mix[:, :wide]], axis=1), jnp.concatenate(
        [mix[:, wide:], mix[:, wide:]], axis=1
    )
    mix_q, mix_w = mix[0].astype(jnp.bfloat16), mix[1].astype(jnp.bfloat16)

    def store(chunk):
        part = pl.ds(pl.multiple_of(chunk * per_chunk, per_chunk), per_chunk)
        return pltpu.make_async_copy(
            out2.reshape(COLS, rows, size_z).at[:, part, :], out_hbm.at[:, part, :], out_sem.at[chunk]
        )

    def combine(chunk, carry):
        result = jnp.dot(mix_q, qs[chunk], preferred_element_type=jnp.float32)
        result = result + jnp.dot(mix_w, ws[chunk], preferred_element_type=jnp.float32)
        result = result[:COLS] + result[COLS:]
        for i in range(per_chunk):
            out2[pl.ds(chunk * per_chunk + i, COLS, stride=rows), :] = result[
                :, i * size_z : (i + 1) * size_z
            ]
        store(chunk).start()
        return carry

    lax.fori_loop(0, chunks, combine, 0, unroll=UNROLL)

    def drain(chunk, carry):
        store(chunk).wait()
        return carry

    lax.fori_loop(0, chunks, drain, 0)
    store_proj.wait()
    store_tri.wait()


def per_device(row_length, basis, classes, ports, taps, port_gain):
    size_x, size_y, size_z = classes.shape
    rows = size_x * size_y
    wide = BLOCKS * COLS
    nx, ny = lax.axis_size("gx"), lax.axis_size("gy")
    per_chunk = 16 if rows % 16 == 0 else 1
    chunks, span = rows // per_chunk, per_chunk * size_z
    vmem = functools.partial(pltpu.VMEM, dtype=jnp.float32)
    dma = pltpu.SemaphoreType.DMA
    hbm = pl.BlockSpec(memory_space=pltpu.HBM)
    vmem_spec = pl.BlockSpec(memory_space=pltpu.VMEM)
    groups = COLS // GROUP
    qs_shape, ws_shape = (chunks, 2 * wide, span), (chunks, 2 * COLS, span)
    sums_shape = (COLS + wide, 128)
    qs, ws, sums = pl.pallas_call(
        functools.partial(gather_kernel, row_length),
        out_shape=(
            jax.ShapeDtypeStruct(qs_shape, jnp.bfloat16),
            jax.ShapeDtypeStruct(ws_shape, jnp.bfloat16),
            jax.ShapeDtypeStruct(sums_shape, jnp.float32),
        ),
        in_specs=[hbm] * 6,
        out_specs=(vmem_spec,) * 3,
        scratch_shapes=[
            pltpu.SMEM(taps.shape, jnp.float32),
            pltpu.SMEM(port_gain.shape, jnp.float32),
            vmem((COLS, size_x + 2 * REACH, 3 * size_y, size_z)),
            vmem((wide * rows, size_z)),
            vmem((COLS * rows, size_z)),
            vmem((6 * REACH, size_x, size_y, size_z)),
            vmem((size_x, size_y, size_z)),
            pltpu.VMEM((size_x, size_y, size_z), jnp.int32),
            pltpu.VMEM((size_x, size_y, size_z), jnp.int32),
            vmem((2, GROUP, REACH, size_y, size_z)),
            vmem((ny, wide, 128)),
            vmem((nx, wide, 128)),
            vmem((ny, COLS, 128)),
            vmem((nx, COLS, 128)),
            dma((5,)),
            dma,
            dma((4, groups)),
            dma((4, groups)),
            dma((2, groups)),
            dma((2,)),
            dma((2,)),
            dma((ny,)),
            dma((ny,)),
            dma((nx,)),
            dma((nx,)),
            dma((ny,)),
            dma((ny,)),
            dma((nx,)),
            dma((nx,)),
        ],
        compiler_params=pltpu.CompilerParams(
            collective_id=0, has_side_effects=True, vmem_limit_bytes=40 * 1024 * 1024
        ),
    )(
        *(
            pltpu.with_memory_space_constraint(operand, pltpu.HBM)
            for operand in (
                taps, port_gain, basis, basis.reshape(wide * rows, size_z), classes, ports
            )
        )
    )
    out, projection, triangle = pl.pallas_call(
        functools.partial(combine_kernel, float(rows * size_z * nx * ny)),
        out_shape=(
            jax.ShapeDtypeStruct((COLS, rows, size_z), jnp.float32),
            jax.ShapeDtypeStruct((COLS, wide), jnp.float32),
            jax.ShapeDtypeStruct((COLS, COLS), jnp.float32),
        ),
        in_specs=[vmem_spec] * 3,
        out_specs=(hbm,) * 3,
        scratch_shapes=[
            vmem((COLS * rows, size_z)),
            vmem((COLS, wide)),
            vmem((COLS, COLS)),
            dma((2,)),
            dma((chunks,)),
        ],
        compiler_params=pltpu.CompilerParams(vmem_limit_bytes=24 * 1024 * 1024),
    )(qs, ws, sums)
    return out.reshape(COLS, size_x, size_y, size_z), projection.T, triangle


def length_of_row(mesh):
    places = [getattr(device, "coords", None) for device in mesh.devices[:, 0]]
    if None in places:
        return 0
    for i in range(1, len(places)):
        if sum(a != b for a, b in zip(places[i - 1], places[i])) > 1:
            return i if len(places) % i == 0 else 0
    return 0


def solution(mesh):
    in_specs = (P(None, "gx", "gy", None), P("gx", "gy", None), P("gx", "gy", None), P(), P())
    out_specs = (P(None, "gx", "gy", None), P(), P())
    return jax.shard_map(
        functools.partial(per_device, length_of_row(mesh)), mesh=mesh, in_specs=in_specs, out_specs=out_specs, check_vma=False
    )
```

```python
import functools

import jax
import jax.numpy as jnp
from jax import lax
from jax.experimental import pallas as pl
from jax.experimental.pallas import tpu as pltpu
from jax.sharding import PartitionSpec as P

COLS = 8
BLOCKS = 4
REACH = 7
MAT = 8
PORTS = 8
GROUP = 4
LAYERS = 4
UNROLL = 4
MESH = pl.DeviceIdType.MESH
NT = (((1,), (1,)), ((), ()))
HIGHEST = lax.Precision.HIGHEST


def offset_of(j):
    return j - REACH if j < REACH else j - REACH + 1


def halves(value):
    high = value.astype(jnp.bfloat16).astype(jnp.float32)
    return jnp.concatenate([high, value - high], axis=0).astype(jnp.bfloat16)


class Exchange:
    def __init__(self, axis, buf, send, recv):
        self.axis, self.buf, self.send, self.recv = axis, buf, send, recv
        self.me, self.count = lax.axis_index(axis), lax.axis_size(axis)

    def copy(self, step, slot, peer):
        return pltpu.make_async_remote_copy(
            src_ref=self.buf.at[slot],
            dst_ref=self.buf.at[slot],
            send_sem=self.send.at[step],
            recv_sem=self.recv.at[slot],
            device_id={self.axis: peer},
            device_id_type=MESH,
        )

    def start(self, value):
        self.buf[self.me] = value

        def body(step, carry):
            self.copy(step, self.me, lax.rem(self.me + step, self.count)).start()
            return carry

        lax.fori_loop(1, self.count, body, 0)

    def finish(self):
        def body(step, carry):
            peer = lax.rem(self.me + step, self.count)
            self.copy(step, peer, peer).wait_recv()
            return carry

        lax.fori_loop(1, self.count, body, 0)
        total = self.buf[0]
        for slot in range(1, self.count):
            total = total + self.buf[slot]
        return total

    def drain(self):
        def body(step, carry):
            self.copy(step, self.me, lax.rem(self.me + step, self.count)).wait_send()
            return carry

        lax.fori_loop(1, self.count, body, 0)


def gather_kernel(
    row_length,
    taps_hbm,
    gain_hbm,
    basis4,
    basis2,
    classes_hbm,
    ports_hbm,
    qs,
    ws,
    sums,
    taps_ref,
    gain_ref,
    pad,
    q2,
    w2,
    coefs,
    diag,
    bands,
    parts,
    classes,
    ports,
    relay,
    qq_y,
    qq_x,
    g_y,
    g_x,
    local_sem,
    block_sem,
    halo_send,
    halo_recv,
    relay_send,
    relay_recv,
    forward_send,
    qq_y_send,
    qq_y_recv,
    qq_x_send,
    qq_x_recv,
    g_y_send,
    g_y_recv,
    g_x_send,
    g_x_recv,
):
    size_x, size_y, size_z = classes.shape
    rows = size_x * size_y
    first = (BLOCKS - 1) * COLS
    gx, gy = lax.axis_index("gx"), lax.axis_index("gy")
    nx, ny = lax.axis_size("gx"), lax.axis_size("gy")
    chunks, _, span = qs.shape
    per_chunk = span // size_z

    barrier = pltpu.get_barrier_semaphore()
    for axis, me, count in (("gx", gx, nx), ("gy", gy, ny)):

        def greet(step, carry, axis=axis, me=me, count=count):
            pl.semaphore_signal(
                barrier, inc=1, device_id={axis: lax.rem(me + step, count)}, device_id_type=MESH
            )
            return carry

        lax.fori_loop(1, count, greet, 0)

    load_classes = pltpu.make_async_copy(classes_hbm, classes, local_sem.at[0])
    load_ports = pltpu.make_async_copy(ports_hbm, ports, local_sem.at[1])
    load_basis = pltpu.make_async_copy(basis2, q2, local_sem.at[2])
    load_block = pltpu.make_async_copy(
        basis4.at[pl.ds(first, COLS)],
        pad.at[:, pl.ds(REACH, size_x), pl.ds(size_y, size_y), :],
        block_sem,
    )
    load_taps = pltpu.make_async_copy(taps_hbm, taps_ref, local_sem.at[3])
    load_gain = pltpu.make_async_copy(gain_hbm, gain_ref, local_sem.at[4])
    load_taps.start()
    load_gain.start()
    load_classes.start()
    load_ports.start()
    load_block.start()
    load_basis.start()
    pl.semaphore_wait(barrier, nx + ny - 2)

    inner_x, inner_y = pl.ds(REACH, size_x), pl.ds(size_y, size_y)
    ways = (
        ("gy", 1, gy < ny - 1, gy > 0,
         (slice(None), pl.ds(size_y - REACH, REACH)), (inner_x, pl.ds(size_y - REACH, REACH))),
        ("gy", -1, gy > 0, gy < ny - 1,
         (slice(None), pl.ds(0, REACH)), (inner_x, pl.ds(2 * size_y, REACH))),
        ("gx", 1, gx < nx - 1, gx > 0,
         (pl.ds(size_x - REACH, REACH), slice(None)), (pl.ds(0, REACH), inner_y)),
        ("gx", -1, gx > 0, gx < nx - 1,
         (pl.ds(0, REACH), slice(None)), (pl.ds(REACH + size_x, REACH), inner_y)),
    )

    def halo(way, group):
        axis, step, _, _, (from_x, from_y), (to_x, to_y) = ways[way]
        return pltpu.make_async_remote_copy(
            src_ref=basis4.at[pl.ds(first + group * GROUP, GROUP), from_x, from_y, :],
            dst_ref=pad.at[pl.ds(group * GROUP, GROUP), to_x, to_y, :],
            send_sem=halo_send.at[way, group],
            recv_sem=halo_recv.at[way, group],
            device_id={axis: lax.axis_index(axis) + step},
            device_id_type=MESH,
        )

    turns = []
    if row_length:
        for last in range(row_length - 1, nx - 1, row_length):
            corners = (last + 1 - row_length, last + row_length)
            turns += [(0, last, last + 1, corners), (1, last + 1, last, corners)]
    turning = [jnp.bool_(False), jnp.bool_(False)]
    for direction, source, _, _ in turns:
        turning[direction] = jnp.logical_or(turning[direction], gx == source)

    def to_corner(direction, group, corner):
        from_x, from_y = ways[2 + direction][4]
        return pltpu.make_async_remote_copy(
            src_ref=basis4.at[pl.ds(first + group * GROUP, GROUP), from_x, from_y, :],
            dst_ref=relay.at[direction],
            send_sem=relay_send.at[direction, group],
            recv_sem=relay_recv.at[direction],
            device_id={"gx": corner},
            device_id_type=MESH,
        )

    def from_corner(direction, group, target):
        to_x, to_y = ways[2 + direction][5]
        return pltpu.make_async_remote_copy(
            src_ref=relay.at[direction],
            dst_ref=pad.at[pl.ds(group * GROUP, GROUP), to_x, to_y, :],
            send_sem=forward_send.at[direction],
            recv_sem=halo_recv.at[2 + direction, group],
            device_id={"gx": target},
            device_id_type=MESH,
        )

    def pass_on(early):
        for direction, _, target, corners in turns:
            group = direction if not early else 1 - direction

            @pl.when(gx == corners[group])
            def _(direction=direction, target=target, group=group):
                to_corner(direction, group, target).wait_recv()
                from_corner(direction, group, target).start()

    for direction, source, _, corners in turns:

        @pl.when(gx == source)
        def _(direction=direction, corners=corners):
            for group in range(2):
                to_corner(direction, group, corners[group]).start()

    sends = [ways[way][2] for way in range(4)]
    for direction in range(2):
        sends[2 + direction] = jnp.logical_and(
            sends[2 + direction], jnp.logical_not(turning[direction])
        )
    for group in range(COLS // GROUP):
        for way in (2, 3, 0, 1):

            @pl.when(sends[way])
            def _(way=way, group=group):
                halo(way, group).start()

    for way in range(4):

        @pl.when(jnp.logical_not(ways[way][3]))
        def _(way=way):
            to_x, to_y = ways[way][5]
            pad[:, to_x, to_y, :] = jnp.zeros((COLS, to_x.size, to_y.size, size_z), jnp.float32)

    load_taps.wait()
    load_gain.wait()
    load_classes.wait()
    load_ports.wait()
    layers = LAYERS if size_x % LAYERS == 0 else 1
    z_sums = []
    for m in range(MAT):
        z_sum = taps_ref[m, 4 * REACH]
        for t in range(4 * REACH + 1, 6 * REACH):
            z_sum = z_sum + taps_ref[m, t]
        z_sums.append(z_sum)

    def make_coefs(step, carry):
        place = pl.ds(step * layers, layers)
        kind, port = classes[place], ports[place]
        bits = [(kind & (1 << b)) != 0 for b in range(3)]
        total = jnp.ones(kind.shape, jnp.float32)
        for p in range(PORTS):
            total = jnp.where(port == p + 1, 1.0 + gain_ref[p], total)
        for t in range(4 * REACH + 1):
            level = [taps_ref[m, t] for m in range(MAT)] if t < 4 * REACH else z_sums
            for bit in bits:
                level = [
                    jnp.where(bit, level[2 * i + 1], level[2 * i]) for i in range(len(level) // 2)
                ]
            total = total + level[0]
            if t < 4 * REACH:
                coefs[t, place] = level[0]
        diag[place] = total
        return carry

    lax.fori_loop(0, size_x // layers, make_coefs, 0)
    load_block.wait()

    distance = lax.broadcasted_iota(jnp.int32, (size_z, size_z), 0) - lax.broadcasted_iota(
        jnp.int32, (size_z, size_z), 1
    )

    def make_bands(pair, carry):
        both = []
        for m in (2 * pair, 2 * pair + 1):
            band = jnp.zeros((size_z, size_z), jnp.float32)
            for j in range(2 * REACH):
                band = jnp.where(distance == offset_of(j), taps_ref[m, 4 * REACH + j], band)
            both.append(band)
        band = jnp.concatenate(both, axis=1)
        high = band.astype(jnp.bfloat16).astype(jnp.float32)
        bands[pair] = jnp.concatenate([high, high, band - high], axis=0).astype(jnp.bfloat16)
        return carry

    lax.fori_loop(0, MAT // 2, make_bands, 0)

    def split_block(c, carry):
        place = pl.ds(pl.multiple_of(c * rows, rows), rows)
        own = pad[c, inner_x, inner_y, :]
        w2[place, :] = (diag[...] * own).reshape(rows, size_z)
        own = own.reshape(rows, size_z)
        high = own.astype(jnp.bfloat16).astype(jnp.float32)
        parts[place, :] = jnp.concatenate([high, own - high, high], axis=1).astype(jnp.bfloat16)
        return carry

    lax.fori_loop(0, COLS, split_block, 0)

    def along_z(pair, carry):
        kind = classes[...].reshape(rows, size_z)
        even, odd = kind == 2 * pair, kind == 2 * pair + 1
        for group in range(COLS // GROUP):
            lines = pl.ds(group * GROUP * rows, GROUP * rows)
            result = jnp.dot(parts[lines, :], bands[pair], preferred_element_type=jnp.float32)
            for i in range(GROUP):
                place = pl.ds((group * GROUP + i) * rows, rows)
                mine = result[i * rows : (i + 1) * rows]
                w2[place, :] -= jnp.where(
                    even, mine[:, :size_z], jnp.where(odd, mine[:, size_z:], 0.0)
                )
        return carry

    lax.fori_loop(0, MAT // 2, along_z, 0)
    pass_on(True)
    load_basis.wait()

    def gather(ref, count, chunk):
        return jnp.concatenate(
            [
                ref[pl.ds(chunk * per_chunk + i, count, stride=rows), :]
                for i in range(per_chunk)
            ],
            axis=1,
        )

    def own_products(chunk, acc):
        both = halves(gather(q2, BLOCKS * COLS, chunk))
        qs[chunk] = both
        return acc + lax.dot_general(both, both, NT, preferred_element_type=jnp.float32)

    wide = BLOCKS * COLS
    acc = lax.fori_loop(
        0, chunks, own_products, jnp.zeros((2 * wide, 2 * wide), jnp.float32), unroll=UNROLL
    )
    pass_on(False)
    acc = acc[:wide] + acc[wide:]
    local_qq = acc[:, :wide] + acc[:, wide:]
    fill = jnp.zeros((wide, 128 - wide), jnp.float32)
    exchange = Exchange("gy", qq_y, qq_y_send, qq_y_recv)
    exchange.start(jnp.concatenate([local_qq, fill], axis=1))

    for axis, first_way in (("gy", 0), ("gx", 2)):
        for group in range(COLS // GROUP):
            for way in (first_way, first_way + 1):

                @pl.when(ways[way][3])
                def _(way=way, group=group):
                    halo(way, group).wait_recv()

            def along(x, carry, axis=axis, group=group):
                columns = range(group * GROUP, (group + 1) * GROUP)
                places = [
                    pl.ds(pl.multiple_of(c * rows + x * size_y, size_y), size_y) for c in columns
                ]
                images = [w2[place, :] for place in places]
                for j in range(2 * REACH):
                    k = offset_of(j)
                    if axis == "gx":
                        coef, at_x, at_y = coefs[j, x], x + REACH + k, inner_y
                    else:
                        coef, at_x = coefs[2 * REACH + j, x], x + REACH
                        at_y = pl.ds(size_y + k, size_y)
                    for i, c in enumerate(columns):
                        images[i] = images[i] - coef * pad[c, at_x, at_y, :]
                for place, image in zip(places, images):
                    w2[place, :] = image
                return carry

            lax.fori_loop(0, size_x, along, 0)

    exchange_x = Exchange("gx", qq_x, qq_x_send, qq_x_recv)
    exchange_x.start(exchange.finish())

    def image_products(chunk, acc):
        both = halves(gather(w2, COLS, chunk))
        ws[chunk] = both
        acc_q, acc_w = acc
        acc_q = acc_q + lax.dot_general(both, qs[chunk], NT, preferred_element_type=jnp.float32)
        acc_w = acc_w + lax.dot_general(both, both, NT, preferred_element_type=jnp.float32)
        return acc_q, acc_w

    acc_q, acc_w = lax.fori_loop(
        0,
        chunks,
        image_products,
        (
            jnp.zeros((2 * COLS, 2 * wide), jnp.float32),
            jnp.zeros((2 * COLS, 2 * COLS), jnp.float32),
        ),
        unroll=UNROLL,
    )
    acc_q, acc_w = acc_q[:COLS] + acc_q[COLS:], acc_w[:COLS] + acc_w[COLS:]
    local_g = jnp.concatenate(
        [
            acc_q[:, :wide] + acc_q[:, wide:],
            acc_w[:, :COLS] + acc_w[:, COLS:],
            jnp.zeros((COLS, 128 - wide - COLS), jnp.float32),
        ],
        axis=1,
    )
    g_exchange = Exchange("gy", g_y, g_y_send, g_y_recv)
    g_exchange.start(local_g)
    sums[COLS:, :] = exchange_x.finish()
    g_exchange_x = Exchange("gx", g_x, g_x_send, g_x_recv)
    g_exchange_x.start(g_exchange.finish())
    sums[:COLS, :] = g_exchange_x.finish()
    for group in range(COLS // GROUP):
        for way in range(4):

            @pl.when(sends[way])
            def _(way=way, group=group):
                halo(way, group).wait_send()

    for direction, source, target, corners in turns:
        for group in range(2):

            @pl.when(gx == source)
            def _(direction=direction, group=group, corner=corners[group]):
                to_corner(direction, group, corner).wait_send()

            @pl.when(gx == corners[group])
            def _(direction=direction, group=group, target=target):
                from_corner(direction, group, target).wait_send()

    for each in (exchange, exchange_x, g_exchange, g_exchange_x):
        each.drain()


def combine_kernel(
    total_cells,
    qs,
    ws,
    both_sums,
    out_hbm,
    proj_hbm,
    tri_hbm,
    out2,
    proj_ref,
    tri_ref,
    small_sem,
    out_sem,
):
    chunks, _, span = qs.shape
    rows, size_z = out2.shape[0] // COLS, out2.shape[1]
    per_chunk = span // size_z
    wide = BLOCKS * COLS
    sums = both_sums[:COLS, :] / total_cells
    sum_qq = both_sums[COLS:, :]
    proj_t = sums[:, :wide]
    proj_ref[...] = proj_t
    row = lax.broadcasted_iota(jnp.int32, (wide, wide), 0)
    column = lax.broadcasted_iota(jnp.int32, (wide, wide), 1)
    middle = jnp.where(row == column, 2.0, 0.0) - sum_qq[:, :wide] / total_cells
    left = jnp.dot(proj_t, middle, precision=HIGHEST, preferred_element_type=jnp.float32)
    gram = sums[:, wide : wide + COLS] - lax.dot_general(
        left, proj_t, NT, precision=HIGHEST, preferred_element_type=jnp.float32
    )
    row = lax.broadcasted_iota(jnp.int32, (COLS, COLS), 0)
    column = lax.broadcasted_iota(jnp.int32, (COLS, COLS), 1)
    eye = jnp.where(row == column, 1.0, 0.0)
    table = jnp.concatenate([-proj_t, eye, gram], axis=1)
    base = wide + COLS
    index = lax.broadcasted_iota(jnp.int32, table.shape, 0)
    for j in range(COLS - 1):
        factor = jnp.broadcast_to(table[:, base + j : base + j + 1], table.shape)
        factor = jnp.where(index > j, factor / factor[j : j + 1, :], 0.0)
        table = table - factor * table[j : j + 1, :]
    pivots = jnp.sum(jnp.where(row == column, table[:, base:], 0.0), axis=1, keepdims=True)
    table = table * lax.rsqrt(pivots)
    tri_ref[...] = jnp.where(row <= column, table[:, base:], 0.0)
    store_proj = pltpu.make_async_copy(proj_ref, proj_hbm, small_sem.at[0])
    store_tri = pltpu.make_async_copy(tri_ref, tri_hbm, small_sem.at[1])
    store_proj.start()
    store_tri.start()

    mix = table[:, :base]
    high = mix.astype(jnp.bfloat16).astype(jnp.float32)
    mix = jnp.concatenate([high, mix - high], axis=0)
    mix = jnp.concatenate([mix[:, :wide], mix[:, :wide]], axis=1), jnp.concatenate(
        [mix[:, wide:], mix[:, wide:]], axis=1
    )
    mix_q, mix_w = mix[0].astype(jnp.bfloat16), mix[1].astype(jnp.bfloat16)

    def store(chunk):
        part = pl.ds(pl.multiple_of(chunk * per_chunk, per_chunk), per_chunk)
        return pltpu.make_async_copy(
            out2.reshape(COLS, rows, size_z).at[:, part, :], out_hbm.at[:, part, :], out_sem.at[chunk]
        )

    def combine(chunk, carry):
        result = jnp.dot(mix_q, qs[chunk], preferred_element_type=jnp.float32)
        result = result + jnp.dot(mix_w, ws[chunk], preferred_element_type=jnp.float32)
        result = result[:COLS] + result[COLS:]
        for i in range(per_chunk):
            out2[pl.ds(chunk * per_chunk + i, COLS, stride=rows), :] = result[
                :, i * size_z : (i + 1) * size_z
            ]
        store(chunk).start()
        return carry

    lax.fori_loop(0, chunks, combine, 0, unroll=UNROLL)

    def drain(chunk, carry):
        store(chunk).wait()
        return carry

    lax.fori_loop(0, chunks, drain, 0)
    store_proj.wait()
    store_tri.wait()


def per_device(row_length, basis, classes, ports, taps, port_gain):
    size_x, size_y, size_z = classes.shape
    rows = size_x * size_y
    wide = BLOCKS * COLS
    nx, ny = lax.axis_size("gx"), lax.axis_size("gy")
    per_chunk = 16 if rows % 16 == 0 else 1
    chunks, span = rows // per_chunk, per_chunk * size_z
    vmem = functools.partial(pltpu.VMEM, dtype=jnp.float32)
    dma = pltpu.SemaphoreType.DMA
    hbm = pl.BlockSpec(memory_space=pltpu.HBM)
    vmem_spec = pl.BlockSpec(memory_space=pltpu.VMEM)
    groups = COLS // GROUP
    qs_shape, ws_shape = (chunks, 2 * wide, span), (chunks, 2 * COLS, span)
    sums_shape = (COLS + wide, 128)
    qs, ws, sums = pl.pallas_call(
        functools.partial(gather_kernel, row_length),
        out_shape=(
            jax.ShapeDtypeStruct(qs_shape, jnp.bfloat16),
            jax.ShapeDtypeStruct(ws_shape, jnp.bfloat16),
            jax.ShapeDtypeStruct(sums_shape, jnp.float32),
        ),
        in_specs=[hbm] * 6,
        out_specs=(vmem_spec,) * 3,
        scratch_shapes=[
            pltpu.SMEM(taps.shape, jnp.float32),
            pltpu.SMEM(port_gain.shape, jnp.float32),
            vmem((COLS, size_x + 2 * REACH, 3 * size_y, size_z)),
            vmem((wide * rows, size_z)),
            vmem((COLS * rows, size_z)),
            vmem((4 * REACH, size_x, size_y, size_z)),
            vmem((size_x, size_y, size_z)),
            pltpu.VMEM((MAT // 2, 3 * size_z, 2 * size_z), jnp.bfloat16),
            pltpu.VMEM((COLS * rows, 3 * size_z), jnp.bfloat16),
            pltpu.VMEM((size_x, size_y, size_z), jnp.int32),
            pltpu.VMEM((size_x, size_y, size_z), jnp.int32),
            vmem((2, GROUP, REACH, size_y, size_z)),
            vmem((ny, wide, 128)),
            vmem((nx, wide, 128)),
            vmem((ny, COLS, 128)),
            vmem((nx, COLS, 128)),
            dma((5,)),
            dma,
            dma((4, groups)),
            dma((4, groups)),
            dma((2, groups)),
            dma((2,)),
            dma((2,)),
            dma((ny,)),
            dma((ny,)),
            dma((nx,)),
            dma((nx,)),
            dma((ny,)),
            dma((ny,)),
            dma((nx,)),
            dma((nx,)),
        ],
        compiler_params=pltpu.CompilerParams(
            collective_id=0, has_side_effects=True, vmem_limit_bytes=40 * 1024 * 1024
        ),
    )(
        *(
            pltpu.with_memory_space_constraint(operand, pltpu.HBM)
            for operand in (
                taps, port_gain, basis, basis.reshape(wide * rows, size_z), classes, ports
            )
        )
    )
    out, projection, triangle = pl.pallas_call(
        functools.partial(combine_kernel, float(rows * size_z * nx * ny)),
        out_shape=(
            jax.ShapeDtypeStruct((COLS, rows, size_z), jnp.float32),
            jax.ShapeDtypeStruct((COLS, wide), jnp.float32),
            jax.ShapeDtypeStruct((COLS, COLS), jnp.float32),
        ),
        in_specs=[vmem_spec] * 3,
        out_specs=(hbm,) * 3,
        scratch_shapes=[
            vmem((COLS * rows, size_z)),
            vmem((COLS, wide)),
            vmem((COLS, COLS)),
            dma((2,)),
            dma((chunks,)),
        ],
        compiler_params=pltpu.CompilerParams(vmem_limit_bytes=24 * 1024 * 1024),
    )(qs, ws, sums)
    return out.reshape(COLS, size_x, size_y, size_z), projection.T, triangle


def length_of_row(mesh):
    places = [getattr(device, "coords", None) for device in mesh.devices[:, 0]]
    if None in places:
        return 0
    for i in range(1, len(places)):
        if sum(a != b for a, b in zip(places[i - 1], places[i])) > 1:
            return i if len(places) % i == 0 else 0
    return 0


def solution(mesh):
    in_specs = (P(None, "gx", "gy", None), P("gx", "gy", None), P("gx", "gy", None), P(), P())
    out_specs = (P(None, "gx", "gy", None), P(), P())
    return jax.shard_map(
        functools.partial(per_device, length_of_row(mesh)), mesh=mesh, in_specs=in_specs, out_specs=out_specs, check_vma=False
    )
```

```python
import functools

import jax
import jax.numpy as jnp
from jax import lax
from jax.experimental import pallas as pl
from jax.experimental.pallas import tpu as pltpu
from jax.sharding import PartitionSpec as P

COLS = 8
BLOCKS = 4
REACH = 7
MAT = 8
PORTS = 8
GROUP = 4
LAYERS = 4
UNROLL = 4
MESH = pl.DeviceIdType.MESH
NT = (((1,), (1,)), ((), ()))
HIGHEST = lax.Precision.HIGHEST


def offset_of(j):
    return j - REACH if j < REACH else j - REACH + 1


def halves(value):
    high = value.astype(jnp.bfloat16).astype(jnp.float32)
    return jnp.concatenate([high, value - high], axis=0).astype(jnp.bfloat16)


class Exchange:
    def __init__(self, axis, buf, send, recv):
        self.axis, self.buf, self.send, self.recv = axis, buf, send, recv
        self.me, self.count = lax.axis_index(axis), lax.axis_size(axis)

    def copy(self, step, slot, peer):
        return pltpu.make_async_remote_copy(
            src_ref=self.buf.at[slot],
            dst_ref=self.buf.at[slot],
            send_sem=self.send.at[step],
            recv_sem=self.recv.at[slot],
            device_id={self.axis: peer},
            device_id_type=MESH,
        )

    def start(self, value):
        self.buf[self.me] = value

        def body(step, carry):
            self.copy(step, self.me, lax.rem(self.me + step, self.count)).start()
            return carry

        lax.fori_loop(1, self.count, body, 0)

    def finish(self):
        def body(step, carry):
            peer = lax.rem(self.me + step, self.count)
            self.copy(step, peer, peer).wait_recv()
            return carry

        lax.fori_loop(1, self.count, body, 0)
        total = self.buf[0]
        for slot in range(1, self.count):
            total = total + self.buf[slot]
        return total

    def drain(self):
        def body(step, carry):
            self.copy(step, self.me, lax.rem(self.me + step, self.count)).wait_send()
            return carry

        lax.fori_loop(1, self.count, body, 0)


def gather_kernel(
    row_length,
    taps_hbm,
    gain_hbm,
    basis4,
    basis2,
    classes_hbm,
    ports_hbm,
    halved,
    sums,
    taps_ref,
    gain_ref,
    pad,
    q2,
    w2,
    coefs,
    diag,
    bands,
    parts,
    classes,
    ports,
    relay,
    qq_y,
    qq_x,
    g_y,
    g_x,
    local_sem,
    block_sem,
    halo_send,
    halo_recv,
    relay_send,
    relay_recv,
    forward_send,
    qq_y_send,
    qq_y_recv,
    qq_x_send,
    qq_x_recv,
    g_y_send,
    g_y_recv,
    g_x_send,
    g_x_recv,
):
    size_x, size_y, size_z = classes.shape
    rows = size_x * size_y
    first = (BLOCKS - 1) * COLS
    gx, gy = lax.axis_index("gx"), lax.axis_index("gy")
    nx, ny = lax.axis_size("gx"), lax.axis_size("gy")
    chunks, _, span = halved.shape
    per_chunk = span // size_z

    barrier = pltpu.get_barrier_semaphore()
    for axis, me, count in (("gx", gx, nx), ("gy", gy, ny)):

        def greet(step, carry, axis=axis, me=me, count=count):
            pl.semaphore_signal(
                barrier, inc=1, device_id={axis: lax.rem(me + step, count)}, device_id_type=MESH
            )
            return carry

        lax.fori_loop(1, count, greet, 0)

    load_classes = pltpu.make_async_copy(classes_hbm, classes, local_sem.at[0])
    load_ports = pltpu.make_async_copy(ports_hbm, ports, local_sem.at[1])
    load_basis = pltpu.make_async_copy(basis2, q2, local_sem.at[2])
    load_block = pltpu.make_async_copy(
        basis4.at[pl.ds(first, COLS)],
        pad.at[:, pl.ds(REACH, size_x), pl.ds(size_y, size_y), :],
        block_sem,
    )
    load_taps = pltpu.make_async_copy(taps_hbm, taps_ref, local_sem.at[3])
    load_gain = pltpu.make_async_copy(gain_hbm, gain_ref, local_sem.at[4])
    load_taps.start()
    load_gain.start()
    load_classes.start()
    load_ports.start()
    load_block.start()
    load_basis.start()
    pl.semaphore_wait(barrier, nx + ny - 2)

    inner_x, inner_y = pl.ds(REACH, size_x), pl.ds(size_y, size_y)
    ways = (
        ("gy", 1, gy < ny - 1, gy > 0,
         (slice(None), pl.ds(size_y - REACH, REACH)), (inner_x, pl.ds(size_y - REACH, REACH))),
        ("gy", -1, gy > 0, gy < ny - 1,
         (slice(None), pl.ds(0, REACH)), (inner_x, pl.ds(2 * size_y, REACH))),
        ("gx", 1, gx < nx - 1, gx > 0,
         (pl.ds(size_x - REACH, REACH), slice(None)), (pl.ds(0, REACH), inner_y)),
        ("gx", -1, gx > 0, gx < nx - 1,
         (pl.ds(0, REACH), slice(None)), (pl.ds(REACH + size_x, REACH), inner_y)),
    )

    def halo(way, group):
        axis, step, _, _, (from_x, from_y), (to_x, to_y) = ways[way]
        return pltpu.make_async_remote_copy(
            src_ref=basis4.at[pl.ds(first + group * GROUP, GROUP), from_x, from_y, :],
            dst_ref=pad.at[pl.ds(group * GROUP, GROUP), to_x, to_y, :],
            send_sem=halo_send.at[way, group],
            recv_sem=halo_recv.at[way, group],
            device_id={axis: lax.axis_index(axis) + step},
            device_id_type=MESH,
        )

    relayed = COLS // GROUP - 1
    turns = []
    if row_length:
        for last in range(row_length - 1, nx - 1, row_length):
            turns += [(0, last, last + 1, last + row_length), (1, last + 1, last, last + 1 - row_length)]
    turning = [jnp.bool_(False), jnp.bool_(False)]
    for direction, source, _, _ in turns:
        turning[direction] = jnp.logical_or(turning[direction], gx == source)

    def to_corner(direction, corner):
        from_x, from_y = ways[2 + direction][4]
        return pltpu.make_async_remote_copy(
            src_ref=basis4.at[pl.ds(first + relayed * GROUP, GROUP), from_x, from_y, :],
            dst_ref=relay.at[direction],
            send_sem=relay_send.at[direction],
            recv_sem=relay_recv.at[direction],
            device_id={"gx": corner},
            device_id_type=MESH,
        )

    def from_corner(direction, target):
        to_x, to_y = ways[2 + direction][5]
        return pltpu.make_async_remote_copy(
            src_ref=relay.at[direction],
            dst_ref=pad.at[pl.ds(relayed * GROUP, GROUP), to_x, to_y, :],
            send_sem=forward_send.at[direction],
            recv_sem=halo_recv.at[2 + direction, relayed],
            device_id={"gx": target},
            device_id_type=MESH,
        )

    for direction, source, _, corner in turns:

        @pl.when(gx == source)
        def _(direction=direction, corner=corner):
            to_corner(direction, corner).start()

    def sends(way, group):
        if way < 2 or group != relayed:
            return ways[way][2]
        return jnp.logical_and(ways[way][2], jnp.logical_not(turning[way - 2]))

    for group in range(COLS // GROUP):
        for way in (2, 3, 0, 1):

            @pl.when(sends(way, group))
            def _(way=way, group=group):
                halo(way, group).start()

    for way in range(4):

        @pl.when(jnp.logical_not(ways[way][3]))
        def _(way=way):
            to_x, to_y = ways[way][5]
            pad[:, to_x, to_y, :] = jnp.zeros((COLS, to_x.size, to_y.size, size_z), jnp.float32)

    load_taps.wait()
    load_gain.wait()
    load_classes.wait()
    load_ports.wait()
    layers = LAYERS if size_x % LAYERS == 0 else 1
    z_sums = []
    for m in range(MAT):
        z_sum = taps_ref[m, 4 * REACH]
        for t in range(4 * REACH + 1, 6 * REACH):
            z_sum = z_sum + taps_ref[m, t]
        z_sums.append(z_sum)

    def make_coefs(step, carry):
        place = pl.ds(step * layers, layers)
        kind, port = classes[place], ports[place]
        bits = [(kind & (1 << b)) != 0 for b in range(3)]
        total = jnp.ones(kind.shape, jnp.float32)
        for p in range(PORTS):
            total = jnp.where(port == p + 1, 1.0 + gain_ref[p], total)
        for t in range(4 * REACH + 1):
            level = [taps_ref[m, t] for m in range(MAT)] if t < 4 * REACH else z_sums
            for bit in bits:
                level = [
                    jnp.where(bit, level[2 * i + 1], level[2 * i]) for i in range(len(level) // 2)
                ]
            total = total + level[0]
            if t < 4 * REACH:
                coefs[t, place] = level[0]
        diag[place] = total
        return carry

    lax.fori_loop(0, size_x // layers, make_coefs, 0)
    load_block.wait()

    distance = lax.broadcasted_iota(jnp.int32, (size_z, size_z), 0) - lax.broadcasted_iota(
        jnp.int32, (size_z, size_z), 1
    )

    def make_bands(pair, carry):
        both = []
        for m in (2 * pair, 2 * pair + 1):
            band = jnp.zeros((size_z, size_z), jnp.float32)
            for j in range(2 * REACH):
                band = jnp.where(distance == offset_of(j), taps_ref[m, 4 * REACH + j], band)
            both.append(band)
        band = jnp.concatenate(both, axis=1)
        high = band.astype(jnp.bfloat16).astype(jnp.float32)
        bands[pair] = jnp.concatenate([high, high, band - high], axis=0).astype(jnp.bfloat16)
        return carry

    lax.fori_loop(0, MAT // 2, make_bands, 0)

    def split_block(c, carry):
        place = pl.ds(pl.multiple_of(c * rows, rows), rows)
        own = pad[c, inner_x, inner_y, :]
        w2[place, :] = (diag[...] * own).reshape(rows, size_z)
        own = own.reshape(rows, size_z)
        high = own.astype(jnp.bfloat16).astype(jnp.float32)
        parts[place, :] = jnp.concatenate([high, own - high, high], axis=1).astype(jnp.bfloat16)
        return carry

    lax.fori_loop(0, COLS, split_block, 0)

    def along_z(pair, carry):
        kind = classes[...].reshape(rows, size_z)
        even, odd = kind == 2 * pair, kind == 2 * pair + 1
        for group in range(COLS // GROUP):
            lines = pl.ds(group * GROUP * rows, GROUP * rows)
            result = jnp.dot(parts[lines, :], bands[pair], preferred_element_type=jnp.float32)
            for i in range(GROUP):
                place = pl.ds((group * GROUP + i) * rows, rows)
                mine = result[i * rows : (i + 1) * rows]
                w2[place, :] -= jnp.where(
                    even, mine[:, :size_z], jnp.where(odd, mine[:, size_z:], 0.0)
                )
        return carry

    lax.fori_loop(0, MAT // 2, along_z, 0)
    for direction, _, target, corner in turns:

        @pl.when(gx == corner)
        def _(direction=direction, target=target):
            to_corner(direction, target).wait_recv()
            from_corner(direction, target).start()

    load_basis.wait()

    def gather(ref, count, chunk):
        return jnp.concatenate(
            [
                ref[pl.ds(chunk * per_chunk + i, count, stride=rows), :]
                for i in range(per_chunk)
            ],
            axis=1,
        )

    def own_products(chunk, acc):
        both = halves(gather(q2, BLOCKS * COLS, chunk))
        halved[chunk, : 2 * wide, :] = both
        return acc + lax.dot_general(both, both, NT, preferred_element_type=jnp.float32)

    wide = BLOCKS * COLS
    acc = lax.fori_loop(
        0, chunks, own_products, jnp.zeros((2 * wide, 2 * wide), jnp.float32), unroll=UNROLL
    )
    acc = acc[:wide] + acc[wide:]
    local_qq = acc[:, :wide] + acc[:, wide:]
    fill = jnp.zeros((wide, 128 - wide), jnp.float32)
    exchange = Exchange("gy", qq_y, qq_y_send, qq_y_recv)
    exchange.start(jnp.concatenate([local_qq, fill], axis=1))

    for axis, first_way in (("gy", 0), ("gx", 2)):
        for group in range(COLS // GROUP):
            for way in (first_way, first_way + 1):

                @pl.when(ways[way][3])
                def _(way=way, group=group):
                    halo(way, group).wait_recv()

            def along(x, carry, axis=axis, group=group):
                columns = range(group * GROUP, (group + 1) * GROUP)
                places = [
                    pl.ds(pl.multiple_of(c * rows + x * size_y, size_y), size_y) for c in columns
                ]
                images = [w2[place, :] for place in places]
                for j in range(2 * REACH):
                    k = offset_of(j)
                    if axis == "gx":
                        coef, at_x, at_y = coefs[j, x], x + REACH + k, inner_y
                    else:
                        coef, at_x = coefs[2 * REACH + j, x], x + REACH
                        at_y = pl.ds(size_y + k, size_y)
                    for i, c in enumerate(columns):
                        images[i] = images[i] - coef * pad[c, at_x, at_y, :]
                for place, image in zip(places, images):
                    w2[place, :] = image
                return carry

            lax.fori_loop(0, size_x, along, 0)

    exchange_x = Exchange("gx", qq_x, qq_x_send, qq_x_recv)
    exchange_x.start(exchange.finish())

    def image_products(chunk, acc):
        both = halves(gather(w2, COLS, chunk))
        halved[chunk, 2 * wide :, :] = both
        return acc + lax.dot_general(halved[chunk], both, NT, preferred_element_type=jnp.float32)

    acc = lax.fori_loop(
        0,
        chunks,
        image_products,
        jnp.zeros((2 * (wide + COLS), 2 * COLS), jnp.float32),
        unroll=UNROLL,
    )
    acc = acc[:, :COLS] + acc[:, COLS:]
    local_g = jnp.concatenate(
        [
            acc[:wide] + acc[wide : 2 * wide],
            acc[2 * wide : 2 * wide + COLS] + acc[2 * wide + COLS :],
            jnp.zeros((128 - wide - COLS, COLS), jnp.float32),
        ],
        axis=0,
    ).T
    g_exchange = Exchange("gy", g_y, g_y_send, g_y_recv)
    g_exchange.start(local_g)
    sums[COLS:, :] = exchange_x.finish()
    g_exchange_x = Exchange("gx", g_x, g_x_send, g_x_recv)
    g_exchange_x.start(g_exchange.finish())
    sums[:COLS, :] = g_exchange_x.finish()
    for group in range(COLS // GROUP):
        for way in range(4):

            @pl.when(sends(way, group))
            def _(way=way, group=group):
                halo(way, group).wait_send()

    for direction, source, target, corner in turns:

        @pl.when(gx == source)
        def _(direction=direction, corner=corner):
            to_corner(direction, corner).wait_send()

        @pl.when(gx == corner)
        def _(direction=direction, target=target):
            from_corner(direction, target).wait_send()

    for each in (exchange, exchange_x, g_exchange, g_exchange_x):
        each.drain()


def combine_kernel(
    total_cells,
    halved,
    both_sums,
    out_hbm,
    proj_hbm,
    tri_hbm,
    out2,
    proj_ref,
    tri_ref,
    small_sem,
    out_sem,
):
    chunks, _, span = halved.shape
    rows, size_z = out2.shape[0] // COLS, out2.shape[1]
    per_chunk = span // size_z
    wide = BLOCKS * COLS
    sums = both_sums[:COLS, :] / total_cells
    sum_qq = both_sums[COLS:, :]
    proj_t = sums[:, :wide]
    proj_ref[...] = proj_t
    row = lax.broadcasted_iota(jnp.int32, (wide, wide), 0)
    column = lax.broadcasted_iota(jnp.int32, (wide, wide), 1)
    middle = jnp.where(row == column, 2.0, 0.0) - sum_qq[:, :wide] / total_cells
    left = jnp.dot(proj_t, middle, precision=HIGHEST, preferred_element_type=jnp.float32)
    gram = sums[:, wide : wide + COLS] - lax.dot_general(
        left, proj_t, NT, precision=HIGHEST, preferred_element_type=jnp.float32
    )
    row = lax.broadcasted_iota(jnp.int32, (COLS, COLS), 0)
    column = lax.broadcasted_iota(jnp.int32, (COLS, COLS), 1)
    eye = jnp.where(row == column, 1.0, 0.0)
    table = jnp.concatenate([-proj_t, eye, gram], axis=1)
    base = wide + COLS
    index = lax.broadcasted_iota(jnp.int32, table.shape, 0)
    for j in range(COLS - 1):
        factor = jnp.broadcast_to(table[:, base + j : base + j + 1], table.shape)
        factor = jnp.where(index > j, factor / factor[j : j + 1, :], 0.0)
        table = table - factor * table[j : j + 1, :]
    pivots = jnp.sum(jnp.where(row == column, table[:, base:], 0.0), axis=1, keepdims=True)
    table = table * lax.rsqrt(pivots)
    tri_ref[...] = jnp.where(row <= column, table[:, base:], 0.0)
    store_proj = pltpu.make_async_copy(proj_ref, proj_hbm, small_sem.at[0])
    store_tri = pltpu.make_async_copy(tri_ref, tri_hbm, small_sem.at[1])
    store_proj.start()
    store_tri.start()

    mix = table[:, :base]
    high = mix.astype(jnp.bfloat16).astype(jnp.float32)
    mix = jnp.concatenate([high, mix - high], axis=0)
    mix_q, mix_w = mix[:, :wide], mix[:, wide:]
    mix = jnp.concatenate([mix_q, mix_q, mix_w, mix_w], axis=1).astype(jnp.bfloat16)

    def store(chunk):
        part = pl.ds(pl.multiple_of(chunk * per_chunk, per_chunk), per_chunk)
        return pltpu.make_async_copy(
            out2.reshape(COLS, rows, size_z).at[:, part, :], out_hbm.at[:, part, :], out_sem.at[chunk]
        )

    def combine(chunk, carry):
        result = jnp.dot(mix, halved[chunk], preferred_element_type=jnp.float32)
        result = result[:COLS] + result[COLS:]
        for i in range(per_chunk):
            out2[pl.ds(chunk * per_chunk + i, COLS, stride=rows), :] = result[
                :, i * size_z : (i + 1) * size_z
            ]
        store(chunk).start()
        return carry

    lax.fori_loop(0, chunks, combine, 0, unroll=UNROLL)

    def drain(chunk, carry):
        store(chunk).wait()
        return carry

    lax.fori_loop(0, chunks, drain, 0)
    store_proj.wait()
    store_tri.wait()


def per_device(row_length, basis, classes, ports, taps, port_gain):
    size_x, size_y, size_z = classes.shape
    rows = size_x * size_y
    wide = BLOCKS * COLS
    nx, ny = lax.axis_size("gx"), lax.axis_size("gy")
    per_chunk = 16 if rows % 16 == 0 else 1
    chunks, span = rows // per_chunk, per_chunk * size_z
    vmem = functools.partial(pltpu.VMEM, dtype=jnp.float32)
    dma = pltpu.SemaphoreType.DMA
    hbm = pl.BlockSpec(memory_space=pltpu.HBM)
    vmem_spec = pl.BlockSpec(memory_space=pltpu.VMEM)
    groups = COLS // GROUP
    halved_shape = (chunks, 2 * (wide + COLS), span)
    sums_shape = (COLS + wide, 128)
    halved, sums = pl.pallas_call(
        functools.partial(gather_kernel, row_length),
        out_shape=(
            jax.ShapeDtypeStruct(halved_shape, jnp.bfloat16),
            jax.ShapeDtypeStruct(sums_shape, jnp.float32),
        ),
        in_specs=[hbm] * 6,
        out_specs=(vmem_spec,) * 2,
        scratch_shapes=[
            pltpu.SMEM(taps.shape, jnp.float32),
            pltpu.SMEM(port_gain.shape, jnp.float32),
            vmem((COLS, size_x + 2 * REACH, 3 * size_y, size_z)),
            vmem((wide * rows, size_z)),
            vmem((COLS * rows, size_z)),
            vmem((4 * REACH, size_x, size_y, size_z)),
            vmem((size_x, size_y, size_z)),
            pltpu.VMEM((MAT // 2, 3 * size_z, 2 * size_z), jnp.bfloat16),
            pltpu.VMEM((COLS * rows, 3 * size_z), jnp.bfloat16),
            pltpu.VMEM((size_x, size_y, size_z), jnp.int32),
            pltpu.VMEM((size_x, size_y, size_z), jnp.int32),
            vmem((2, GROUP, REACH, size_y, size_z)),
            vmem((ny, wide, 128)),
            vmem((nx, wide, 128)),
            vmem((ny, COLS, 128)),
            vmem((nx, COLS, 128)),
            dma((5,)),
            dma,
            dma((4, groups)),
            dma((4, groups)),
            dma((2,)),
            dma((2,)),
            dma((2,)),
            dma((ny,)),
            dma((ny,)),
            dma((nx,)),
            dma((nx,)),
            dma((ny,)),
            dma((ny,)),
            dma((nx,)),
            dma((nx,)),
        ],
        compiler_params=pltpu.CompilerParams(
            collective_id=0, has_side_effects=True, vmem_limit_bytes=40 * 1024 * 1024
        ),
    )(
        *(
            pltpu.with_memory_space_constraint(operand, pltpu.HBM)
            for operand in (
                taps, port_gain, basis, basis.reshape(wide * rows, size_z), classes, ports
            )
        )
    )
    out, projection, triangle = pl.pallas_call(
        functools.partial(combine_kernel, float(rows * size_z * nx * ny)),
        out_shape=(
            jax.ShapeDtypeStruct((COLS, rows, size_z), jnp.float32),
            jax.ShapeDtypeStruct((COLS, wide), jnp.float32),
            jax.ShapeDtypeStruct((COLS, COLS), jnp.float32),
        ),
        in_specs=[vmem_spec] * 2,
        out_specs=(hbm,) * 3,
        scratch_shapes=[
            vmem((COLS * rows, size_z)),
            vmem((COLS, wide)),
            vmem((COLS, COLS)),
            dma((2,)),
            dma((chunks,)),
        ],
        compiler_params=pltpu.CompilerParams(vmem_limit_bytes=24 * 1024 * 1024),
    )(halved, sums)
    return out.reshape(COLS, size_x, size_y, size_z), projection.T, triangle


def length_of_row(mesh):
    places = [getattr(device, "coords", None) for device in mesh.devices[:, 0]]
    if None in places:
        return 0
    for i in range(1, len(places)):
        if sum(a != b for a, b in zip(places[i - 1], places[i])) > 1:
            return i if len(places) % i == 0 else 0
    return 0


def solution(mesh):
    in_specs = (P(None, "gx", "gy", None), P("gx", "gy", None), P("gx", "gy", None), P(), P())
    out_specs = (P(None, "gx", "gy", None), P(), P())
    return jax.shard_map(
        functools.partial(per_device, length_of_row(mesh)), mesh=mesh, in_specs=in_specs, out_specs=out_specs, check_vma=False
    )
```

```python
import functools

import jax
import jax.numpy as jnp
from jax import lax
from jax.experimental import pallas as pl
from jax.experimental.pallas import tpu as pltpu
from jax.sharding import PartitionSpec as P

COLS = 8
BLOCKS = 4
REACH = 7
MAT = 8
PORTS = 8
GROUP = 4
LAYERS = 4
UNROLL = 4
PITCH = 8
MESH = pl.DeviceIdType.MESH
NT = (((1,), (1,)), ((), ()))
HIGHEST = lax.Precision.HIGHEST


def offset_of(j):
    return j - REACH if j < REACH else j - REACH + 1


def halves(value):
    high = value.astype(jnp.bfloat16).astype(jnp.float32)
    return jnp.concatenate([high, value - high], axis=0).astype(jnp.bfloat16)


class Exchange:
    def __init__(self, axis, buf, send, recv):
        self.axis, self.buf, self.send, self.recv = axis, buf, send, recv
        self.me, self.count = lax.axis_index(axis), lax.axis_size(axis)

    def copy(self, step, slot, peer):
        return pltpu.make_async_remote_copy(
            src_ref=self.buf.at[slot],
            dst_ref=self.buf.at[slot],
            send_sem=self.send.at[step],
            recv_sem=self.recv.at[slot],
            device_id={self.axis: peer},
            device_id_type=MESH,
        )

    def start(self, value):
        self.buf[self.me] = value

        def body(step, carry):
            self.copy(step, self.me, lax.rem(self.me + step, self.count)).start()
            return carry

        lax.fori_loop(1, self.count, body, 0)

    def finish(self):
        def body(step, carry):
            peer = lax.rem(self.me + step, self.count)
            self.copy(step, peer, peer).wait_recv()
            return carry

        lax.fori_loop(1, self.count, body, 0)
        total = self.buf[0]
        for slot in range(1, self.count):
            total = total + self.buf[slot]
        return total

    def drain(self):
        def body(step, carry):
            self.copy(step, self.me, lax.rem(self.me + step, self.count)).wait_send()
            return carry

        lax.fori_loop(1, self.count, body, 0)


def gather_kernel(
    row_length,
    taps_hbm,
    gain_hbm,
    basis4,
    basis2,
    classes_hbm,
    ports_hbm,
    halved,
    sums,
    taps_ref,
    gain_ref,
    pad,
    q2,
    w2,
    coefs,
    diag,
    bands,
    parts,
    classes,
    ports,
    relay,
    qq_y,
    qq_x,
    g_y,
    g_x,
    local_sem,
    block_sem,
    halo_send,
    halo_recv,
    relay_send,
    relay_recv,
    forward_send,
    qq_y_send,
    qq_y_recv,
    qq_x_send,
    qq_x_recv,
    g_y_send,
    g_y_recv,
    g_x_send,
    g_x_recv,
):
    size_x, size_y, size_z = classes.shape
    rows = size_x * size_y
    pitch = rows + PITCH
    first = (BLOCKS - 1) * COLS
    gx, gy = lax.axis_index("gx"), lax.axis_index("gy")
    nx, ny = lax.axis_size("gx"), lax.axis_size("gy")
    chunks, _, span = halved.shape
    per_chunk = span // size_z

    barrier = pltpu.get_barrier_semaphore()
    for axis, me, count in (("gx", gx, nx), ("gy", gy, ny)):

        def greet(step, carry, axis=axis, me=me, count=count):
            pl.semaphore_signal(
                barrier, inc=1, device_id={axis: lax.rem(me + step, count)}, device_id_type=MESH
            )
            return carry

        lax.fori_loop(1, count, greet, 0)

    load_classes = pltpu.make_async_copy(classes_hbm, classes, local_sem.at[0])
    load_ports = pltpu.make_async_copy(ports_hbm, ports, local_sem.at[1])
    load_basis = pltpu.make_async_copy(
        basis2.reshape(BLOCKS * COLS, rows, size_z),
        q2.reshape(BLOCKS * COLS, pitch, size_z).at[:, pl.ds(0, rows), :],
        local_sem.at[2],
    )
    load_block = pltpu.make_async_copy(
        basis4.at[pl.ds(first, COLS)],
        pad.at[:, pl.ds(REACH, size_x), pl.ds(size_y, size_y), :],
        block_sem,
    )
    load_taps = pltpu.make_async_copy(taps_hbm, taps_ref, local_sem.at[3])
    load_gain = pltpu.make_async_copy(gain_hbm, gain_ref, local_sem.at[4])
    load_taps.start()
    load_gain.start()
    load_classes.start()
    load_ports.start()
    load_block.start()
    load_basis.start()
    pl.semaphore_wait(barrier, nx + ny - 2)

    inner_x, inner_y = pl.ds(REACH, size_x), pl.ds(size_y, size_y)
    ways = (
        ("gy", 1, gy < ny - 1, gy > 0,
         (slice(None), pl.ds(size_y - REACH, REACH)), (inner_x, pl.ds(size_y - REACH, REACH))),
        ("gy", -1, gy > 0, gy < ny - 1,
         (slice(None), pl.ds(0, REACH)), (inner_x, pl.ds(2 * size_y, REACH))),
        ("gx", 1, gx < nx - 1, gx > 0,
         (pl.ds(size_x - REACH, REACH), slice(None)), (pl.ds(0, REACH), inner_y)),
        ("gx", -1, gx > 0, gx < nx - 1,
         (pl.ds(0, REACH), slice(None)), (pl.ds(REACH + size_x, REACH), inner_y)),
    )

    def halo(way, group):
        axis, step, _, _, (from_x, from_y), (to_x, to_y) = ways[way]
        return pltpu.make_async_remote_copy(
            src_ref=basis4.at[pl.ds(first + group * GROUP, GROUP), from_x, from_y, :],
            dst_ref=pad.at[pl.ds(group * GROUP, GROUP), to_x, to_y, :],
            send_sem=halo_send.at[way, group],
            recv_sem=halo_recv.at[way, group],
            device_id={axis: lax.axis_index(axis) + step},
            device_id_type=MESH,
        )

    relayed = COLS // GROUP - 1
    turns = []
    if row_length:
        for last in range(row_length - 1, nx - 1, row_length):
            turns += [(0, last, last + 1, last + row_length), (1, last + 1, last, last + 1 - row_length)]
    turning = [jnp.bool_(False), jnp.bool_(False)]
    for direction, source, _, _ in turns:
        turning[direction] = jnp.logical_or(turning[direction], gx == source)

    def to_corner(direction, corner):
        from_x, from_y = ways[2 + direction][4]
        return pltpu.make_async_remote_copy(
            src_ref=basis4.at[pl.ds(first + relayed * GROUP, GROUP), from_x, from_y, :],
            dst_ref=relay.at[direction],
            send_sem=relay_send.at[direction],
            recv_sem=relay_recv.at[direction],
            device_id={"gx": corner},
            device_id_type=MESH,
        )

    def from_corner(direction, target):
        to_x, to_y = ways[2 + direction][5]
        return pltpu.make_async_remote_copy(
            src_ref=relay.at[direction],
            dst_ref=pad.at[pl.ds(relayed * GROUP, GROUP), to_x, to_y, :],
            send_sem=forward_send.at[direction],
            recv_sem=halo_recv.at[2 + direction, relayed],
            device_id={"gx": target},
            device_id_type=MESH,
        )

    for direction, source, _, corner in turns:

        @pl.when(gx == source)
        def _(direction=direction, corner=corner):
            to_corner(direction, corner).start()

    def sends(way, group):
        if way < 2 or group != relayed:
            return ways[way][2]
        return jnp.logical_and(ways[way][2], jnp.logical_not(turning[way - 2]))

    for group in range(COLS // GROUP):
        for way in (2, 3, 0, 1):

            @pl.when(sends(way, group))
            def _(way=way, group=group):
                halo(way, group).start()

    for way in range(4):

        @pl.when(jnp.logical_not(ways[way][3]))
        def _(way=way):
            to_x, to_y = ways[way][5]
            pad[:, to_x, to_y, :] = jnp.zeros((COLS, to_x.size, to_y.size, size_z), jnp.float32)

    load_taps.wait()
    load_gain.wait()
    load_classes.wait()
    load_ports.wait()
    layers = LAYERS if size_x % LAYERS == 0 else 1
    z_sums = []
    for m in range(MAT):
        z_sum = taps_ref[m, 4 * REACH]
        for t in range(4 * REACH + 1, 6 * REACH):
            z_sum = z_sum + taps_ref[m, t]
        z_sums.append(z_sum)

    def make_coefs(step, carry):
        place = pl.ds(step * layers, layers)
        kind, port = classes[place], ports[place]
        bits = [(kind & (1 << b)) != 0 for b in range(3)]
        total = jnp.ones(kind.shape, jnp.float32)
        for p in range(PORTS):
            total = jnp.where(port == p + 1, 1.0 + gain_ref[p], total)
        for t in range(4 * REACH + 1):
            level = [taps_ref[m, t] for m in range(MAT)] if t < 4 * REACH else z_sums
            for bit in bits:
                level = [
                    jnp.where(bit, level[2 * i + 1], level[2 * i]) for i in range(len(level) // 2)
                ]
            total = total + level[0]
            if t < 4 * REACH:
                coefs[t, place] = level[0]
        diag[place] = total
        return carry

    lax.fori_loop(0, size_x // layers, make_coefs, 0)
    load_block.wait()

    distance = lax.broadcasted_iota(jnp.int32, (size_z, size_z), 0) - lax.broadcasted_iota(
        jnp.int32, (size_z, size_z), 1
    )

    def make_bands(pair, carry):
        both = []
        for m in (2 * pair, 2 * pair + 1):
            band = jnp.zeros((size_z, size_z), jnp.float32)
            for j in range(2 * REACH):
                band = jnp.where(distance == offset_of(j), taps_ref[m, 4 * REACH + j], band)
            both.append(band)
        band = jnp.concatenate(both, axis=1)
        high = band.astype(jnp.bfloat16).astype(jnp.float32)
        bands[pair] = jnp.concatenate([high, high, band - high], axis=0).astype(jnp.bfloat16)
        return carry

    lax.fori_loop(0, MAT // 2, make_bands, 0)

    def split_block(c, carry):
        place = pl.ds(pl.multiple_of(c * rows, rows), rows)
        image_place = pl.ds(pl.multiple_of(c * pitch, size_y), rows)
        own = pad[c, inner_x, inner_y, :]
        w2[image_place, :] = (diag[...] * own).reshape(rows, size_z)
        own = own.reshape(rows, size_z)
        high = own.astype(jnp.bfloat16).astype(jnp.float32)
        parts[place, :] = jnp.concatenate([high, own - high, high], axis=1).astype(jnp.bfloat16)
        return carry

    lax.fori_loop(0, COLS, split_block, 0)

    def along_z(pair, carry):
        kind = classes[...].reshape(rows, size_z)
        even, odd = kind == 2 * pair, kind == 2 * pair + 1
        for group in range(COLS // GROUP):
            lines = pl.ds(group * GROUP * rows, GROUP * rows)
            result = jnp.dot(parts[lines, :], bands[pair], preferred_element_type=jnp.float32)
            for i in range(GROUP):
                place = pl.ds((group * GROUP + i) * pitch, rows)
                mine = result[i * rows : (i + 1) * rows]
                w2[place, :] -= jnp.where(
                    even, mine[:, :size_z], jnp.where(odd, mine[:, size_z:], 0.0)
                )
        return carry

    lax.fori_loop(0, MAT // 2, along_z, 0)
    for direction, _, target, corner in turns:

        @pl.when(gx == corner)
        def _(direction=direction, target=target):
            to_corner(direction, target).wait_recv()
            from_corner(direction, target).start()

    load_basis.wait()

    def gather(ref, count, chunk):
        return jnp.concatenate(
            [
                ref[pl.ds(chunk * per_chunk + i, count, stride=pitch), :]
                for i in range(per_chunk)
            ],
            axis=1,
        )

    def own_products(chunk, acc):
        both = halves(gather(q2, BLOCKS * COLS, chunk))
        halved[chunk, : 2 * wide, :] = both
        return acc + lax.dot_general(both, both, NT, preferred_element_type=jnp.float32)

    wide = BLOCKS * COLS
    acc = lax.fori_loop(
        0, chunks, own_products, jnp.zeros((2 * wide, 2 * wide), jnp.float32), unroll=UNROLL
    )
    acc = acc[:wide] + acc[wide:]
    local_qq = acc[:, :wide] + acc[:, wide:]
    fill = jnp.zeros((wide, 128 - wide), jnp.float32)
    exchange = Exchange("gy", qq_y, qq_y_send, qq_y_recv)
    exchange.start(jnp.concatenate([local_qq, fill], axis=1))

    for axis, first_way in (("gy", 0), ("gx", 2)):
        for group in range(COLS // GROUP):
            for way in (first_way, first_way + 1):

                @pl.when(ways[way][3])
                def _(way=way, group=group):
                    halo(way, group).wait_recv()

            def along(x, carry, axis=axis, group=group):
                columns = range(group * GROUP, (group + 1) * GROUP)
                places = [
                    pl.ds(pl.multiple_of(c * pitch + x * size_y, size_y), size_y) for c in columns
                ]
                images = [w2[place, :] for place in places]
                for j in range(2 * REACH):
                    k = offset_of(j)
                    if axis == "gx":
                        coef, at_x, at_y = coefs[j, x], x + REACH + k, inner_y
                    else:
                        coef, at_x = coefs[2 * REACH + j, x], x + REACH
                        at_y = pl.ds(size_y + k, size_y)
                    for i, c in enumerate(columns):
                        images[i] = images[i] - coef * pad[c, at_x, at_y, :]
                for place, image in zip(places, images):
                    w2[place, :] = image
                return carry

            lax.fori_loop(0, size_x, along, 0, unroll=2)

    exchange_x = Exchange("gx", qq_x, qq_x_send, qq_x_recv)
    exchange_x.start(exchange.finish())

    def image_products(chunk, acc):
        both = halves(gather(w2, COLS, chunk))
        halved[chunk, 2 * wide :, :] = both
        return acc + lax.dot_general(halved[chunk], both, NT, preferred_element_type=jnp.float32)

    acc = lax.fori_loop(
        0,
        chunks,
        image_products,
        jnp.zeros((2 * (wide + COLS), 2 * COLS), jnp.float32),
        unroll=UNROLL,
    )
    acc = acc[:, :COLS] + acc[:, COLS:]
    local_g = jnp.concatenate(
        [
            acc[:wide] + acc[wide : 2 * wide],
            acc[2 * wide : 2 * wide + COLS] + acc[2 * wide + COLS :],
            jnp.zeros((128 - wide - COLS, COLS), jnp.float32),
        ],
        axis=0,
    ).T
    g_exchange = Exchange("gy", g_y, g_y_send, g_y_recv)
    g_exchange.start(local_g)
    sums[COLS:, :] = exchange_x.finish()
    g_exchange_x = Exchange("gx", g_x, g_x_send, g_x_recv)
    g_exchange_x.start(g_exchange.finish())
    sums[:COLS, :] = g_exchange_x.finish()
    for group in range(COLS // GROUP):
        for way in range(4):

            @pl.when(sends(way, group))
            def _(way=way, group=group):
                halo(way, group).wait_send()

    for direction, source, target, corner in turns:

        @pl.when(gx == source)
        def _(direction=direction, corner=corner):
            to_corner(direction, corner).wait_send()

        @pl.when(gx == corner)
        def _(direction=direction, target=target):
            from_corner(direction, target).wait_send()

    for each in (exchange, exchange_x, g_exchange, g_exchange_x):
        each.drain()


def combine_kernel(
    total_cells,
    halved,
    both_sums,
    out_hbm,
    proj_hbm,
    tri_hbm,
    out2,
    proj_ref,
    tri_ref,
    small_sem,
    out_sem,
):
    chunks, _, span = halved.shape
    pitch, size_z = out2.shape[0] // COLS, out2.shape[1]
    rows = pitch - PITCH
    per_chunk = span // size_z
    wide = BLOCKS * COLS
    sums = both_sums[:COLS, :] / total_cells
    sum_qq = both_sums[COLS:, :]
    proj_t = sums[:, :wide]
    proj_ref[...] = proj_t
    row = lax.broadcasted_iota(jnp.int32, (wide, wide), 0)
    column = lax.broadcasted_iota(jnp.int32, (wide, wide), 1)
    middle = jnp.where(row == column, 2.0, 0.0) - sum_qq[:, :wide] / total_cells
    left = jnp.dot(proj_t, middle, precision=HIGHEST, preferred_element_type=jnp.float32)
    gram = sums[:, wide : wide + COLS] - lax.dot_general(
        left, proj_t, NT, precision=HIGHEST, preferred_element_type=jnp.float32
    )
    row = lax.broadcasted_iota(jnp.int32, (COLS, COLS), 0)
    column = lax.broadcasted_iota(jnp.int32, (COLS, COLS), 1)
    eye = jnp.where(row == column, 1.0, 0.0)
    table = jnp.concatenate([-proj_t, eye, gram], axis=1)
    base = wide + COLS
    index = lax.broadcasted_iota(jnp.int32, table.shape, 0)
    for j in range(COLS - 1):
        factor = jnp.broadcast_to(table[:, base + j : base + j + 1], table.shape)
        factor = jnp.where(index > j, factor / factor[j : j + 1, :], 0.0)
        table = table - factor * table[j : j + 1, :]
    pivots = jnp.sum(jnp.where(row == column, table[:, base:], 0.0), axis=1, keepdims=True)
    table = table * lax.rsqrt(pivots)
    tri_ref[...] = jnp.where(row <= column, table[:, base:], 0.0)
    store_proj = pltpu.make_async_copy(proj_ref, proj_hbm, small_sem.at[0])
    store_tri = pltpu.make_async_copy(tri_ref, tri_hbm, small_sem.at[1])
    store_proj.start()
    store_tri.start()

    mix = table[:, :base]
    high = mix.astype(jnp.bfloat16).astype(jnp.float32)
    mix = jnp.concatenate([high, mix - high], axis=0)
    mix_q, mix_w = mix[:, :wide], mix[:, wide:]
    mix = jnp.concatenate([mix_q, mix_q, mix_w, mix_w], axis=1).astype(jnp.bfloat16)

    def store(chunk):
        part = pl.ds(pl.multiple_of(chunk * per_chunk, per_chunk), per_chunk)
        return pltpu.make_async_copy(
            out2.reshape(COLS, pitch, size_z).at[:, part, :], out_hbm.at[:, part, :], out_sem.at[chunk]
        )

    def combine(chunk, carry):
        result = jnp.dot(mix, halved[chunk], preferred_element_type=jnp.float32)
        result = result[:COLS] + result[COLS:]
        for i in range(per_chunk):
            out2[pl.ds(chunk * per_chunk + i, COLS, stride=pitch), :] = result[
                :, i * size_z : (i + 1) * size_z
            ]
        store(chunk).start()
        return carry

    lax.fori_loop(0, chunks, combine, 0, unroll=UNROLL)

    def drain(chunk, carry):
        store(chunk).wait()
        return carry

    lax.fori_loop(0, chunks, drain, 0)
    store_proj.wait()
    store_tri.wait()


def per_device(row_length, basis, classes, ports, taps, port_gain):
    size_x, size_y, size_z = classes.shape
    rows = size_x * size_y
    wide = BLOCKS * COLS
    nx, ny = lax.axis_size("gx"), lax.axis_size("gy")
    per_chunk = 16 if rows % 16 == 0 else 1
    chunks, span = rows // per_chunk, per_chunk * size_z
    vmem = functools.partial(pltpu.VMEM, dtype=jnp.float32)
    dma = pltpu.SemaphoreType.DMA
    hbm = pl.BlockSpec(memory_space=pltpu.HBM)
    vmem_spec = pl.BlockSpec(memory_space=pltpu.VMEM)
    groups = COLS // GROUP
    halved_shape = (chunks, 2 * (wide + COLS), span)
    sums_shape = (COLS + wide, 128)
    halved, sums = pl.pallas_call(
        functools.partial(gather_kernel, row_length),
        out_shape=(
            jax.ShapeDtypeStruct(halved_shape, jnp.bfloat16),
            jax.ShapeDtypeStruct(sums_shape, jnp.float32),
        ),
        in_specs=[hbm] * 6,
        out_specs=(vmem_spec,) * 2,
        scratch_shapes=[
            pltpu.SMEM(taps.shape, jnp.float32),
            pltpu.SMEM(port_gain.shape, jnp.float32),
            vmem((COLS, size_x + 2 * REACH, 3 * size_y, size_z)),
            vmem((wide * (rows + PITCH), size_z)),
            vmem((COLS * (rows + PITCH), size_z)),
            vmem((4 * REACH, size_x, size_y, size_z)),
            vmem((size_x, size_y, size_z)),
            pltpu.VMEM((MAT // 2, 3 * size_z, 2 * size_z), jnp.bfloat16),
            pltpu.VMEM((COLS * rows, 3 * size_z), jnp.bfloat16),
            pltpu.VMEM((size_x, size_y, size_z), jnp.int32),
            pltpu.VMEM((size_x, size_y, size_z), jnp.int32),
            vmem((2, GROUP, REACH, size_y, size_z)),
            vmem((ny, wide, 128)),
            vmem((nx, wide, 128)),
            vmem((ny, COLS, 128)),
            vmem((nx, COLS, 128)),
            dma((5,)),
            dma,
            dma((4, groups)),
            dma((4, groups)),
            dma((2,)),
            dma((2,)),
            dma((2,)),
            dma((ny,)),
            dma((ny,)),
            dma((nx,)),
            dma((nx,)),
            dma((ny,)),
            dma((ny,)),
            dma((nx,)),
            dma((nx,)),
        ],
        compiler_params=pltpu.CompilerParams(
            collective_id=0, has_side_effects=True, vmem_limit_bytes=40 * 1024 * 1024
        ),
    )(
        *(
            pltpu.with_memory_space_constraint(operand, pltpu.HBM)
            for operand in (
                taps, port_gain, basis, basis.reshape(wide * rows, size_z), classes, ports
            )
        )
    )
    out, projection, triangle = pl.pallas_call(
        functools.partial(combine_kernel, float(rows * size_z * nx * ny)),
        out_shape=(
            jax.ShapeDtypeStruct((COLS, rows, size_z), jnp.float32),
            jax.ShapeDtypeStruct((COLS, wide), jnp.float32),
            jax.ShapeDtypeStruct((COLS, COLS), jnp.float32),
        ),
        in_specs=[vmem_spec] * 2,
        out_specs=(hbm,) * 3,
        scratch_shapes=[
            vmem((COLS * (rows + PITCH), size_z)),
            vmem((COLS, wide)),
            vmem((COLS, COLS)),
            dma((2,)),
            dma((chunks,)),
        ],
        compiler_params=pltpu.CompilerParams(vmem_limit_bytes=24 * 1024 * 1024),
    )(halved, sums)
    return out.reshape(COLS, size_x, size_y, size_z), projection.T, triangle


def length_of_row(mesh):
    places = [getattr(device, "coords", None) for device in mesh.devices[:, 0]]
    if None in places:
        return 0
    for i in range(1, len(places)):
        if sum(a != b for a, b in zip(places[i - 1], places[i])) > 1:
            return i if len(places) % i == 0 else 0
    return 0


def solution(mesh):
    in_specs = (P(None, "gx", "gy", None), P("gx", "gy", None), P("gx", "gy", None), P(), P())
    out_specs = (P(None, "gx", "gy", None), P(), P())
    return jax.shard_map(
        functools.partial(per_device, length_of_row(mesh)), mesh=mesh, in_specs=in_specs, out_specs=out_specs, check_vma=False
    )
```

```python
import functools

import jax
import jax.numpy as jnp
from jax import lax
from jax.experimental import pallas as pl
from jax.experimental.pallas import tpu as pltpu
from jax.sharding import PartitionSpec as P

COLS = 8
BLOCKS = 4
REACH = 7
MAT = 8
PORTS = 8
GROUP = 4
LAYERS = 4
UNROLL = 4
PITCH = 8
MESH = pl.DeviceIdType.MESH
NT = (((1,), (1,)), ((), ()))
HIGHEST = lax.Precision.HIGHEST


def offset_of(j):
    return j - REACH if j < REACH else j - REACH + 1


def halves(value):
    high = value.astype(jnp.bfloat16).astype(jnp.float32)
    return jnp.concatenate([high, value - high], axis=0).astype(jnp.bfloat16)


class Exchange:
    def __init__(self, axis, buf, send, recv):
        self.axis, self.buf, self.send, self.recv = axis, buf, send, recv
        self.me, self.count = lax.axis_index(axis), lax.axis_size(axis)

    def copy(self, step, slot, peer):
        return pltpu.make_async_remote_copy(
            src_ref=self.buf.at[slot],
            dst_ref=self.buf.at[slot],
            send_sem=self.send.at[step],
            recv_sem=self.recv.at[slot],
            device_id={self.axis: peer},
            device_id_type=MESH,
        )

    def start(self, value):
        self.buf[self.me] = value

        def body(step, carry):
            self.copy(step, self.me, lax.rem(self.me + step, self.count)).start()
            return carry

        lax.fori_loop(1, self.count, body, 0, unroll=self.count <= 8)

    def finish(self):
        def body(step, carry):
            peer = lax.rem(self.me + step, self.count)
            self.copy(step, peer, peer).wait_recv()
            return carry

        lax.fori_loop(1, self.count, body, 0, unroll=self.count <= 8)
        total = self.buf[0]
        for slot in range(1, self.count):
            total = total + self.buf[slot]
        return total

    def drain(self):
        def body(step, carry):
            self.copy(step, self.me, lax.rem(self.me + step, self.count)).wait_send()
            return carry

        lax.fori_loop(1, self.count, body, 0, unroll=self.count <= 8)


def gather_kernel(
    row_length,
    taps_hbm,
    gain_hbm,
    basis4,
    basis2,
    classes_hbm,
    ports_hbm,
    halved,
    sums,
    taps_ref,
    gain_ref,
    pad,
    q2,
    w2,
    coefs,
    diag,
    bands,
    parts,
    classes,
    ports,
    relay,
    qq_y,
    qq_x,
    g_y,
    g_x,
    local_sem,
    block_sem,
    halo_send,
    halo_recv,
    relay_send,
    relay_recv,
    forward_send,
    qq_y_send,
    qq_y_recv,
    qq_x_send,
    qq_x_recv,
    g_y_send,
    g_y_recv,
    g_x_send,
    g_x_recv,
):
    size_x, size_y, size_z = classes.shape
    rows = size_x * size_y
    pitch = rows + PITCH
    first = (BLOCKS - 1) * COLS
    gx, gy = lax.axis_index("gx"), lax.axis_index("gy")
    nx, ny = lax.axis_size("gx"), lax.axis_size("gy")
    chunks, _, span = halved.shape
    per_chunk = span // size_z

    barrier = pltpu.get_barrier_semaphore()
    for axis, me, count in (("gx", gx, nx), ("gy", gy, ny)):

        def greet(step, carry, axis=axis, me=me, count=count):
            pl.semaphore_signal(
                barrier, inc=1, device_id={axis: lax.rem(me + step, count)}, device_id_type=MESH
            )
            return carry

        lax.fori_loop(1, count, greet, 0)

    load_classes = pltpu.make_async_copy(classes_hbm, classes, local_sem.at[0])
    load_ports = pltpu.make_async_copy(ports_hbm, ports, local_sem.at[1])
    load_basis = pltpu.make_async_copy(
        basis2.reshape(BLOCKS * COLS, rows, size_z),
        q2.reshape(BLOCKS * COLS, pitch, size_z).at[:, pl.ds(0, rows), :],
        local_sem.at[2],
    )
    load_block = pltpu.make_async_copy(
        basis4.at[pl.ds(first, COLS)],
        pad.at[:, pl.ds(REACH, size_x), pl.ds(size_y, size_y), :],
        block_sem,
    )
    load_taps = pltpu.make_async_copy(taps_hbm, taps_ref, local_sem.at[3])
    load_gain = pltpu.make_async_copy(gain_hbm, gain_ref, local_sem.at[4])
    load_taps.start()
    load_gain.start()
    load_classes.start()
    load_ports.start()
    load_block.start()
    load_basis.start()
    pl.semaphore_wait(barrier, nx + ny - 2)

    inner_x, inner_y = pl.ds(REACH, size_x), pl.ds(size_y, size_y)
    ways = (
        ("gy", 1, gy < ny - 1, gy > 0,
         (slice(None), pl.ds(size_y - REACH, REACH)), (inner_x, pl.ds(size_y - REACH, REACH))),
        ("gy", -1, gy > 0, gy < ny - 1,
         (slice(None), pl.ds(0, REACH)), (inner_x, pl.ds(2 * size_y, REACH))),
        ("gx", 1, gx < nx - 1, gx > 0,
         (pl.ds(size_x - REACH, REACH), slice(None)), (pl.ds(0, REACH), inner_y)),
        ("gx", -1, gx > 0, gx < nx - 1,
         (pl.ds(0, REACH), slice(None)), (pl.ds(REACH + size_x, REACH), inner_y)),
    )

    def halo(way, group):
        axis, step, _, _, (from_x, from_y), (to_x, to_y) = ways[way]
        return pltpu.make_async_remote_copy(
            src_ref=basis4.at[pl.ds(first + group * GROUP, GROUP), from_x, from_y, :],
            dst_ref=pad.at[pl.ds(group * GROUP, GROUP), to_x, to_y, :],
            send_sem=halo_send.at[way, group],
            recv_sem=halo_recv.at[way, group],
            device_id={axis: lax.axis_index(axis) + step},
            device_id_type=MESH,
        )

    relayed = COLS // GROUP - 1
    turns = []
    if row_length:
        for last in range(row_length - 1, nx - 1, row_length):
            turns += [(0, last, last + 1, last + row_length), (1, last + 1, last, last + 1 - row_length)]
    turning = [jnp.bool_(False), jnp.bool_(False)]
    for direction, source, _, _ in turns:
        turning[direction] = jnp.logical_or(turning[direction], gx == source)

    def to_corner(direction, corner):
        from_x, from_y = ways[2 + direction][4]
        return pltpu.make_async_remote_copy(
            src_ref=basis4.at[pl.ds(first + relayed * GROUP, GROUP), from_x, from_y, :],
            dst_ref=relay.at[direction],
            send_sem=relay_send.at[direction],
            recv_sem=relay_recv.at[direction],
            device_id={"gx": corner},
            device_id_type=MESH,
        )

    def from_corner(direction, target):
        to_x, to_y = ways[2 + direction][5]
        return pltpu.make_async_remote_copy(
            src_ref=relay.at[direction],
            dst_ref=pad.at[pl.ds(relayed * GROUP, GROUP), to_x, to_y, :],
            send_sem=forward_send.at[direction],
            recv_sem=halo_recv.at[2 + direction, relayed],
            device_id={"gx": target},
            device_id_type=MESH,
        )

    for direction, source, _, corner in turns:

        @pl.when(gx == source)
        def _(direction=direction, corner=corner):
            to_corner(direction, corner).start()

    def sends(way, group):
        if way < 2 or group != relayed:
            return ways[way][2]
        return jnp.logical_and(ways[way][2], jnp.logical_not(turning[way - 2]))

    for group in range(COLS // GROUP):
        for way in (2, 3, 0, 1):

            @pl.when(sends(way, group))
            def _(way=way, group=group):
                halo(way, group).start()

    for way in range(4):

        @pl.when(jnp.logical_not(ways[way][3]))
        def _(way=way):
            to_x, to_y = ways[way][5]
            pad[:, to_x, to_y, :] = jnp.zeros((COLS, to_x.size, to_y.size, size_z), jnp.float32)

    load_taps.wait()
    load_gain.wait()
    load_classes.wait()
    load_ports.wait()
    layers = LAYERS if size_x % LAYERS == 0 else 1
    z_sums = []
    for m in range(MAT):
        z_sum = taps_ref[m, 4 * REACH]
        for t in range(4 * REACH + 1, 6 * REACH):
            z_sum = z_sum + taps_ref[m, t]
        z_sums.append(z_sum)

    def make_coefs(step, carry):
        place = pl.ds(step * layers, layers)
        kind, port = classes[place], ports[place]
        bits = [(kind & (1 << b)) != 0 for b in range(3)]
        total = jnp.ones(kind.shape, jnp.float32)
        for p in range(PORTS):
            total = jnp.where(port == p + 1, 1.0 + gain_ref[p], total)
        for t in range(4 * REACH + 1):
            level = [taps_ref[m, t] for m in range(MAT)] if t < 4 * REACH else z_sums
            for bit in bits:
                level = [
                    jnp.where(bit, level[2 * i + 1], level[2 * i]) for i in range(len(level) // 2)
                ]
            total = total + level[0]
            if t < 4 * REACH:
                coefs[t, place] = level[0]
        diag[place] = total
        return carry

    lax.fori_loop(0, size_x // layers, make_coefs, 0)
    load_block.wait()

    distance = lax.broadcasted_iota(jnp.int32, (size_z, size_z), 0) - lax.broadcasted_iota(
        jnp.int32, (size_z, size_z), 1
    )

    def make_bands(pair, carry):
        both = []
        for m in (2 * pair, 2 * pair + 1):
            band = jnp.zeros((size_z, size_z), jnp.float32)
            for j in range(2 * REACH):
                band = jnp.where(distance == offset_of(j), taps_ref[m, 4 * REACH + j], band)
            both.append(band)
        band = jnp.concatenate(both, axis=1)
        high = band.astype(jnp.bfloat16).astype(jnp.float32)
        bands[pair] = jnp.concatenate([high, high, band - high], axis=0).astype(jnp.bfloat16)
        return carry

    lax.fori_loop(0, MAT // 2, make_bands, 0)

    def split_block(c, carry):
        place = pl.ds(pl.multiple_of(c * rows, rows), rows)
        image_place = pl.ds(pl.multiple_of(c * pitch, size_y), rows)
        own = pad[c, inner_x, inner_y, :]
        w2[image_place, :] = (diag[...] * own).reshape(rows, size_z)
        own = own.reshape(rows, size_z)
        high = own.astype(jnp.bfloat16).astype(jnp.float32)
        parts[place, :] = jnp.concatenate([high, own - high, high], axis=1).astype(jnp.bfloat16)
        return carry

    lax.fori_loop(0, COLS, split_block, 0)

    def along_z(pair, carry):
        kind = classes[...].reshape(rows, size_z)
        even, odd = kind == 2 * pair, kind == 2 * pair + 1
        for group in range(COLS // GROUP):
            lines = pl.ds(group * GROUP * rows, GROUP * rows)
            result = jnp.dot(parts[lines, :], bands[pair], preferred_element_type=jnp.float32)
            for i in range(GROUP):
                place = pl.ds((group * GROUP + i) * pitch, rows)
                mine = result[i * rows : (i + 1) * rows]
                w2[place, :] -= jnp.where(
                    even, mine[:, :size_z], jnp.where(odd, mine[:, size_z:], 0.0)
                )
        return carry

    lax.fori_loop(0, MAT // 2, along_z, 0)
    for direction, _, target, corner in turns:

        @pl.when(gx == corner)
        def _(direction=direction, target=target):
            to_corner(direction, target).wait_recv()
            from_corner(direction, target).start()

    load_basis.wait()

    def gather(ref, count, chunk):
        return jnp.concatenate(
            [
                ref[pl.ds(chunk * per_chunk + i, count, stride=pitch), :]
                for i in range(per_chunk)
            ],
            axis=1,
        )

    def own_products(chunk, acc):
        both = halves(gather(q2, BLOCKS * COLS, chunk))
        halved[chunk, : 2 * wide, :] = both
        return acc + lax.dot_general(both, both[:wide], NT, preferred_element_type=jnp.float32)

    wide = BLOCKS * COLS
    acc = lax.fori_loop(
        0, chunks, own_products, jnp.zeros((2 * wide, wide), jnp.float32), unroll=UNROLL
    )
    local_qq = acc[:wide] + acc[wide:] + acc[wide:].T
    exchange = Exchange("gy", qq_y, qq_y_send, qq_y_recv)
    exchange.start(
        jnp.concatenate([local_qq[i : i + COLS] for i in range(0, wide, COLS)], axis=1)
    )

    for axis, first_way in (("gy", 0), ("gx", 2)):
        for group in range(COLS // GROUP):
            for way in (first_way, first_way + 1):

                @pl.when(ways[way][3])
                def _(way=way, group=group):
                    halo(way, group).wait_recv()

            def along(x, carry, axis=axis, group=group):
                columns = range(group * GROUP, (group + 1) * GROUP)
                places = [
                    pl.ds(pl.multiple_of(c * pitch + x * size_y, size_y), size_y) for c in columns
                ]
                images = [w2[place, :] for place in places]
                for j in range(2 * REACH):
                    k = offset_of(j)
                    if axis == "gx":
                        coef, at_x, at_y = coefs[j, x], x + REACH + k, inner_y
                    else:
                        coef, at_x = coefs[2 * REACH + j, x], x + REACH
                        at_y = pl.ds(size_y + k, size_y)
                    for i, c in enumerate(columns):
                        images[i] = images[i] - coef * pad[c, at_x, at_y, :]
                for place, image in zip(places, images):
                    w2[place, :] = image
                return carry

            lax.fori_loop(0, size_x, along, 0, unroll=2)

    exchange_x = Exchange("gx", qq_x, qq_x_send, qq_x_recv)
    exchange_x.start(exchange.finish())

    def image_products(chunk, acc):
        both = halves(gather(w2, COLS, chunk))
        halved[chunk, 2 * wide :, :] = both
        return acc + lax.dot_general(halved[chunk], both, NT, preferred_element_type=jnp.float32)

    acc = lax.fori_loop(
        0,
        chunks,
        image_products,
        jnp.zeros((2 * (wide + COLS), 2 * COLS), jnp.float32),
        unroll=UNROLL,
    )
    acc = acc[:, :COLS] + acc[:, COLS:]
    local_g = jnp.concatenate(
        [
            acc[:wide] + acc[wide : 2 * wide],
            acc[2 * wide : 2 * wide + COLS] + acc[2 * wide + COLS :],
            jnp.zeros((128 - wide - COLS, COLS), jnp.float32),
        ],
        axis=0,
    ).T
    g_exchange = Exchange("gy", g_y, g_y_send, g_y_recv)
    g_exchange.start(local_g)
    sums[COLS:, :] = exchange_x.finish()
    for group in range(COLS // GROUP):
        for way in range(4):

            @pl.when(sends(way, group))
            def _(way=way, group=group):
                halo(way, group).wait_send()

    for direction, source, target, corner in turns:

        @pl.when(gx == source)
        def _(direction=direction, corner=corner):
            to_corner(direction, corner).wait_send()

        @pl.when(gx == corner)
        def _(direction=direction, target=target):
            from_corner(direction, target).wait_send()

    exchange.drain()
    exchange_x.drain()
    g_exchange_x = Exchange("gx", g_x, g_x_send, g_x_recv)
    g_exchange_x.start(g_exchange.finish())
    sums[:COLS, :] = g_exchange_x.finish()
    g_exchange.drain()
    g_exchange_x.drain()


def combine_kernel(
    total_cells,
    halved,
    both_sums,
    out_hbm,
    proj_hbm,
    tri_hbm,
    out2,
    proj_ref,
    tri_ref,
    small_sem,
    out_sem,
):
    chunks, _, span = halved.shape
    pitch, size_z = out2.shape[0] // COLS, out2.shape[1]
    rows = pitch - PITCH
    per_chunk = span // size_z
    wide = BLOCKS * COLS
    sums = both_sums[:COLS, :] / total_cells
    sum_qq = jnp.concatenate(
        [both_sums[COLS:, i * wide : (i + 1) * wide] for i in range(BLOCKS)], axis=0
    )
    proj_t = sums[:, :wide]
    proj_ref[...] = proj_t
    row = lax.broadcasted_iota(jnp.int32, (wide, wide), 0)
    column = lax.broadcasted_iota(jnp.int32, (wide, wide), 1)
    middle = jnp.where(row == column, 2.0, 0.0) - sum_qq / total_cells
    left = jnp.dot(proj_t, middle, precision=HIGHEST, preferred_element_type=jnp.float32)
    gram = sums[:, wide : wide + COLS] - lax.dot_general(
        left, proj_t, NT, precision=HIGHEST, preferred_element_type=jnp.float32
    )
    row = lax.broadcasted_iota(jnp.int32, (COLS, COLS), 0)
    column = lax.broadcasted_iota(jnp.int32, (COLS, COLS), 1)
    eye = jnp.where(row == column, 1.0, 0.0)
    table = jnp.concatenate([-proj_t, eye, gram], axis=1)
    base = wide + COLS
    index = lax.broadcasted_iota(jnp.int32, table.shape, 0)
    for j in range(COLS - 1):
        factor = jnp.broadcast_to(table[:, base + j : base + j + 1], table.shape)
        factor = jnp.where(index > j, factor / factor[j : j + 1, :], 0.0)
        table = table - factor * table[j : j + 1, :]
    pivots = jnp.sum(jnp.where(row == column, table[:, base:], 0.0), axis=1, keepdims=True)
    table = table * lax.rsqrt(pivots)
    tri_ref[...] = jnp.where(row <= column, table[:, base:], 0.0)
    store_proj = pltpu.make_async_copy(proj_ref, proj_hbm, small_sem.at[0])
    store_tri = pltpu.make_async_copy(tri_ref, tri_hbm, small_sem.at[1])
    store_proj.start()
    store_tri.start()

    mix = table[:, :base]
    high = mix.astype(jnp.bfloat16).astype(jnp.float32)
    mix = jnp.concatenate([high, mix - high], axis=0)
    mix_q, mix_w = mix[:, :wide], mix[:, wide:]
    mix = jnp.concatenate([mix_q, mix_q, mix_w, mix_w], axis=1).astype(jnp.bfloat16)

    def store(chunk):
        part = pl.ds(pl.multiple_of(chunk * per_chunk, per_chunk), per_chunk)
        return pltpu.make_async_copy(
            out2.reshape(COLS, pitch, size_z).at[:, part, :], out_hbm.at[:, part, :], out_sem.at[chunk]
        )

    def combine(chunk, carry):
        result = jnp.dot(mix, halved[chunk], preferred_element_type=jnp.float32)
        result = result[:COLS] + result[COLS:]
        for i in range(per_chunk):
            out2[pl.ds(chunk * per_chunk + i, COLS, stride=pitch), :] = result[
                :, i * size_z : (i + 1) * size_z
            ]
        store(chunk).start()
        return carry

    lax.fori_loop(0, chunks, combine, 0, unroll=UNROLL)

    def drain(chunk, carry):
        store(chunk).wait()
        return carry

    lax.fori_loop(0, chunks, drain, 0)
    store_proj.wait()
    store_tri.wait()


def per_device(row_length, basis, classes, ports, taps, port_gain):
    size_x, size_y, size_z = classes.shape
    rows = size_x * size_y
    wide = BLOCKS * COLS
    nx, ny = lax.axis_size("gx"), lax.axis_size("gy")
    per_chunk = 16 if rows % 16 == 0 else 1
    chunks, span = rows // per_chunk, per_chunk * size_z
    vmem = functools.partial(pltpu.VMEM, dtype=jnp.float32)
    dma = pltpu.SemaphoreType.DMA
    hbm = pl.BlockSpec(memory_space=pltpu.HBM)
    vmem_spec = pl.BlockSpec(memory_space=pltpu.VMEM)
    groups = COLS // GROUP
    halved_shape = (chunks, 2 * (wide + COLS), span)
    sums_shape = (2 * COLS, BLOCKS * wide)
    halved, sums = pl.pallas_call(
        functools.partial(gather_kernel, row_length),
        out_shape=(
            jax.ShapeDtypeStruct(halved_shape, jnp.bfloat16),
            jax.ShapeDtypeStruct(sums_shape, jnp.float32),
        ),
        in_specs=[hbm] * 6,
        out_specs=(vmem_spec,) * 2,
        scratch_shapes=[
            pltpu.SMEM(taps.shape, jnp.float32),
            pltpu.SMEM(port_gain.shape, jnp.float32),
            vmem((COLS, size_x + 2 * REACH, 3 * size_y, size_z)),
            vmem((wide * (rows + PITCH), size_z)),
            vmem((COLS * (rows + PITCH), size_z)),
            vmem((4 * REACH, size_x, size_y, size_z)),
            vmem((size_x, size_y, size_z)),
            pltpu.VMEM((MAT // 2, 3 * size_z, 2 * size_z), jnp.bfloat16),
            pltpu.VMEM((COLS * rows, 3 * size_z), jnp.bfloat16),
            pltpu.VMEM((size_x, size_y, size_z), jnp.int32),
            pltpu.VMEM((size_x, size_y, size_z), jnp.int32),
            vmem((2, GROUP, REACH, size_y, size_z)),
            vmem((ny, COLS, BLOCKS * wide)),
            vmem((nx, COLS, BLOCKS * wide)),
            vmem((ny, COLS, 128)),
            vmem((nx, COLS, 128)),
            dma((5,)),
            dma,
            dma((4, groups)),
            dma((4, groups)),
            dma((2,)),
            dma((2,)),
            dma((2,)),
            dma((ny,)),
            dma((ny,)),
            dma((nx,)),
            dma((nx,)),
            dma((ny,)),
            dma((ny,)),
            dma((nx,)),
            dma((nx,)),
        ],
        compiler_params=pltpu.CompilerParams(
            collective_id=0, has_side_effects=True, vmem_limit_bytes=40 * 1024 * 1024
        ),
    )(
        *(
            pltpu.with_memory_space_constraint(operand, pltpu.HBM)
            for operand in (
                taps, port_gain, basis, basis.reshape(wide * rows, size_z), classes, ports
            )
        )
    )
    out, projection, triangle = pl.pallas_call(
        functools.partial(combine_kernel, float(rows * size_z * nx * ny)),
        out_shape=(
            jax.ShapeDtypeStruct((COLS, rows, size_z), jnp.float32),
            jax.ShapeDtypeStruct((COLS, wide), jnp.float32),
            jax.ShapeDtypeStruct((COLS, COLS), jnp.float32),
        ),
        in_specs=[vmem_spec] * 2,
        out_specs=(hbm,) * 3,
        scratch_shapes=[
            vmem((COLS * (rows + PITCH), size_z)),
            vmem((COLS, wide)),
            vmem((COLS, COLS)),
            dma((2,)),
            dma((chunks,)),
        ],
        compiler_params=pltpu.CompilerParams(vmem_limit_bytes=24 * 1024 * 1024),
    )(halved, sums)
    return out.reshape(COLS, size_x, size_y, size_z), projection.T, triangle


def length_of_row(mesh):
    places = [getattr(device, "coords", None) for device in mesh.devices[:, 0]]
    if None in places:
        return 0
    for i in range(1, len(places)):
        if sum(a != b for a, b in zip(places[i - 1], places[i])) > 1:
            return i if len(places) % i == 0 else 0
    return 0


def solution(mesh):
    in_specs = (P(None, "gx", "gy", None), P("gx", "gy", None), P("gx", "gy", None), P(), P())
    out_specs = (P(None, "gx", "gy", None), P(), P())
    return jax.shard_map(
        functools.partial(per_device, length_of_row(mesh)), mesh=mesh, in_specs=in_specs, out_specs=out_specs, check_vma=False
    )
```

```python
import functools

import jax
import jax.numpy as jnp
from jax import lax
from jax.experimental import pallas as pl
from jax.experimental.pallas import tpu as pltpu
from jax.sharding import PartitionSpec as P

COLS = 8
BLOCKS = 4
REACH = 7
MAT = 8
PORTS = 8
GROUP = 4
LAYERS = 4
UNROLL = 4
PITCH = 8
MESH = pl.DeviceIdType.MESH
NT = (((1,), (1,)), ((), ()))
HIGHEST = lax.Precision.HIGHEST


def offset_of(j):
    return j - REACH if j < REACH else j - REACH + 1


def halves(value):
    high = value.astype(jnp.bfloat16).astype(jnp.float32)
    return jnp.concatenate([high, value - high], axis=0).astype(jnp.bfloat16)


class Exchange:
    def __init__(self, axis, buf, send, recv):
        self.axis, self.buf, self.send, self.recv = axis, buf, send, recv
        self.me, self.count = lax.axis_index(axis), lax.axis_size(axis)

    def copy(self, step, slot, peer):
        return pltpu.make_async_remote_copy(
            src_ref=self.buf.at[slot],
            dst_ref=self.buf.at[slot],
            send_sem=self.send.at[step],
            recv_sem=self.recv.at[slot],
            device_id={self.axis: peer},
            device_id_type=MESH,
        )

    def start(self, value):
        self.buf[self.me] = value

        def body(step, carry):
            self.copy(step, self.me, lax.rem(self.me + step, self.count)).start()
            return carry

        lax.fori_loop(1, self.count, body, 0, unroll=self.count <= 8)

    def finish(self):
        def body(step, carry):
            peer = lax.rem(self.me + step, self.count)
            self.copy(step, peer, peer).wait_recv()
            return carry

        lax.fori_loop(1, self.count, body, 0, unroll=self.count <= 8)
        total = self.buf[0]
        for slot in range(1, self.count):
            total = total + self.buf[slot]
        return total

    def drain(self):
        def body(step, carry):
            self.copy(step, self.me, lax.rem(self.me + step, self.count)).wait_send()
            return carry

        lax.fori_loop(1, self.count, body, 0, unroll=self.count <= 8)


def gather_kernel(
    row_length,
    taps_hbm,
    gain_hbm,
    basis4,
    basis2,
    classes_hbm,
    ports_hbm,
    halved,
    sums,
    taps_ref,
    gain_ref,
    pad,
    q2,
    w2,
    coefs,
    diag,
    bands,
    parts,
    classes,
    ports,
    relay,
    qq_y,
    qq_x,
    g_y,
    g_x,
    local_sem,
    block_sem,
    halo_send,
    halo_recv,
    relay_send,
    relay_recv,
    forward_send,
    qq_y_send,
    qq_y_recv,
    qq_x_send,
    qq_x_recv,
    g_y_send,
    g_y_recv,
    g_x_send,
    g_x_recv,
):
    size_x, size_y, size_z = classes.shape
    rows = size_x * size_y
    pitch = rows + PITCH
    first = (BLOCKS - 1) * COLS
    gx, gy = lax.axis_index("gx"), lax.axis_index("gy")
    nx, ny = lax.axis_size("gx"), lax.axis_size("gy")
    chunks, _, span = halved.shape
    per_chunk = span // size_z

    barrier = pltpu.get_barrier_semaphore()
    for axis, me, count in (("gx", gx, nx), ("gy", gy, ny)):

        def greet(step, carry, axis=axis, me=me, count=count):
            pl.semaphore_signal(
                barrier, inc=1, device_id={axis: lax.rem(me + step, count)}, device_id_type=MESH
            )
            return carry

        lax.fori_loop(1, count, greet, 0)

    load_classes = pltpu.make_async_copy(classes_hbm, classes, local_sem.at[0])
    load_ports = pltpu.make_async_copy(ports_hbm, ports, local_sem.at[1])
    load_basis = pltpu.make_async_copy(
        basis2.reshape(BLOCKS * COLS, rows, size_z),
        q2.reshape(BLOCKS * COLS, pitch, size_z).at[:, pl.ds(0, rows), :],
        local_sem.at[2],
    )
    load_block = pltpu.make_async_copy(
        basis4.at[pl.ds(first, COLS)],
        pad.at[:, pl.ds(REACH, size_x), pl.ds(size_y, size_y), :],
        block_sem,
    )
    load_taps = pltpu.make_async_copy(taps_hbm, taps_ref, local_sem.at[3])
    load_gain = pltpu.make_async_copy(gain_hbm, gain_ref, local_sem.at[4])
    load_taps.start()
    load_gain.start()
    load_classes.start()
    load_ports.start()
    load_block.start()
    load_basis.start()
    pl.semaphore_wait(barrier, nx + ny - 2)

    inner_x, inner_y = pl.ds(REACH, size_x), pl.ds(size_y, size_y)
    ways = (
        ("gy", 1, gy < ny - 1, gy > 0,
         (slice(None), pl.ds(size_y - REACH, REACH)), (inner_x, pl.ds(size_y - REACH, REACH))),
        ("gy", -1, gy > 0, gy < ny - 1,
         (slice(None), pl.ds(0, REACH)), (inner_x, pl.ds(2 * size_y, REACH))),
        ("gx", 1, gx < nx - 1, gx > 0,
         (pl.ds(size_x - REACH, REACH), slice(None)), (pl.ds(0, REACH), inner_y)),
        ("gx", -1, gx > 0, gx < nx - 1,
         (pl.ds(0, REACH), slice(None)), (pl.ds(REACH + size_x, REACH), inner_y)),
    )

    def halo(way, group):
        axis, step, _, _, (from_x, from_y), (to_x, to_y) = ways[way]
        return pltpu.make_async_remote_copy(
            src_ref=basis4.at[pl.ds(first + group * GROUP, GROUP), from_x, from_y, :],
            dst_ref=pad.at[pl.ds(group * GROUP, GROUP), to_x, to_y, :],
            send_sem=halo_send.at[way, group],
            recv_sem=halo_recv.at[way, group],
            device_id={axis: lax.axis_index(axis) + step},
            device_id_type=MESH,
        )

    relayed = COLS // GROUP - 1
    turns = []
    if row_length:
        for last in range(row_length - 1, nx - 1, row_length):
            turns += [(0, last, last + 1, last + row_length), (1, last + 1, last, last + 1 - row_length)]
    turning = [jnp.bool_(False), jnp.bool_(False)]
    for direction, source, _, _ in turns:
        turning[direction] = jnp.logical_or(turning[direction], gx == source)

    def to_corner(direction, corner):
        from_x, from_y = ways[2 + direction][4]
        return pltpu.make_async_remote_copy(
            src_ref=basis4.at[pl.ds(first + relayed * GROUP, GROUP), from_x, from_y, :],
            dst_ref=relay.at[direction],
            send_sem=relay_send.at[direction],
            recv_sem=relay_recv.at[direction],
            device_id={"gx": corner},
            device_id_type=MESH,
        )

    def from_corner(direction, target):
        to_x, to_y = ways[2 + direction][5]
        return pltpu.make_async_remote_copy(
            src_ref=relay.at[direction],
            dst_ref=pad.at[pl.ds(relayed * GROUP, GROUP), to_x, to_y, :],
            send_sem=forward_send.at[direction],
            recv_sem=halo_recv.at[2 + direction, relayed],
            device_id={"gx": target},
            device_id_type=MESH,
        )

    for direction, source, _, corner in turns:

        @pl.when(gx == source)
        def _(direction=direction, corner=corner):
            to_corner(direction, corner).start()

    def sends(way, group):
        if way < 2 or group != relayed:
            return ways[way][2]
        return jnp.logical_and(ways[way][2], jnp.logical_not(turning[way - 2]))

    for group in range(COLS // GROUP):
        for way in (2, 3, 0, 1):

            @pl.when(sends(way, group))
            def _(way=way, group=group):
                halo(way, group).start()

    for way in range(4):

        @pl.when(jnp.logical_not(ways[way][3]))
        def _(way=way):
            to_x, to_y = ways[way][5]
            pad[:, to_x, to_y, :] = jnp.zeros((COLS, to_x.size, to_y.size, size_z), jnp.float32)

    load_taps.wait()
    load_gain.wait()
    load_classes.wait()
    load_ports.wait()
    layers = LAYERS if size_x % LAYERS == 0 else 1
    z_sums = []
    for m in range(MAT):
        z_sum = taps_ref[m, 4 * REACH]
        for t in range(4 * REACH + 1, 6 * REACH):
            z_sum = z_sum + taps_ref[m, t]
        z_sums.append(z_sum)

    def make_coefs(step, carry):
        place = pl.ds(step * layers, layers)
        kind, port = classes[place], ports[place]
        bits = [(kind & (1 << b)) != 0 for b in range(3)]
        total = jnp.ones(kind.shape, jnp.float32)
        for p in range(PORTS):
            total = jnp.where(port == p + 1, 1.0 + gain_ref[p], total)
        for t in range(4 * REACH + 1):
            level = [taps_ref[m, t] for m in range(MAT)] if t < 4 * REACH else z_sums
            for bit in bits:
                level = [
                    jnp.where(bit, level[2 * i + 1], level[2 * i]) for i in range(len(level) // 2)
                ]
            total = total + level[0]
            if t < 4 * REACH:
                coefs[t, place] = level[0]
        diag[place] = total
        return carry

    lax.fori_loop(0, size_x // layers, make_coefs, 0)
    load_block.wait()

    distance = lax.broadcasted_iota(jnp.int32, (size_z, size_z), 0) - lax.broadcasted_iota(
        jnp.int32, (size_z, size_z), 1
    )

    def make_bands(pair, carry):
        both = []
        for m in (2 * pair, 2 * pair + 1):
            band = jnp.zeros((size_z, size_z), jnp.float32)
            for j in range(2 * REACH):
                band = jnp.where(distance == offset_of(j), taps_ref[m, 4 * REACH + j], band)
            both.append(band)
        band = jnp.concatenate(both, axis=1)
        high = band.astype(jnp.bfloat16).astype(jnp.float32)
        bands[pair] = jnp.concatenate([high, high, band - high], axis=0).astype(jnp.bfloat16)
        return carry

    lax.fori_loop(0, MAT // 2, make_bands, 0)

    def split_block(c, carry):
        place = pl.ds(pl.multiple_of(c * rows, rows), rows)
        image_place = pl.ds(pl.multiple_of(c * pitch, size_y), rows)
        own = pad[c, inner_x, inner_y, :]
        w2[image_place, :] = (diag[...] * own).reshape(rows, size_z)
        own = own.reshape(rows, size_z)
        high = own.astype(jnp.bfloat16).astype(jnp.float32)
        parts[place, :] = jnp.concatenate([high, own - high, high], axis=1).astype(jnp.bfloat16)
        return carry

    lax.fori_loop(0, COLS, split_block, 0)

    def along_z(pair, carry):
        kind = classes[...].reshape(rows, size_z)
        even, odd = kind == 2 * pair, kind == 2 * pair + 1
        for group in range(COLS // GROUP):
            lines = pl.ds(group * GROUP * rows, GROUP * rows)
            result = jnp.dot(parts[lines, :], bands[pair], preferred_element_type=jnp.float32)
            for i in range(GROUP):
                place = pl.ds((group * GROUP + i) * pitch, rows)
                mine = result[i * rows : (i + 1) * rows]
                w2[place, :] -= jnp.where(
                    even, mine[:, :size_z], jnp.where(odd, mine[:, size_z:], 0.0)
                )
        return carry

    lax.fori_loop(0, MAT // 2, along_z, 0)
    for direction, _, target, corner in turns:

        @pl.when(gx == corner)
        def _(direction=direction, target=target):
            to_corner(direction, target).wait_recv()
            from_corner(direction, target).start()

    load_basis.wait()

    def gather(ref, count, chunk):
        return jnp.concatenate(
            [
                ref[pl.ds(chunk * per_chunk + i, count, stride=pitch), :]
                for i in range(per_chunk)
            ],
            axis=1,
        )

    def own_products(chunk, acc):
        both = halves(gather(q2, BLOCKS * COLS, chunk))
        halved[chunk, : 2 * wide, :] = both
        return acc + lax.dot_general(both, both[:wide], NT, preferred_element_type=jnp.float32)

    wide = BLOCKS * COLS
    acc = lax.fori_loop(
        0, chunks, own_products, jnp.zeros((2 * wide, wide), jnp.float32), unroll=UNROLL
    )
    local_qq = acc[:wide] + acc[wide:] + acc[wide:].T
    exchange = Exchange("gy", qq_y, qq_y_send, qq_y_recv)
    exchange.start(
        jnp.concatenate([local_qq[i : i + COLS] for i in range(0, wide, COLS)], axis=1)
    )

    for axis, first_way in (("gy", 0), ("gx", 2)):
        for group in range(COLS // GROUP):
            for way in (first_way, first_way + 1):

                @pl.when(ways[way][3])
                def _(way=way, group=group):
                    halo(way, group).wait_recv()

            def along(x, carry, axis=axis, group=group):
                columns = range(group * GROUP, (group + 1) * GROUP)
                places = [
                    pl.ds(pl.multiple_of(c * pitch + x * size_y, size_y), size_y) for c in columns
                ]
                images = [w2[place, :] for place in places]
                for j in range(2 * REACH):
                    k = offset_of(j)
                    if axis == "gx":
                        coef, at_x, at_y = coefs[j, x], x + REACH + k, inner_y
                    else:
                        coef, at_x = coefs[2 * REACH + j, x], x + REACH
                        at_y = pl.ds(size_y + k, size_y)
                    for i, c in enumerate(columns):
                        images[i] = images[i] - coef * pad[c, at_x, at_y, :]
                for place, image in zip(places, images):
                    w2[place, :] = image
                return carry

            lax.fori_loop(0, size_x, along, 0, unroll=2)

    exchange_x = Exchange("gx", qq_x, qq_x_send, qq_x_recv)
    exchange_x.start(exchange.finish())

    acc = jnp.zeros((2 * (wide + COLS), 2 * COLS), jnp.float32)
    for chunk in range(chunks):
        both = halves(gather(w2, COLS, chunk))
        halved[chunk, 2 * wide :, :] = both
        all_rows = jnp.concatenate([halved[chunk, : 2 * wide, :], both], axis=0)
        acc = acc + lax.dot_general(all_rows, both, NT, preferred_element_type=jnp.float32)
    acc = acc[:, :COLS] + acc[:, COLS:]
    local_g = jnp.concatenate(
        [
            acc[:wide] + acc[wide : 2 * wide],
            acc[2 * wide : 2 * wide + COLS] + acc[2 * wide + COLS :],
            jnp.zeros((128 - wide - COLS, COLS), jnp.float32),
        ],
        axis=0,
    ).T
    g_exchange = Exchange("gy", g_y, g_y_send, g_y_recv)
    g_exchange.start(local_g)
    sums[COLS:, :] = exchange_x.finish()
    for group in range(COLS // GROUP):
        for way in range(4):

            @pl.when(sends(way, group))
            def _(way=way, group=group):
                halo(way, group).wait_send()

    for direction, source, target, corner in turns:

        @pl.when(gx == source)
        def _(direction=direction, corner=corner):
            to_corner(direction, corner).wait_send()

        @pl.when(gx == corner)
        def _(direction=direction, target=target):
            from_corner(direction, target).wait_send()

    exchange.drain()
    exchange_x.drain()
    g_exchange_x = Exchange("gx", g_x, g_x_send, g_x_recv)
    g_exchange_x.start(g_exchange.finish())
    g_exchange.drain()
    sums[:COLS, :] = g_exchange_x.finish()
    g_exchange_x.drain()


def combine_kernel(
    total_cells,
    halved,
    both_sums,
    out_hbm,
    proj_hbm,
    tri_hbm,
    out2,
    proj_ref,
    tri_ref,
    small_sem,
    out_sem,
):
    chunks, _, span = halved.shape
    pitch, size_z = out2.shape[0] // COLS, out2.shape[1]
    rows = pitch - PITCH
    per_chunk = span // size_z
    wide = BLOCKS * COLS
    sums = both_sums[:COLS, :] / total_cells
    sum_qq = jnp.concatenate(
        [both_sums[COLS:, i * wide : (i + 1) * wide] for i in range(BLOCKS)], axis=0
    )
    proj_t = sums[:, :wide]
    proj_ref[...] = proj_t
    row = lax.broadcasted_iota(jnp.int32, (wide, wide), 0)
    column = lax.broadcasted_iota(jnp.int32, (wide, wide), 1)
    middle = jnp.where(row == column, 2.0, 0.0) - sum_qq / total_cells
    left = jnp.dot(proj_t, middle, precision=HIGHEST, preferred_element_type=jnp.float32)
    gram = sums[:, wide : wide + COLS] - lax.dot_general(
        left, proj_t, NT, precision=HIGHEST, preferred_element_type=jnp.float32
    )
    row = lax.broadcasted_iota(jnp.int32, (COLS, COLS), 0)
    column = lax.broadcasted_iota(jnp.int32, (COLS, COLS), 1)
    eye = jnp.where(row == column, 1.0, 0.0)
    table = jnp.concatenate([-proj_t, eye, gram], axis=1)
    base = wide + COLS
    index = lax.broadcasted_iota(jnp.int32, table.shape, 0)
    for j in range(COLS - 1):
        factor = jnp.broadcast_to(table[:, base + j : base + j + 1], table.shape)
        factor = jnp.where(index > j, factor / factor[j : j + 1, :], 0.0)
        table = table - factor * table[j : j + 1, :]
    pivots = jnp.sum(jnp.where(row == column, table[:, base:], 0.0), axis=1, keepdims=True)
    table = table * lax.rsqrt(pivots)
    tri_ref[...] = jnp.where(row <= column, table[:, base:], 0.0)
    store_proj = pltpu.make_async_copy(proj_ref, proj_hbm, small_sem.at[0])
    store_tri = pltpu.make_async_copy(tri_ref, tri_hbm, small_sem.at[1])
    store_proj.start()
    store_tri.start()

    mix = table[:, :base]
    high = mix.astype(jnp.bfloat16).astype(jnp.float32)
    mix = jnp.concatenate([high, mix - high], axis=0)
    mix_q, mix_w = mix[:, :wide], mix[:, wide:]
    mix = jnp.concatenate([mix_q, mix_q, mix_w, mix_w], axis=1).astype(jnp.bfloat16)

    pieces = 2 if chunks % 2 == 0 else 1
    lines = rows // pieces
    stores = []
    for piece in range(pieces):
        for chunk in range(piece * chunks // pieces, (piece + 1) * chunks // pieces):
            result = jnp.dot(mix, halved[chunk], preferred_element_type=jnp.float32)
            result = result[:COLS] + result[COLS:]
            for i in range(per_chunk):
                out2[pl.ds(chunk * per_chunk + i, COLS, stride=pitch), :] = result[
                    :, i * size_z : (i + 1) * size_z
                ]
        part = pl.ds(piece * lines, lines)
        store = pltpu.make_async_copy(
            out2.reshape(COLS, pitch, size_z).at[:, part, :], out_hbm.at[:, part, :], out_sem.at[piece]
        )
        store.start()
        stores.append(store)
    for store in stores:
        store.wait()
    store_proj.wait()
    store_tri.wait()


def per_device(row_length, basis, classes, ports, taps, port_gain):
    size_x, size_y, size_z = classes.shape
    rows = size_x * size_y
    wide = BLOCKS * COLS
    nx, ny = lax.axis_size("gx"), lax.axis_size("gy")
    per_chunk = 16 if rows % 16 == 0 else 1
    chunks, span = rows // per_chunk, per_chunk * size_z
    vmem = functools.partial(pltpu.VMEM, dtype=jnp.float32)
    dma = pltpu.SemaphoreType.DMA
    hbm = pl.BlockSpec(memory_space=pltpu.HBM)
    vmem_spec = pl.BlockSpec(memory_space=pltpu.VMEM)
    groups = COLS // GROUP
    halved_shape = (chunks, 2 * (wide + COLS), span)
    sums_shape = (2 * COLS, BLOCKS * wide)
    halved, sums = pl.pallas_call(
        functools.partial(gather_kernel, row_length),
        out_shape=(
            jax.ShapeDtypeStruct(halved_shape, jnp.bfloat16),
            jax.ShapeDtypeStruct(sums_shape, jnp.float32),
        ),
        in_specs=[hbm] * 6,
        out_specs=(vmem_spec,) * 2,
        scratch_shapes=[
            pltpu.SMEM(taps.shape, jnp.float32),
            pltpu.SMEM(port_gain.shape, jnp.float32),
            vmem((COLS, size_x + 2 * REACH, 3 * size_y, size_z)),
            vmem((wide * (rows + PITCH), size_z)),
            vmem((COLS * (rows + PITCH), size_z)),
            vmem((4 * REACH, size_x, size_y, size_z)),
            vmem((size_x, size_y, size_z)),
            pltpu.VMEM((MAT // 2, 3 * size_z, 2 * size_z), jnp.bfloat16),
            pltpu.VMEM((COLS * rows, 3 * size_z), jnp.bfloat16),
            pltpu.VMEM((size_x, size_y, size_z), jnp.int32),
            pltpu.VMEM((size_x, size_y, size_z), jnp.int32),
            vmem((2, GROUP, REACH, size_y, size_z)),
            vmem((ny, COLS, BLOCKS * wide)),
            vmem((nx, COLS, BLOCKS * wide)),
            vmem((ny, COLS, 128)),
            vmem((nx, COLS, 128)),
            dma((5,)),
            dma,
            dma((4, groups)),
            dma((4, groups)),
            dma((2,)),
            dma((2,)),
            dma((2,)),
            dma((ny,)),
            dma((ny,)),
            dma((nx,)),
            dma((nx,)),
            dma((ny,)),
            dma((ny,)),
            dma((nx,)),
            dma((nx,)),
        ],
        compiler_params=pltpu.CompilerParams(
            collective_id=0, has_side_effects=True, vmem_limit_bytes=40 * 1024 * 1024
        ),
    )(
        *(
            pltpu.with_memory_space_constraint(operand, pltpu.HBM)
            for operand in (
                taps, port_gain, basis, basis.reshape(wide * rows, size_z), classes, ports
            )
        )
    )
    out, projection, triangle = pl.pallas_call(
        functools.partial(combine_kernel, float(rows * size_z * nx * ny)),
        out_shape=(
            jax.ShapeDtypeStruct((COLS, rows, size_z), jnp.float32),
            jax.ShapeDtypeStruct((COLS, wide), jnp.float32),
            jax.ShapeDtypeStruct((COLS, COLS), jnp.float32),
        ),
        in_specs=[vmem_spec] * 2,
        out_specs=(hbm,) * 3,
        scratch_shapes=[
            vmem((COLS * (rows + PITCH), size_z)),
            vmem((COLS, wide)),
            vmem((COLS, COLS)),
            dma((2,)),
            dma((2,)),
        ],
        compiler_params=pltpu.CompilerParams(vmem_limit_bytes=24 * 1024 * 1024),
    )(halved, sums)
    return out.reshape(COLS, size_x, size_y, size_z), projection.T, triangle


def length_of_row(mesh):
    places = [getattr(device, "coords", None) for device in mesh.devices[:, 0]]
    if None in places:
        return 0
    for i in range(1, len(places)):
        if sum(a != b for a, b in zip(places[i - 1], places[i])) > 1:
            return i if len(places) % i == 0 else 0
    return 0


def solution(mesh):
    in_specs = (P(None, "gx", "gy", None), P("gx", "gy", None), P("gx", "gy", None), P(), P())
    out_specs = (P(None, "gx", "gy", None), P(), P())
    return jax.shard_map(
        functools.partial(per_device, length_of_row(mesh)), mesh=mesh, in_specs=in_specs, out_specs=out_specs, check_vma=False
    )
```

```python
import functools

import jax
import jax.numpy as jnp
from jax import lax
from jax.experimental import pallas as pl
from jax.experimental.pallas import tpu as pltpu
from jax.sharding import PartitionSpec as P

COLS = 8
BLOCKS = 4
REACH = 7
MAT = 8
PORTS = 8
GROUP = 4
LAYERS = 4
PITCH = 8
MESH = pl.DeviceIdType.MESH
NT = (((1,), (1,)), ((), ()))
HIGHEST = lax.Precision.HIGHEST


def offset_of(j):
    return j - REACH if j < REACH else j - REACH + 1


def halves(value):
    high = value.astype(jnp.bfloat16).astype(jnp.float32)
    return jnp.concatenate([high, value - high], axis=0).astype(jnp.bfloat16)


class Exchange:
    def __init__(self, axis, buf, send, recv):
        self.axis, self.buf, self.send, self.recv = axis, buf, send, recv
        self.me, self.count = lax.axis_index(axis), lax.axis_size(axis)

    def copy(self, step, slot, peer):
        return pltpu.make_async_remote_copy(
            src_ref=self.buf.at[slot],
            dst_ref=self.buf.at[slot],
            send_sem=self.send.at[step],
            recv_sem=self.recv.at[slot],
            device_id={self.axis: peer},
            device_id_type=MESH,
        )

    def start(self, value):
        self.buf[self.me] = value

        def body(step, carry):
            self.copy(step, self.me, lax.rem(self.me + step, self.count)).start()
            return carry

        lax.fori_loop(1, self.count, body, 0, unroll=self.count <= 8)

    def finish(self):
        def body(step, carry):
            peer = lax.rem(self.me + step, self.count)
            self.copy(step, peer, peer).wait_recv()
            return carry

        lax.fori_loop(1, self.count, body, 0, unroll=self.count <= 8)
        total = self.buf[0]
        for slot in range(1, self.count):
            total = total + self.buf[slot]
        return total

    def drain(self):
        def body(step, carry):
            self.copy(step, self.me, lax.rem(self.me + step, self.count)).wait_send()
            return carry

        lax.fori_loop(1, self.count, body, 0, unroll=self.count <= 8)


def gather_kernel(
    row_length,
    taps_hbm,
    gain_hbm,
    basis4,
    basis2,
    classes_hbm,
    ports_hbm,
    halved,
    sums,
    taps_ref,
    gain_ref,
    pad,
    q2,
    w2,
    coefs,
    diag,
    bands,
    parts,
    classes,
    ports,
    relay,
    qq_y,
    qq_x,
    g_y,
    g_x,
    local_sem,
    block_sem,
    halo_send,
    halo_recv,
    relay_send,
    relay_recv,
    forward_send,
    qq_y_send,
    qq_y_recv,
    qq_x_send,
    qq_x_recv,
    g_y_send,
    g_y_recv,
    g_x_send,
    g_x_recv,
):
    size_x, size_y, size_z = classes.shape
    rows = size_x * size_y
    pitch = rows + PITCH
    first = (BLOCKS - 1) * COLS
    gx, gy = lax.axis_index("gx"), lax.axis_index("gy")
    nx, ny = lax.axis_size("gx"), lax.axis_size("gy")
    chunks, _, span = halved.shape
    per_chunk = span // size_z

    barrier = pltpu.get_barrier_semaphore()
    for axis, me, count in (("gx", gx, nx), ("gy", gy, ny)):

        def greet(step, carry, axis=axis, me=me, count=count):
            pl.semaphore_signal(
                barrier, inc=1, device_id={axis: lax.rem(me + step, count)}, device_id_type=MESH
            )
            return carry

        lax.fori_loop(1, count, greet, 0)

    load_classes = pltpu.make_async_copy(classes_hbm, classes, local_sem.at[0])
    load_ports = pltpu.make_async_copy(ports_hbm, ports, local_sem.at[1])
    load_basis = pltpu.make_async_copy(
        basis2.reshape(BLOCKS * COLS, rows, size_z),
        q2.reshape(BLOCKS * COLS, pitch, size_z).at[:, pl.ds(0, rows), :],
        local_sem.at[2],
    )
    load_block = pltpu.make_async_copy(
        basis4.at[pl.ds(first, COLS)],
        pad.at[:, pl.ds(REACH, size_x), pl.ds(size_y, size_y), :],
        block_sem,
    )
    load_taps = pltpu.make_async_copy(taps_hbm, taps_ref, local_sem.at[3])
    load_gain = pltpu.make_async_copy(gain_hbm, gain_ref, local_sem.at[4])
    load_taps.start()
    load_gain.start()
    load_classes.start()
    load_ports.start()
    load_block.start()
    load_basis.start()
    pl.semaphore_wait(barrier, nx + ny - 2)

    inner_x, inner_y = pl.ds(REACH, size_x), pl.ds(size_y, size_y)
    ways = (
        ("gy", 1, gy < ny - 1, gy > 0,
         (slice(None), pl.ds(size_y - REACH, REACH)), (inner_x, pl.ds(size_y - REACH, REACH))),
        ("gy", -1, gy > 0, gy < ny - 1,
         (slice(None), pl.ds(0, REACH)), (inner_x, pl.ds(2 * size_y, REACH))),
        ("gx", 1, gx < nx - 1, gx > 0,
         (pl.ds(size_x - REACH, REACH), slice(None)), (pl.ds(0, REACH), inner_y)),
        ("gx", -1, gx > 0, gx < nx - 1,
         (pl.ds(0, REACH), slice(None)), (pl.ds(REACH + size_x, REACH), inner_y)),
    )

    def halo(way, group):
        axis, step, _, _, (from_x, from_y), (to_x, to_y) = ways[way]
        return pltpu.make_async_remote_copy(
            src_ref=basis4.at[pl.ds(first + group * GROUP, GROUP), from_x, from_y, :],
            dst_ref=pad.at[pl.ds(group * GROUP, GROUP), to_x, to_y, :],
            send_sem=halo_send.at[way, group],
            recv_sem=halo_recv.at[way, group],
            device_id={axis: lax.axis_index(axis) + step},
            device_id_type=MESH,
        )

    relayed = COLS // GROUP - 1
    turns = []
    if row_length:
        for last in range(row_length - 1, nx - 1, row_length):
            turns += [(0, last, last + 1, last + row_length), (1, last + 1, last, last + 1 - row_length)]
    turning = [jnp.bool_(False), jnp.bool_(False)]
    for direction, source, _, _ in turns:
        turning[direction] = jnp.logical_or(turning[direction], gx == source)

    def to_corner(direction, corner):
        from_x, from_y = ways[2 + direction][4]
        return pltpu.make_async_remote_copy(
            src_ref=basis4.at[pl.ds(first + relayed * GROUP, GROUP), from_x, from_y, :],
            dst_ref=relay.at[direction],
            send_sem=relay_send.at[direction],
            recv_sem=relay_recv.at[direction],
            device_id={"gx": corner},
            device_id_type=MESH,
        )

    def from_corner(direction, target):
        to_x, to_y = ways[2 + direction][5]
        return pltpu.make_async_remote_copy(
            src_ref=relay.at[direction],
            dst_ref=pad.at[pl.ds(relayed * GROUP, GROUP), to_x, to_y, :],
            send_sem=forward_send.at[direction],
            recv_sem=halo_recv.at[2 + direction, relayed],
            device_id={"gx": target},
            device_id_type=MESH,
        )

    for direction, source, _, corner in turns:

        @pl.when(gx == source)
        def _(direction=direction, corner=corner):
            to_corner(direction, corner).start()

    def sends(way, group):
        if way < 2 or group != relayed:
            return ways[way][2]
        return jnp.logical_and(ways[way][2], jnp.logical_not(turning[way - 2]))

    for group in range(COLS // GROUP):
        for way in (2, 3, 0, 1):

            @pl.when(sends(way, group))
            def _(way=way, group=group):
                halo(way, group).start()

    for way in range(4):

        @pl.when(jnp.logical_not(ways[way][3]))
        def _(way=way):
            to_x, to_y = ways[way][5]
            pad[:, to_x, to_y, :] = jnp.zeros((COLS, to_x.size, to_y.size, size_z), jnp.float32)

    load_taps.wait()
    load_gain.wait()
    load_classes.wait()
    load_ports.wait()
    layers = LAYERS if size_x % LAYERS == 0 else 1
    z_sums = []
    for m in range(MAT):
        z_sum = taps_ref[m, 4 * REACH]
        for t in range(4 * REACH + 1, 6 * REACH):
            z_sum = z_sum + taps_ref[m, t]
        z_sums.append(z_sum)

    def make_coefs(step, carry):
        place = pl.ds(step * layers, layers)
        kind, port = classes[place], ports[place]
        bits = [(kind & (1 << b)) != 0 for b in range(3)]
        total = jnp.ones(kind.shape, jnp.float32)
        for p in range(PORTS):
            total = jnp.where(port == p + 1, 1.0 + gain_ref[p], total)
        for t in range(4 * REACH + 1):
            level = [taps_ref[m, t] for m in range(MAT)] if t < 4 * REACH else z_sums
            for bit in bits:
                level = [
                    jnp.where(bit, level[2 * i + 1], level[2 * i]) for i in range(len(level) // 2)
                ]
            total = total + level[0]
            if t < 4 * REACH:
                coefs[t, place] = level[0]
        diag[place] = total
        return carry

    lax.fori_loop(0, size_x // layers, make_coefs, 0)
    load_block.wait()

    distance = lax.broadcasted_iota(jnp.int32, (size_z, size_z), 0) - lax.broadcasted_iota(
        jnp.int32, (size_z, size_z), 1
    )

    def make_bands(pair, carry):
        both = []
        for m in (2 * pair, 2 * pair + 1):
            band = jnp.zeros((size_z, size_z), jnp.float32)
            for j in range(2 * REACH):
                band = jnp.where(distance == offset_of(j), taps_ref[m, 4 * REACH + j], band)
            both.append(band)
        band = jnp.concatenate(both, axis=1)
        high = band.astype(jnp.bfloat16).astype(jnp.float32)
        bands[pair] = jnp.concatenate([high, high, band - high], axis=0).astype(jnp.bfloat16)
        return carry

    lax.fori_loop(0, MAT // 2, make_bands, 0)

    def split_block(c, carry):
        place = pl.ds(pl.multiple_of(c * rows, rows), rows)
        image_place = pl.ds(pl.multiple_of(c * pitch, size_y), rows)
        own = pad[c, inner_x, inner_y, :]
        w2[image_place, :] = (diag[...] * own).reshape(rows, size_z)
        own = own.reshape(rows, size_z)
        high = own.astype(jnp.bfloat16).astype(jnp.float32)
        parts[place, :] = jnp.concatenate([high, own - high, high], axis=1).astype(jnp.bfloat16)
        return carry

    lax.fori_loop(0, COLS, split_block, 0)

    def along_z(pair, carry):
        kind = classes[...].reshape(rows, size_z)
        even, odd = kind == 2 * pair, kind == 2 * pair + 1
        for group in range(COLS // GROUP):
            lines = pl.ds(group * GROUP * rows, GROUP * rows)
            result = jnp.dot(parts[lines, :], bands[pair], preferred_element_type=jnp.float32)
            for i in range(GROUP):
                place = pl.ds((group * GROUP + i) * pitch, rows)
                mine = result[i * rows : (i + 1) * rows]
                w2[place, :] -= jnp.where(
                    even, mine[:, :size_z], jnp.where(odd, mine[:, size_z:], 0.0)
                )
        return carry

    lax.fori_loop(0, MAT // 2, along_z, 0)
    for direction, _, target, corner in turns:

        @pl.when(gx == corner)
        def _(direction=direction, target=target):
            to_corner(direction, target).wait_recv()
            from_corner(direction, target).start()

    load_basis.wait()

    def gather(ref, count, chunk):
        return jnp.concatenate(
            [
                ref[pl.ds(chunk * per_chunk + i, count, stride=pitch), :]
                for i in range(per_chunk)
            ],
            axis=1,
        )

    def own_products(chunk, acc):
        both = halves(gather(q2, BLOCKS * COLS, chunk))
        halved[chunk, : 2 * wide, :] = both
        return acc + lax.dot_general(both, both[:wide], NT, preferred_element_type=jnp.float32)

    wide = BLOCKS * COLS
    acc = lax.fori_loop(
        0, chunks, own_products, jnp.zeros((2 * wide, wide), jnp.float32), unroll=True
    )
    local_qq = acc[:wide] + acc[wide:] + acc[wide:].T
    exchange = Exchange("gy", qq_y, qq_y_send, qq_y_recv)
    exchange.start(
        jnp.concatenate([local_qq[i : i + COLS] for i in range(0, wide, COLS)], axis=1)
    )

    for axis, first_way in (("gy", 0), ("gx", 2)):
        for group in range(COLS // GROUP):
            for way in (first_way, first_way + 1):

                @pl.when(ways[way][3])
                def _(way=way, group=group):
                    halo(way, group).wait_recv()

            def along(x, carry, axis=axis, group=group):
                columns = range(group * GROUP, (group + 1) * GROUP)
                places = [
                    pl.ds(pl.multiple_of(c * pitch + x * size_y, size_y), size_y) for c in columns
                ]
                images = [w2[place, :] for place in places]
                for j in range(2 * REACH):
                    k = offset_of(j)
                    if axis == "gx":
                        coef, at_x, at_y = coefs[j, x], x + REACH + k, inner_y
                    else:
                        coef, at_x = coefs[2 * REACH + j, x], x + REACH
                        at_y = pl.ds(size_y + k, size_y)
                    for i, c in enumerate(columns):
                        images[i] = images[i] - coef * pad[c, at_x, at_y, :]
                for place, image in zip(places, images):
                    w2[place, :] = image
                return carry

            lax.fori_loop(0, size_x, along, 0, unroll=4)

    exchange_x = Exchange("gx", qq_x, qq_x_send, qq_x_recv)
    exchange_x.start(exchange.finish())

    acc = jnp.zeros((2 * (wide + COLS), 2 * COLS), jnp.float32)
    for chunk in range(chunks):
        both = halves(gather(w2, COLS, chunk))
        halved[chunk, 2 * wide :, :] = both
        all_rows = jnp.concatenate([halved[chunk, : 2 * wide, :], both], axis=0)
        acc = acc + lax.dot_general(all_rows, both, NT, preferred_element_type=jnp.float32)
    acc = acc[:, :COLS] + acc[:, COLS:]
    local_g = jnp.concatenate(
        [
            acc[:wide] + acc[wide : 2 * wide],
            acc[2 * wide : 2 * wide + COLS] + acc[2 * wide + COLS :],
            jnp.zeros((128 - wide - COLS, COLS), jnp.float32),
        ],
        axis=0,
    ).T
    g_exchange = Exchange("gy", g_y, g_y_send, g_y_recv)
    g_exchange.start(local_g)
    sums[COLS:, :] = exchange_x.finish()
    for group in range(COLS // GROUP):
        for way in range(4):

            @pl.when(sends(way, group))
            def _(way=way, group=group):
                halo(way, group).wait_send()

    for direction, source, target, corner in turns:

        @pl.when(gx == source)
        def _(direction=direction, corner=corner):
            to_corner(direction, corner).wait_send()

        @pl.when(gx == corner)
        def _(direction=direction, target=target):
            from_corner(direction, target).wait_send()

    exchange.drain()
    exchange_x.drain()
    g_exchange_x = Exchange("gx", g_x, g_x_send, g_x_recv)
    g_exchange_x.start(g_exchange.finish())
    g_exchange.drain()
    sums[:COLS, :] = g_exchange_x.finish()
    g_exchange_x.drain()


def combine_kernel(
    total_cells,
    halved,
    both_sums,
    out_hbm,
    proj_hbm,
    tri_hbm,
    out2,
    proj_ref,
    tri_ref,
    small_sem,
    out_sem,
):
    chunks, _, span = halved.shape
    pitch, size_z = out2.shape[0] // COLS, out2.shape[1]
    rows = pitch - PITCH
    per_chunk = span // size_z
    wide = BLOCKS * COLS
    sums = both_sums[:COLS, :] / total_cells
    sum_qq = jnp.concatenate(
        [both_sums[COLS:, i * wide : (i + 1) * wide] for i in range(BLOCKS)], axis=0
    )
    proj_t = sums[:, :wide]
    proj_ref[...] = proj_t
    row = lax.broadcasted_iota(jnp.int32, (wide, wide), 0)
    column = lax.broadcasted_iota(jnp.int32, (wide, wide), 1)
    middle = jnp.where(row == column, 2.0, 0.0) - sum_qq / total_cells
    left = jnp.dot(proj_t, middle, precision=HIGHEST, preferred_element_type=jnp.float32)
    gram = sums[:, wide : wide + COLS] - lax.dot_general(
        left, proj_t, NT, precision=HIGHEST, preferred_element_type=jnp.float32
    )
    row = lax.broadcasted_iota(jnp.int32, (COLS, COLS), 0)
    column = lax.broadcasted_iota(jnp.int32, (COLS, COLS), 1)
    eye = jnp.where(row == column, 1.0, 0.0)
    table = jnp.concatenate([-proj_t, eye, gram], axis=1)
    base = wide + COLS
    index = lax.broadcasted_iota(jnp.int32, table.shape, 0)
    for j in range(COLS - 1):
        factor = jnp.broadcast_to(table[:, base + j : base + j + 1], table.shape)
        factor = jnp.where(index > j, factor / factor[j : j + 1, :], 0.0)
        table = table - factor * table[j : j + 1, :]
    pivots = jnp.sum(jnp.where(row == column, table[:, base:], 0.0), axis=1, keepdims=True)
    table = table * lax.rsqrt(pivots)
    tri_ref[...] = jnp.where(row <= column, table[:, base:], 0.0)
    store_proj = pltpu.make_async_copy(proj_ref, proj_hbm, small_sem.at[0])
    store_tri = pltpu.make_async_copy(tri_ref, tri_hbm, small_sem.at[1])
    store_proj.start()
    store_tri.start()

    mix = table[:, :base]
    high = mix.astype(jnp.bfloat16).astype(jnp.float32)
    mix = jnp.concatenate([high, mix - high], axis=0)
    mix_q, mix_w = mix[:, :wide], mix[:, wide:]
    mix = jnp.concatenate([mix_q, mix_q, mix_w, mix_w], axis=1).astype(jnp.bfloat16)

    pieces = 2 if chunks % 2 == 0 else 1
    lines = rows // pieces
    stores = []
    for piece in range(pieces):
        for chunk in range(piece * chunks // pieces, (piece + 1) * chunks // pieces):
            result = jnp.dot(mix, halved[chunk], preferred_element_type=jnp.float32)
            result = result[:COLS] + result[COLS:]
            for i in range(per_chunk):
                out2[pl.ds(chunk * per_chunk + i, COLS, stride=pitch), :] = result[
                    :, i * size_z : (i + 1) * size_z
                ]
        part = pl.ds(piece * lines, lines)
        store = pltpu.make_async_copy(
            out2.reshape(COLS, pitch, size_z).at[:, part, :], out_hbm.at[:, part, :], out_sem.at[piece]
        )
        store.start()
        stores.append(store)
    for store in stores:
        store.wait()
    store_proj.wait()
    store_tri.wait()


def per_device(row_length, basis, classes, ports, taps, port_gain):
    size_x, size_y, size_z = classes.shape
    rows = size_x * size_y
    wide = BLOCKS * COLS
    nx, ny = lax.axis_size("gx"), lax.axis_size("gy")
    per_chunk = 16 if rows % 16 == 0 else 1
    chunks, span = rows // per_chunk, per_chunk * size_z
    vmem = functools.partial(pltpu.VMEM, dtype=jnp.float32)
    dma = pltpu.SemaphoreType.DMA
    hbm = pl.BlockSpec(memory_space=pltpu.HBM)
    vmem_spec = pl.BlockSpec(memory_space=pltpu.VMEM)
    groups = COLS // GROUP
    halved_shape = (chunks, 2 * (wide + COLS), span)
    sums_shape = (2 * COLS, BLOCKS * wide)
    halved, sums = pl.pallas_call(
        functools.partial(gather_kernel, row_length),
        out_shape=(
            jax.ShapeDtypeStruct(halved_shape, jnp.bfloat16),
            jax.ShapeDtypeStruct(sums_shape, jnp.float32),
        ),
        in_specs=[hbm] * 6,
        out_specs=(vmem_spec,) * 2,
        scratch_shapes=[
            pltpu.SMEM(taps.shape, jnp.float32),
            pltpu.SMEM(port_gain.shape, jnp.float32),
            vmem((COLS, size_x + 2 * REACH, 3 * size_y, size_z)),
            vmem((wide * (rows + PITCH), size_z)),
            vmem((COLS * (rows + PITCH), size_z)),
            vmem((4 * REACH, size_x, size_y, size_z)),
            vmem((size_x, size_y, size_z)),
            pltpu.VMEM((MAT // 2, 3 * size_z, 2 * size_z), jnp.bfloat16),
            pltpu.VMEM((COLS * rows, 3 * size_z), jnp.bfloat16),
            pltpu.VMEM((size_x, size_y, size_z), jnp.int32),
            pltpu.VMEM((size_x, size_y, size_z), jnp.int32),
            vmem((2, GROUP, REACH, size_y, size_z)),
            vmem((ny, COLS, BLOCKS * wide)),
            vmem((nx, COLS, BLOCKS * wide)),
            vmem((ny, COLS, 128)),
            vmem((nx, COLS, 128)),
            dma((5,)),
            dma,
            dma((4, groups)),
            dma((4, groups)),
            dma((2,)),
            dma((2,)),
            dma((2,)),
            dma((ny,)),
            dma((ny,)),
            dma((nx,)),
            dma((nx,)),
            dma((ny,)),
            dma((ny,)),
            dma((nx,)),
            dma((nx,)),
        ],
        compiler_params=pltpu.CompilerParams(
            collective_id=0, has_side_effects=True, vmem_limit_bytes=40 * 1024 * 1024
        ),
    )(
        *(
            pltpu.with_memory_space_constraint(operand, pltpu.HBM)
            for operand in (
                taps, port_gain, basis, basis.reshape(wide * rows, size_z), classes, ports
            )
        )
    )
    out, projection, triangle = pl.pallas_call(
        functools.partial(combine_kernel, float(rows * size_z * nx * ny)),
        out_shape=(
            jax.ShapeDtypeStruct((COLS, rows, size_z), jnp.float32),
            jax.ShapeDtypeStruct((COLS, wide), jnp.float32),
            jax.ShapeDtypeStruct((COLS, COLS), jnp.float32),
        ),
        in_specs=[vmem_spec] * 2,
        out_specs=(hbm,) * 3,
        scratch_shapes=[
            vmem((COLS * (rows + PITCH), size_z)),
            vmem((COLS, wide)),
            vmem((COLS, COLS)),
            dma((2,)),
            dma((2,)),
        ],
        compiler_params=pltpu.CompilerParams(vmem_limit_bytes=24 * 1024 * 1024),
    )(halved, sums)
    return out.reshape(COLS, size_x, size_y, size_z), projection.T, triangle


def length_of_row(mesh):
    places = [getattr(device, "coords", None) for device in mesh.devices[:, 0]]
    if None in places:
        return 0
    for i in range(1, len(places)):
        if sum(a != b for a, b in zip(places[i - 1], places[i])) > 1:
            return i if len(places) % i == 0 else 0
    return 0


def solution(mesh):
    in_specs = (P(None, "gx", "gy", None), P("gx", "gy", None), P("gx", "gy", None), P(), P())
    out_specs = (P(None, "gx", "gy", None), P(), P())
    return jax.shard_map(
        functools.partial(per_device, length_of_row(mesh)), mesh=mesh, in_specs=in_specs, out_specs=out_specs, check_vma=False
    )
```
